32 devices in a mesh: rep: 4 (over z), shard: 8 (over y, x, core).
Axes of the slice: x: 2, y: 2, z: 4, core: 2. Of those that a mesh axis runs over, the one named last changes fastest.
Arguments:
- tokens: bfloat16 [2, 64, 128, 2048], P(None, ('rep', 'shard')), may hold values from -6 to 6
- cotangent: bfloat16 [2, 64, 128, 2048], P(None, 'rep', None, 'shard'), may hold values from -6 to 6
- seq_blocks: int32 [2, 4, 4], P(None, 'rep'), may hold values from 1 to 8, 16 in all within a row
- seq_pad: int32 [2, 4, 4], P(None, 'rep'), may hold values from 0 to 63
- deal_order: int32 [2, 4, 16], P(None, 'rep'), may hold values from 0 to 15, each once within a row
- ln1_gain: bfloat16 [2048], P('shard'), may hold values from 0.5 to 1.5
- ln1_bias: bfloat16 [2048], P('shard'), may hold values from -1.25 to 1.25
- ln2_gain: bfloat16 [2048], P('shard'), may hold values from 0.5 to 1.5
- ln2_bias: bfloat16 [2048], P('shard'), may hold values from -1.25 to 1.25
- qkv_weight: bfloat16 [2048, 6144], P('shard'), may hold values from -0.125 to 0.125
- qkv_bias: bfloat16 [6144], P('shard'), may hold values from -1.25 to 1.25
- out_weight: bfloat16 [2048, 2048], P('shard'), may hold values from -1 to 1
- out_bias: bfloat16 [2048], P('shard'), may hold values from -1.25 to 1.25
- up_weight: bfloat16 [2048, 8192], P('shard'), may hold values from -0.125 to 0.125
- up_bias: bfloat16 [8192], P('shard'), may hold values from -3 to 3
- down_weight: bfloat16 [8192, 2048], P('shard'), may hold values from -0.0625 to 0.0625
- down_bias: bfloat16 [2048], P('shard'), may hold values from -1.25 to 1.25
Outputs:
- out: bfloat16 [2, 64, 128, 2048], P(None, 'rep', None, 'shard')
- tokens_grad: bfloat16 [2, 64, 128, 2048], P(None, ('rep', 'shard'))
- ln1_gain_grad: float32 [2048], P('shard')
- ln1_bias_grad: float32 [2048], P('shard')
- ln2_gain_grad: float32 [2048], P('shard')
- ln2_bias_grad: float32 [2048], P('shard')
- qkv_weight_grad: float32 [2048, 6144], P('shard')
- qkv_bias_grad: float32 [6144], P('shard')
- out_weight_grad: float32 [2048, 2048], P('shard')
- out_bias_grad: float32 [2048], P('shard')
- up_weight_grad: float32 [2048, 8192], P('shard')
- up_bias_grad: float32 [8192], P('shard')
- down_weight_grad: float32 [8192, 2048], P('shard')
- down_bias_grad: float32 [2048], P('shard')
The draws below stay inside these ranges and needn't reach their ends.
Inputs may be any that keep to these rules, and one draw needn't show every extreme that they name: `seq_blocks`: each row of 4 counts sums to 16, and its largest count is exactly 8. `deal_order`: each row is a permutation of the 16 block indices of one group.
All inputs are finite; a program needn't handle non-finite values.
Results may differ from the reference program's by a relative error of at most 0.014.
Values may be sent and summed in bfloat16 or wider, within the bound.
No kernel may reach another device: no remote copies, remote signals or barrier semaphores. Data moves between devices by JAX's collectives and lax.ppermute only.
A program may use at most 640 MiB of HBM per device.

```python
import math
import jax
import jax.numpy as jnp
import numpy as np
from jax import lax

D = 2048
HEADS = 8
HD = 256
ROT = 64
FF = 8192
BLK = 128
SEQ_MOST = 8
MB = 2
GB = 16
NSEQ = 4
BLOCKS = 64
N_REP = 4


def touch_ends(entries, rng, least, top_value):
    dims = entries.shape
    place = [jax.random.randint(jax.random.fold_in(rng, axis), (), 0, dims[axis]) for axis in range(len(dims))]
    entries = entries.at[tuple(place)].set(least)
    longest = dims.index(max(dims))
    place[longest] = (place[longest] + 1) % dims[longest]
    return entries.at[tuple(place)].set(top_value)


def block_scale(stream_key, shape, cuts, smallest, top_value):
    factor_of, own = 1.0, jax.random.fold_in(stream_key, 6)
    for dim, blocks in cuts:
        draws = jnp.exp(jax.random.uniform(jax.random.fold_in(own, dim), (blocks,), jnp.float32, smallest / len(cuts), top_value / len(cuts)))
        factor_of = factor_of * jnp.repeat(draws, shape[dim] // blocks).reshape([-1 if axis == dim else 1 for axis in range(len(shape))])
    return factor_of


def split_up(amount, total, most, skew):
    loads = [(1 << 20) // math.isqrt(grade ** skew) + 1 for grade in range(2, amount + 1)]
    spare, counts = total - most - (amount - 1), [1] * (amount - 1)
    while spare > 0:
        free = [i for i in range(amount - 1) if counts[i] < most]
        whole, budget = sum([loads[i] for i in free]), spare
        for i in free:
            addition = min(most - counts[i], max(1, budget * loads[i] // whole), spare)
            counts[i] = counts[i] + addition
            spare = spare - addition
    return np.array([most] + counts)


def uneven_parts(key, amount, total, reach, skew):
    if amount == 2:
        one = jax.random.randint(key, (), max(1, total - reach), min(reach, total - 1) + 1)
        return jnp.stack([one, total - one])
    tallies = jnp.asarray(split_up(amount, total, reach, skew), jnp.int32)
    twos = (amount - 1) // 2
    giver, sink = tallies[1:1 + 2 * twos:2], tallies[2:2 + 2 * twos:2]
    slack = jnp.minimum(giver - 1, reach - sink)
    shifted = jax.random.randint(jax.random.fold_in(key, 1), (twos,), 0, 1 << 20) % (slack + 1)
    tallies = tallies.at[1:1 + 2 * twos:2].set(giver - shifted).at[2:2 + 2 * twos:2].set(sink + shifted)
    return tallies[jax.random.permutation(jax.random.fold_in(key, 2), amount)]


def scatter_about(rng, dims, width, bound, pieces=(), kind=jnp.bfloat16):
    level = block_scale(rng, dims, pieces, -0.22, 0.18) if pieces else 1.0
    entries = jax.random.normal(rng, dims, jnp.float32) * width * level
    return jnp.minimum(jnp.maximum(entries, -bound), bound).astype(kind)


def setup_inputs(seed: int = 0) -> dict:
    streams_of = jax.random.split(jax.random.key(seed), 18)
    tokens = scatter_about(streams_of[0], (MB, BLOCKS, BLK, D), 1.0, 6.0, ((1, 32),))
    cotangent = scatter_about(streams_of[1], (MB, BLOCKS, BLK, D), 1.0, 6.0, ((1, 4), (3, 8)))
    seq_blocks = jax.vmap(lambda own: uneven_parts(own, NSEQ, GB, SEQ_MOST, 2))(jax.random.split(streams_of[2], MB * N_REP)).reshape((MB, N_REP, NSEQ)).astype(jnp.int32)
    seq_pad = touch_ends(jax.random.randint(streams_of[3], (MB, N_REP, NSEQ), 0, BLK // 2), jax.random.fold_in(streams_of[3], 1), 0, (BLK // 2) - 1).astype(jnp.int32)
    deal_order = jax.vmap(lambda own: jax.random.permutation(own, GB))(jax.random.split(streams_of[4], MB * N_REP)).reshape((MB, N_REP, GB)).astype(jnp.int32)
    ln1_gain = jnp.clip(1.0 + 0.1 * jax.random.normal(streams_of[5], (D,), jnp.float32), 0.5, 1.5).astype(jnp.bfloat16)
    ln1_bias = scatter_about(streams_of[6], (D,), 0.2, 1.25, ((0, 8),))
    ln2_gain = jnp.clip(1.0 + 0.1 * jax.random.normal(streams_of[7], (D,), jnp.float32), 0.5, 1.5).astype(jnp.bfloat16)
    ln2_bias = scatter_about(streams_of[8], (D,), 0.2, 1.25, ((0, 8),))
    qkv_weight = scatter_about(streams_of[9], (D, 3 * D), D ** -0.5, 0.125, ((0, 8),))
    qkv_bias = scatter_about(streams_of[10], (3 * D,), 0.2, 1.25, ((0, 8),))
    out_weight = scatter_about(streams_of[11], (D, D), (max(D // 64, 16)) ** -0.5, 1.0, ((0, 8),))
    out_bias = scatter_about(streams_of[12], (D,), 0.2, 1.25, ((0, 8),))
    up_weight = scatter_about(streams_of[13], (D, FF), D ** -0.5, 0.125, ((0, 8),))
    up_bias = scatter_about(streams_of[14], (FF,), 0.5, 3.0, ((0, 8),))
    down_weight = scatter_about(streams_of[15], (FF, D), FF ** -0.5, 0.0625, ((0, 8),))
    down_bias = scatter_about(streams_of[16], (D,), 0.2, 1.25, ((0, 8),))
    return {"tokens": tokens, "cotangent": cotangent, "seq_blocks": seq_blocks, "seq_pad": seq_pad, "deal_order": deal_order, "ln1_gain": ln1_gain, "ln1_bias": ln1_bias, "ln2_gain": ln2_gain, "ln2_bias": ln2_bias, "qkv_weight": qkv_weight, "qkv_bias": qkv_bias, "out_weight": out_weight, "out_bias": out_bias, "up_weight": up_weight, "up_bias": up_bias, "down_weight": down_weight, "down_bias": down_bias}


EPS = 1e-05
HIGH = lax.Precision.HIGHEST

@jax.custom_vjp
def low(v):
    return lax.optimization_barrier(v.astype(jnp.bfloat16)).astype(jnp.float32)

@jax.custom_vjp
def low_back(v):
    return v

def low_keep(v):
    return (low(v), None)

def low_pass(kept, grad):
    return (grad,)

def back_keep(v):
    return (v, None)

def back_low(kept, grad):
    return (low(grad),)
low.defvjp(low_keep, low_pass)
low_back.defvjp(back_keep, back_low)

def rotary_tables(positions):
    half = ROT // 2
    freqs = 10000.0 ** (-2.0 * jnp.arange(half, dtype=jnp.float32) / ROT)
    angles = positions.astype(jnp.float32)[:, None] * freqs[None, :]
    cosine = jnp.concatenate([jnp.cos(angles), jnp.cos(angles)], axis=-1)
    sine = jnp.concatenate([jnp.sin(angles), jnp.sin(angles)], axis=-1)
    return (cosine, sine)

def rotate(values, cosine, sine):
    half = ROT // 2
    front = values[..., :ROT]
    turned = jnp.concatenate([-front[..., half:], front[..., :half]], axis=-1)
    moved = front * cosine[:, None, :] + turned * sine[:, None, :]
    return jnp.concatenate([moved, values[..., ROT:]], axis=-1)

def pick_rows(table, chosen):
    return table[chosen]

def block_layer(params, tokens_f, blocks, pad_counts):
    gain_first, offset_first, gain_second, offset_second, qkv_w, qkv_b, out_w, out_b, up_w, up_b, down_w, down_b = params
    span = tokens_f.shape[0]
    token_ids = jnp.arange(span, dtype=jnp.int32)
    ends = (jnp.cumsum(blocks) * BLK).astype(jnp.int32)
    starts = (ends - blocks * BLK).astype(jnp.int32)
    lengths = (blocks * BLK - pad_counts).astype(jnp.int32)
    inside = (token_ids[:, None] >= starts[None, :]) & (token_ids[:, None] < ends[None, :])
    seq_first = lax.optimization_barrier(jnp.sum(jnp.where(inside, starts[None, :], 0), axis=1)).astype(jnp.int32)
    seq_end = seq_first + lax.optimization_barrier(jnp.sum(jnp.where(inside, lengths[None, :], 0), axis=1)).astype(jnp.int32)
    positions = token_ids - seq_first
    allowed = (token_ids[None, :] >= seq_first[:, None]) & (token_ids[None, :] <= token_ids[:, None]) & (token_ids[None, :] < seq_end[:, None])
    center = tokens_f - lax.optimization_barrier(jnp.mean(tokens_f, axis=-1, keepdims=True))
    inv_std = lax.rsqrt(lax.optimization_barrier(jnp.mean(center * center, axis=-1, keepdims=True)) + EPS)
    normed = center * inv_std
    in_one = low(normed * gain_first + offset_first)
    in_two = low(normed * gain_second + offset_second)
    mixed = low_back(jnp.dot(in_one, qkv_w, precision=HIGH) + qkv_b)
    cosine, sine = rotary_tables(positions)
    query = low(rotate(mixed[:, :D].reshape(span, HEADS, HD), cosine, sine))
    keys = low(rotate(mixed[:, D:2 * D].reshape(span, HEADS, HD), cosine, sine))
    values = low(mixed[:, 2 * D:].reshape(span, HEADS, HD))
    scores = low_back(jnp.einsum('qhd,khd->hqk', query, keys, precision=HIGH) * HD ** (-0.5))
    scores = jnp.where(allowed[None], scores, -jnp.inf)
    attention = jax.nn.softmax(scores, axis=-1)
    context = jnp.einsum('hqk,khd->qhd', low(attention), values, precision=HIGH).reshape(span, D)
    context = low_back(low(context))
    hidden = low_back(jnp.dot(in_two, up_w, precision=HIGH) + up_b)
    active = low_back(low(jax.nn.gelu(hidden, approximate=False)))
    attended = jnp.dot(context, out_w, precision=HIGH) + out_b
    fed = jnp.dot(active, down_w, precision=HIGH) + down_b
    return tokens_f + attended + fed

def forward(params, packs, block_rows, pad_rows):

    def scan_step(carry, items):
        tokens_f, blocks, pad_counts = items
        return (carry, jax.checkpoint(block_layer)(params, tokens_f, blocks, pad_counts))
    _, outputs = lax.scan(scan_step, jnp.zeros((), jnp.float32), (packs, block_rows, pad_rows))
    return outputs

def reference(tokens, cotangent, seq_blocks, seq_pad, deal_order, ln1_gain, ln1_bias, ln2_gain, ln2_bias, qkv_weight, qkv_bias, out_weight, out_bias, up_weight, up_bias, down_weight, down_bias):
    order = deal_order.astype(jnp.int32)
    inverse = jnp.argsort(order, axis=-1).astype(jnp.int32)
    dealt = tokens.astype(jnp.float32).reshape(MB, N_REP, GB, BLK, D)
    given = jax.vmap(jax.vmap(pick_rows))(dealt, inverse)
    packs = given.reshape(MB * N_REP, GB * BLK, D)
    cot_packs = cotangent.astype(jnp.float32).reshape(MB * N_REP, GB * BLK, D)
    block_rows = seq_blocks.reshape(MB * N_REP, NSEQ).astype(jnp.int32)
    pad_rows = seq_pad.reshape(MB * N_REP, NSEQ).astype(jnp.int32)
    params = tuple((p.astype(jnp.float32) for p in (ln1_gain, ln1_bias, ln2_gain, ln2_bias, qkv_weight, qkv_bias, out_weight, out_bias, up_weight, up_bias, down_weight, down_bias)))

    def layer_stack(weights, tokens_f):
        return forward(weights, tokens_f, block_rows, pad_rows)
    outputs, pull_back = jax.vjp(layer_stack, params, packs)
    param_grads, token_grads = pull_back(cot_packs)
    out = outputs.reshape(MB, N_REP * GB, BLK, D).astype(jnp.bfloat16)
    grads_given = token_grads.reshape(MB, N_REP, GB, BLK, D)
    grads_dealt = jax.vmap(jax.vmap(pick_rows))(grads_given, order)
    tokens_grad = grads_dealt.reshape(MB, N_REP * GB, BLK, D).astype(jnp.bfloat16)
    grads = param_grads
    return (out, tokens_grad, grads[0], grads[1], grads[2], grads[3], grads[4], grads[5], grads[6], grads[7], grads[8], grads[9], grads[10], grads[11])
```

```python
import jax
import jax.numpy as jnp
from jax import lax
from jax.experimental import pallas as pl
from jax.experimental.pallas import tpu as pltpu
from jax.sharding import PartitionSpec as P

D = 2048
HEADS = 8
HD = 256
ROT = 64
FF = 8192
BLK = 128
SEQ_MOST = 8
MB = 2
EPS = 1e-05
SCALE = HD ** (-0.5)

bf16 = jnp.bfloat16
f32 = jnp.float32

ORDER = (0, 2, 4, 6, 1, 3, 5, 7)
SPOT = tuple(ORDER.index(r) for r in range(8))


def dot(a, b, ca, cb):
    return lax.dot_general(a, b, (((ca,), (cb,)), ((), ())), preferred_element_type=f32)


def flip(value, bit):
    return lax.ppermute(value, "shard", [(i, i ^ bit) for i in range(8)])


def gather_pieces(own):
    x_got = [flip(h, 2) for h in own]
    y_got = [flip(h, 4) for h in own]
    core = [flip(h, 1) for h in own]
    far = [flip(x_got[0], 4), flip(y_got[1], 2)]
    x_core = [flip(h, 1) for h in x_got]
    y_core = [flip(h, 1) for h in y_got]
    far_core = [flip(h, 1) for h in far]
    return [own, core, x_got, x_core, y_got, y_core, far, far_core]


def turn_rows(value, bit):
    lead, n, c = value.shape[:-2], value.shape[-2], value.shape[-1]
    if bit == 1:
        return lax.rev(value, (value.ndim - 3,))
    value = value.reshape(lead + (2, 2, n // 4, c))
    value = lax.rev(value, (value.ndim - (3 if bit == 2 else 4),))
    return value.reshape(lead + (n, c))


def reduce_pieces(odd, even_of, turn=lambda value, bit: value):
    even = even_of(turn(flip(odd, 1), 1))
    one, two = even[:, 0], even[:, 1]
    got_one = turn(flip(one[1::2], 2), 2)
    got_two = turn(flip(two[2:], 4), 4)
    mid_one = [(one[2 * i].astype(f32) + got_one[i].astype(f32)).astype(bf16) for i in range(2)]
    mid_two = [(two[i].astype(f32) + got_two[i].astype(f32)).astype(bf16) for i in range(2)]
    last_one = turn(flip(mid_one[1], 4), 4)
    last_two = turn(flip(mid_two[1], 2), 2)
    return [
        mid_one[0].astype(f32) + last_one.astype(f32),
        mid_two[0].astype(f32) + last_two.astype(f32),
    ]


def rep_sum(value):
    if lax.axis_size("rep") != 4:
        return lax.psum(value, "rep")
    spot = lax.axis_index("rep")
    inner = (spot == 1) | (spot == 2)
    came = lax.ppermute(value, "rep", [(0, 1), (3, 2)])
    pair = (value.astype(f32) + came.astype(f32)).astype(bf16)
    other = lax.ppermute(pair, "rep", [(1, 2), (2, 1)])
    total = (pair.astype(f32) + other.astype(f32)).astype(bf16)
    back = lax.ppermute(total, "rep", [(1, 0), (2, 3)])
    return jnp.where(inner, total, back)


def rotary_tables():
    half = ROT // 2
    freqs = 10000.0 ** (-2.0 * jnp.arange(half, dtype=f32) / ROT)
    angles = jnp.arange(SEQ_MOST * BLK, dtype=f32)[:, None] * freqs[None, :]
    rest = 128 - ROT
    cosine = jnp.concatenate(
        [jnp.cos(angles), jnp.cos(angles), jnp.ones((SEQ_MOST * BLK, rest), f32)], axis=-1
    )
    sine = jnp.concatenate(
        [-jnp.sin(angles), jnp.sin(angles), jnp.zeros((SEQ_MOST * BLK, rest), f32)], axis=-1
    )
    return cosine.reshape(SEQ_MOST, BLK, 128), sine.reshape(SEQ_MOST, BLK, 128)


def attention_kernel(
    piece_of, inner_of, first_of, end_of,
    qkv_ref, grad_ref, cos_ref, sin_ref,
    ctx_ref, out_ref,
    q_buf, k_buf, v_buf, dk_buf, dv_buf,
):
    m = pl.program_id(0)
    blocks = piece_of.shape[1]
    lane = lax.broadcasted_iota(jnp.int32, (BLK, 128), 1)

    def turned(x):
        return jnp.where(lane < ROT // 2, pltpu.roll(x, 128 - ROT // 2, 1), pltpu.roll(x, ROT // 2, 1))

    def load(g, carry):
        p, i = piece_of[m, g], inner_of[m, g]
        at = g - first_of[m, g]
        cosine, sine = cos_ref[at], sin_ref[at]
        rows = pl.ds(pl.multiple_of(g * BLK, BLK), BLK)
        for buf, start in ((q_buf, 0), (k_buf, HD)):
            front = qkv_ref[p, 0, i, :, start:start + 128]
            buf[rows, 0:128] = (front * cosine + turned(front) * sine).astype(bf16)
            buf[rows, 128:HD] = qkv_ref[p, 0, i, :, start + 128:start + HD].astype(bf16)
        v_buf[rows, :] = qkv_ref[p, 0, i, :, 2 * HD:].astype(bf16)
        return carry

    lax.fori_loop(0, blocks, load, 0)
    k_buf[blocks * BLK:, :] = jnp.zeros((BLK, HD), bf16)
    v_buf[blocks * BLK:, :] = jnp.zeros((BLK, HD), bf16)
    dk_buf[...] = jnp.zeros(dk_buf.shape, f32)
    dv_buf[...] = jnp.zeros(dv_buf.shape, f32)

    def attend(g, span):
        p, i = piece_of[m, g], inner_of[m, g]
        first = first_of[m, g]
        rows = pl.ds(pl.multiple_of(g * BLK, BLK), BLK)
        keys = pl.ds(pl.multiple_of(first * BLK, BLK), span)
        query, key, value = q_buf[rows, :], k_buf[keys, :], v_buf[keys, :]
        grad = grad_ref[p, 0, i]
        scores = dot(query, key, 1, 1) * SCALE
        key_tok = first * BLK + lax.broadcasted_iota(jnp.int32, (BLK, span), 1)
        query_tok = g * BLK + lax.broadcasted_iota(jnp.int32, (BLK, span), 0)
        allowed = (key_tok <= query_tok) & (key_tok < end_of[m, g])
        scores = jnp.where(allowed, scores, -jnp.inf)
        exponent = jnp.exp(scores - jnp.max(scores, axis=1, keepdims=True))
        prob = exponent * (1.0 / jnp.sum(exponent, axis=1, keepdims=True))
        prob_low = prob.astype(bf16)
        ctx_ref[p, 0, i] = dot(prob_low, value, 1, 0).astype(bf16)
        prob_grad = dot(grad, value, 1, 1)
        delta = jnp.sum(prob * prob_grad, axis=1, keepdims=True)
        score_grad = (prob * (prob_grad - delta)).astype(bf16)
        dk_buf[keys, :] += dot(score_grad, query, 0, 0)
        dv_buf[keys, :] += dot(prob_low, grad, 0, 0)
        query_grad = dot(score_grad, key, 1, 0) * SCALE
        at = g - first
        front = query_grad[:, 0:128]
        out_ref[p, 0, i, :, 0:128] = (front * cos_ref[at] - turned(front) * sin_ref[at]).astype(bf16)
        out_ref[p, 0, i, :, 128:HD] = query_grad[:, 128:].astype(bf16)

    def one_block(g, carry):
        pairs = (g - first_of[m, g]) // 2
        for count in range(SEQ_MOST // 2):
            pl.when(pairs == count)(lambda: attend(g, (count + 1) * 2 * BLK))
        return carry

    lax.fori_loop(0, blocks, one_block, 0)

    def store(g, carry):
        p, i = piece_of[m, g], inner_of[m, g]
        at = g - first_of[m, g]
        rows = pl.ds(pl.multiple_of(g * BLK, BLK), BLK)
        front = dk_buf[rows, 0:128] * SCALE
        out_ref[p, 0, i, :, HD:HD + 128] = (
            front * cos_ref[at] - turned(front) * sin_ref[at]
        ).astype(bf16)
        out_ref[p, 0, i, :, HD + 128:2 * HD] = (dk_buf[rows, 128:HD] * SCALE).astype(bf16)
        out_ref[p, 0, i, :, 2 * HD:] = dv_buf[rows, :].astype(bf16)
        return carry

    lax.fori_loop(0, blocks, store, 0)


def attention(tables, qkv, grad, cosine, sine):
    pieces, _, own = qkv.shape[:3]
    blocks = tables[0].shape[1]

    def part(width):
        return pl.BlockSpec((pieces, 1, own, BLK, width), lambda m, *_: (0, m, 0, 0, 0))

    whole = pl.BlockSpec((SEQ_MOST, BLK, 128), lambda m, *_: (0, 0, 0))
    rows = (blocks + 1) * BLK
    return pl.pallas_call(
        attention_kernel,
        grid_spec=pltpu.PrefetchScalarGridSpec(
            num_scalar_prefetch=4,
            grid=(MB,),
            in_specs=[part(3 * HD), part(HD), whole, whole],
            out_specs=[part(HD), part(3 * HD)],
            scratch_shapes=[
                pltpu.VMEM((rows, HD), bf16),
                pltpu.VMEM((rows, HD), bf16),
                pltpu.VMEM((rows, HD), bf16),
                pltpu.VMEM((rows, HD), f32),
                pltpu.VMEM((rows, HD), f32),
            ],
        ),
        out_shape=[
            jax.ShapeDtypeStruct((pieces, MB, own, BLK, HD), bf16),
            jax.ShapeDtypeStruct((pieces, MB, own, BLK, 3 * HD), bf16),
        ],
        compiler_params=pltpu.CompilerParams(vmem_limit_bytes=52 * 2**20),
        cost_estimate=pl.CostEstimate(
            flops=MB * blocks * 6 * BLK * 640 * HD * 2, bytes_accessed=30 * 2**20, transcendentals=2**21
        ),
    )(*tables, qkv, grad, cosine, sine)


def local(
    tokens, cotangent, seq_blocks, seq_pad, deal_order,
    ln1_gain, ln1_bias, ln2_gain, ln2_bias,
    qkv_weight, qkv_bias, out_weight, out_bias, up_weight, up_bias, down_weight, down_bias,
):
    shards = lax.axis_size("shard")
    place = lax.axis_index("shard")
    cube = shards == 8
    own = tokens.shape[1]
    blocks = deal_order.shape[2]
    own_rows = MB * own * BLK
    rows = shards * own_rows
    cols = D // shards
    wide = FF // shards
    split = shards // HEADS
    head, share = place // split, place % split
    share_cols = 3 * HD // split

    if cube:
        owners = jnp.bitwise_xor(place, jnp.array(ORDER, jnp.int32))
        spots = jnp.array(SPOT, jnp.int32)[jnp.bitwise_xor(place, jnp.arange(8))]
    else:
        owners = jnp.arange(shards, dtype=jnp.int32)
    deal = deal_order[:, 0, :]
    counts = seq_blocks[:, 0, :]
    pads = seq_pad[:, 0, :]
    ids = jnp.arange(blocks, dtype=jnp.int32)
    inverse = jnp.sum(
        jnp.where(deal[:, None, :] == ids[None, :, None], ids[None, None, :], 0), axis=-1
    )
    owner_of = inverse // own
    piece_of = jnp.sum(
        jnp.where(
            owner_of[:, :, None] == owners, jnp.arange(shards, dtype=jnp.int32)[None, None, :], 0
        ),
        axis=-1,
    )
    inner_of = inverse % own
    ends = jnp.cumsum(counts, axis=1)
    starts = ends - counts
    inside = (ids[None, :, None] >= starts[:, None, :]) & (ids[None, :, None] < ends[:, None, :])
    first_of = jnp.sum(jnp.where(inside, starts[:, None, :], 0), axis=-1)
    valid = jnp.sum(jnp.where(inside, (counts * BLK - pads)[:, None, :], 0), axis=-1)
    tables = [t.astype(jnp.int32) for t in (piece_of, inner_of, first_of, first_of * BLK + valid)]
    given = jnp.take(deal.reshape(MB, shards, own), owners, axis=1)

    cot_own = jnp.stack([cotangent[m][given[m]] for m in range(MB)], axis=1)
    if cube:
        cot_own = cot_own.reshape(2, 4, own_rows, cols)
        got = gather_pieces([cot_own[0], cot_own[1]])
        got = [jnp.concatenate(g, axis=0) for g in got]
        parts = []
        for r in ORDER:
            parts.append(jnp.concatenate([got[r][SPOT[o ^ r]] for o in ORDER], axis=0))
        grad_out = jnp.stack(parts)
        out_w = jnp.take(out_weight.reshape(-1, shards, cols), owners, axis=1)
        down_w = jnp.take(down_weight.reshape(-1, shards, cols), owners, axis=1)
    else:
        grad_out = lax.all_gather(cot_own.reshape(rows, cols), "shard", axis=0)
        out_w = out_weight.reshape(-1, shards, cols)
        down_w = down_weight.reshape(-1, shards, cols)

    params = jnp.concatenate([ln1_gain, ln1_bias, ln2_gain, ln2_bias, qkv_bias])
    params = lax.all_gather(params, "shard", axis=0).astype(f32)
    gain_one, shift_one, gain_two, shift_two = [
        params[:, i * cols:(i + 1) * cols].reshape(D) for i in range(4)
    ]
    bias_qkv = params[:, 4 * cols:].reshape(3, HEADS, HD)
    bias_qkv = lax.dynamic_index_in_dim(bias_qkv, head, 1, keepdims=False).reshape(3 * HD)

    up_send = up_weight.astype(f32) * ln2_gain.astype(f32)[:, None]
    up_send = up_send.astype(bf16).reshape(cols, shards, wide).transpose(1, 0, 2)
    up_w = lax.all_to_all(up_send, "shard", split_axis=0, concat_axis=0, tiled=True).reshape(D, wide)
    qkv_send = qkv_weight.astype(f32) * ln1_gain.astype(f32)[:, None]
    qkv_send = qkv_send.astype(bf16).reshape(cols, 3, HEADS, HD).transpose(2, 0, 1, 3)
    qkv_send = jnp.repeat(qkv_send.reshape(HEADS, cols, 3 * HD), split, axis=0)
    qkv_w = lax.all_to_all(qkv_send, "shard", split_axis=0, concat_axis=0, tiled=True)
    qkv_w = qkv_w.reshape(D, 3 * HD)

    bias_up = up_bias.astype(f32) + jnp.sum(up_w.astype(f32) * (shift_two / gain_two)[:, None], axis=0)
    bias_qkv = bias_qkv + jnp.sum(qkv_w.astype(f32) * (shift_one / gain_one)[:, None], axis=0)

    flat = tokens.reshape(own_rows, D).astype(f32)
    center = flat - jnp.mean(flat, axis=-1, keepdims=True)
    inv_std = lax.rsqrt(jnp.mean(center * center, axis=-1, keepdims=True) + EPS)
    normed_own = center * inv_std
    normed_low = normed_own.astype(bf16)
    if cube:
        half = own_rows // 2
        got = gather_pieces([normed_low[:half], normed_low[half:]])
        normed = jnp.concatenate([h for r in ORDER for h in got[r]], axis=0)
    else:
        normed = lax.all_gather(normed_low, "shard", axis=0, tiled=True)

    def back(weights):
        return lax.dot_general(
            grad_out, weights, (((0, 2), (1, 2)), ((), ())), preferred_element_type=f32
        ).astype(bf16)

    active_grad = back(down_w)
    hidden = dot(normed, up_w, 1, 0) + bias_up
    cdf = 0.5 + 0.5 * lax.erf(hidden * (0.5 ** 0.5))
    density = jnp.exp(-0.5 * hidden * hidden) * 0.3989422804014327
    active = (hidden * cdf).astype(bf16)
    hidden_grad = (active_grad.astype(f32) * (cdf + hidden * density)).astype(bf16)

    def spread(grads):
        return lax.all_to_all(
            grads.reshape(shards, cols, grads.shape[-1]), "shard", split_axis=0, concat_axis=0, tiled=True
        )

    def grad_dot(left):
        return lax.dot_general(
            left, grad_out, (((0,), (1,)), ((), ())), preferred_element_type=f32
        ).astype(bf16)

    down_sum = rep_sum(grad_dot(active))
    up_sum = rep_sum(spread(dot(normed, hidden_grad, 0, 0).astype(bf16)))

    context_w = out_w
    if split > 1:
        groups = [list(range(h * split, (h + 1) * split)) for h in range(HEADS)]
        context_w = lax.all_gather(out_w, "shard", axis=0, tiled=True, axis_index_groups=groups)
    context_grad = back(context_w)
    mixed = dot(normed, qkv_w, 1, 0) + bias_qkv
    cosine, sine = rotary_tables()
    context, mixed_grad = attention(
        tables,
        mixed.reshape(shards, MB, own, BLK, 3 * HD),
        context_grad.reshape(shards, MB, own, BLK, HD),
        cosine,
        sine,
    )
    context = context.reshape(rows, HD)
    mixed_grad = mixed_grad.reshape(rows, 3 * HD)
    if split > 1:
        context = lax.dynamic_slice_in_dim(context, share * (HD // split), HD // split, 1)
        mixed_grad = lax.dynamic_slice_in_dim(mixed_grad, share * share_cols, share_cols, 1)
        qkv_w = lax.dynamic_slice_in_dim(qkv_w, share * share_cols, share_cols, 1)
    qkv_sum = rep_sum(spread(dot(normed, mixed_grad, 0, 0).astype(bf16)))
    out_sum = rep_sum(grad_dot(context))

    both = jnp.concatenate([context, active], axis=1)
    both_w = jnp.concatenate([out_w, down_w], axis=0)
    resid = flat.reshape(own_rows, shards, cols)
    resid = jnp.take(resid, owners, axis=1) if cube else resid

    def out_terms(lo, hi):
        sums = lax.dot_general(both, both_w[:, lo:hi], (((1,), (0,)), ((), ())), preferred_element_type=f32)
        if cube:
            add = jnp.pad(resid[:, lo:hi], ((0, rows - own_rows), (0, 0), (0, 0)))
            sums = sums + add
        return sums.transpose(1, 0, 2)

    if cube:
        odd = out_terms(4, 8).astype(bf16).reshape(4, 2, rows // 2, cols)
        even = out_terms(0, 4).reshape(4, 2, rows // 2, cols)
        out_own = jnp.concatenate(
            reduce_pieces(odd, lambda came: (even + came.astype(f32)).astype(bf16), turn_rows), axis=0
        )
    else:
        terms = out_terms(0, shards)
        terms = lax.dynamic_update_slice(
            terms,
            lax.dynamic_slice(terms, (0, place * own_rows, 0), (shards, own_rows, cols))
            + resid.transpose(1, 0, 2),
            (0, place * own_rows, 0),
        )
        out_own = lax.psum_scatter(terms.astype(bf16), "shard", scatter_dimension=0, tiled=True)
        out_own = out_own.reshape(rows, cols).astype(f32)
    out_own = out_own + (out_bias.astype(f32) + down_bias.astype(f32))
    out_own = out_own.astype(bf16).reshape(shards, MB, own, BLK, cols)
    out_given = jnp.stack([out_own[piece_of[m], m, inner_of[m]] for m in range(MB)])

    both_grad = jnp.concatenate([mixed_grad, hidden_grad], axis=1)
    both_w = jnp.concatenate([qkv_w, up_w], axis=1)
    if cube:
        half = rows // 2
        odd = dot(both_grad[half:], both_w, 1, 1).astype(bf16).reshape(4, 2, -1, D)
        even = dot(both_grad[:half], both_w, 1, 1).reshape(4, 2, -1, D)
        normed_grad = jnp.concatenate(
            reduce_pieces(odd, lambda came: (even + came.astype(f32)).astype(bf16)), axis=0
        )
        grad_rows = jnp.take(grad_out[:, :own_rows], spots, axis=0)
    else:
        terms = dot(both_grad, both_w, 1, 1).astype(bf16)
        normed_grad = lax.psum_scatter(terms, "shard", scatter_dimension=0, tiled=True).astype(f32)
        grad_rows = lax.dynamic_slice_in_dim(grad_out, place * own_rows, own_rows, 1)
    grad_rows = grad_rows.transpose(1, 0, 2).reshape(own_rows, D).astype(f32)
    mean_grad = jnp.mean(normed_grad, axis=-1, keepdims=True)
    mean_proj = jnp.mean(normed_grad * normed_own, axis=-1, keepdims=True)
    tokens_grad = grad_rows + inv_std * (normed_grad - mean_grad - normed_own * mean_proj)
    tokens_grad = tokens_grad.astype(bf16).reshape(MB, own, BLK, D)

    small = jnp.concatenate(
        [
            jnp.sum(mixed_grad, axis=0, dtype=f32),
            jnp.sum(hidden_grad, axis=0, dtype=f32),
            jnp.sum(cot_own, axis=tuple(range(cot_own.ndim - 1)), dtype=f32),
        ]
    )
    small = jnp.sum(lax.all_gather(lax.all_gather(small, "rep"), "shard"), axis=1)
    sum_qkv = small[:, :share_cols].reshape(HEADS, 3, HD).transpose(1, 0, 2).reshape(3 * D)
    sum_up = small[:, share_cols:share_cols + wide].reshape(FF)
    out_bias_grad = lax.dynamic_index_in_dim(small[:, share_cols + wide:], place, 0, keepdims=False)
    qkv_bias_grad = lax.dynamic_slice_in_dim(sum_qkv, place * 3 * cols, 3 * cols)
    up_bias_grad = lax.dynamic_slice_in_dim(sum_up, place * wide, wide)

    qkv_rows = qkv_sum.reshape(HEADS, split, cols, share_cols).transpose(2, 0, 1, 3)
    qkv_rows = qkv_rows.reshape(cols, HEADS, 3, HD).transpose(0, 2, 1, 3).reshape(cols, 3 * D).astype(f32)
    up_rows = up_sum.transpose(1, 0, 2).reshape(cols, FF).astype(f32)

    def finish(sums, weight, gain, shift, total):
        weight_f = weight.astype(f32)
        grads = gain.astype(f32)[:, None] * sums + shift.astype(f32)[:, None] * total
        return grads, jnp.sum(weight_f * sums, axis=1), jnp.sum(weight_f * total, axis=1)

    qkv_grad, gain_one_grad, shift_one_grad = finish(qkv_rows, qkv_weight, ln1_gain, ln1_bias, sum_qkv)
    up_grad, gain_two_grad, shift_two_grad = finish(up_rows, up_weight, ln2_gain, ln2_bias, sum_up)

    def in_order(sums):
        sums = jnp.take(sums, spots, axis=1) if cube else sums
        return sums.reshape(-1, D).astype(f32)

    return (
        out_given,
        tokens_grad,
        gain_one_grad,
        shift_one_grad,
        gain_two_grad,
        shift_two_grad,
        qkv_grad,
        qkv_bias_grad,
        in_order(out_sum),
        out_bias_grad,
        up_grad,
        up_bias_grad,
        in_order(down_sum),
        out_bias_grad,
    )


def solution(mesh):
    in_specs = (
        P(None, ("rep", "shard"), None, None),
        P(None, "rep", None, "shard"),
        P(None, "rep", None),
        P(None, "rep", None),
        P(None, "rep", None),
        P("shard"),
        P("shard"),
        P("shard"),
        P("shard"),
        P("shard", None),
        P("shard"),
        P("shard", None),
        P("shard"),
        P("shard", None),
        P("shard"),
        P("shard", None),
        P("shard"),
    )
    out_specs = (
        P(None, "rep", None, "shard"),
        P(None, ("rep", "shard"), None, None),
        P("shard"),
        P("shard"),
        P("shard"),
        P("shard"),
        P("shard", None),
        P("shard"),
        P("shard", None),
        P("shard"),
        P("shard", None),
        P("shard"),
        P("shard", None),
        P("shard"),
    )
    return jax.shard_map(local, mesh=mesh, in_specs=in_specs, out_specs=out_specs, check_vma=False)
```

```python
import jax
import jax.numpy as jnp
from jax import lax
from jax.experimental import pallas as pl
from jax.experimental.pallas import tpu as pltpu
from jax.sharding import PartitionSpec as P

D = 2048
HEADS = 8
HD = 256
ROT = 64
FF = 8192
BLK = 128
SEQ_MOST = 8
MB = 2
EPS = 1e-05
SCALE = HD ** (-0.5)

bf16 = jnp.bfloat16
f32 = jnp.float32

ORDER = (0, 2, 4, 6, 1, 3, 5, 7)


def dot(a, b, ca, cb):
    return lax.dot_general(a, b, (((ca,), (cb,)), ((), ())), preferred_element_type=f32)


def flip(value, bit):
    return lax.ppermute(value, "shard", [(i, i ^ bit) for i in range(8)])


def tie(*values):
    return lax.optimization_barrier(values)


def plus(a, b):
    return a.astype(f32) + b.astype(f32)


def rep_in(value):
    return lax.ppermute(value, "rep", [(0, 1), (3, 2)])


def rep_over(value):
    return lax.ppermute(value, "rep", [(1, 2), (2, 1)])


def rep_out(value):
    return lax.ppermute(value, "rep", [(1, 0), (2, 3)])


def rotary_tables():
    half = ROT // 2
    freqs = 10000.0 ** (-2.0 * jnp.arange(half, dtype=f32) / ROT)
    angles = jnp.arange(SEQ_MOST * BLK, dtype=f32)[:, None] * freqs[None, :]
    rest = 128 - ROT
    cosine = jnp.concatenate(
        [jnp.cos(angles), jnp.cos(angles), jnp.ones((SEQ_MOST * BLK, rest), f32)], axis=-1
    )
    sine = jnp.concatenate(
        [-jnp.sin(angles), jnp.sin(angles), jnp.zeros((SEQ_MOST * BLK, rest), f32)], axis=-1
    )
    return cosine.reshape(SEQ_MOST, BLK, 128), sine.reshape(SEQ_MOST, BLK, 128)


def params_of(vmem=52):
    return pltpu.CompilerParams(vmem_limit_bytes=vmem * 2**20)


def cost(us):
    return pl.CostEstimate(flops=int(us * 1.1e9) + 1024, bytes_accessed=1024, transcendentals=0)


def tick(token, *arrays):
    def body(*refs):
        refs[-1][...] = refs[0][...]

    return pl.pallas_call(
        body,
        in_specs=[pl.BlockSpec(memory_space=pltpu.VMEM)] + [pl.BlockSpec(memory_space=pl.ANY)] * len(arrays),
        out_specs=pl.BlockSpec(memory_space=pltpu.VMEM),
        out_shape=jax.ShapeDtypeStruct(token.shape, token.dtype),
        compiler_params=params_of(16), cost_estimate=cost(2000),
    )(token, *arrays)


def spec(shape, index):
    return pl.BlockSpec(shape, index)


def attention_kernel(
    piece_of, inner_of, first_of, end_of,
    qkv_ref, grad_ref, cos_ref, sin_ref,
    ctx_ref, out_ref,
    q_buf, k_buf, v_buf, g_buf, dk_buf, dv_buf,
):
    m = pl.program_id(0)
    blocks = piece_of.shape[1]
    lane = lax.broadcasted_iota(jnp.int32, (BLK, 128), 1)
    tile = 2 * BLK

    def turned(x):
        return jnp.where(lane < ROT // 2, pltpu.roll(x, 128 - ROT // 2, 1), pltpu.roll(x, ROT // 2, 1))

    def block_rows(g):
        return pl.ds(pl.multiple_of(g * BLK, BLK), BLK)

    def load(g, carry):
        p, i = piece_of[m, g], inner_of[m, g]
        at = g - first_of[m, g]
        cosine, sine = cos_ref[at], sin_ref[at]
        rows = block_rows(g)
        for buf, start in ((q_buf, 0), (k_buf, HD)):
            front = qkv_ref[p, 0, i, :, start:start + 128]
            buf[rows, 0:128] = (front * cosine + turned(front) * sine).astype(bf16)
            buf[rows, 128:HD] = qkv_ref[p, 0, i, :, start + 128:start + HD].astype(bf16)
        v_buf[rows, :] = qkv_ref[p, 0, i, :, 2 * HD:].astype(bf16)
        g_buf[rows, :] = grad_ref[p, 0, i]
        return carry

    lax.fori_loop(0, blocks, load, 0)
    for buf in (q_buf, k_buf, v_buf, g_buf):
        buf[blocks * BLK:, :] = jnp.zeros((BLK, HD), bf16)
    dk_buf[...] = jnp.zeros(dk_buf.shape, f32)
    dv_buf[...] = jnp.zeros(dv_buf.shape, f32)

    def attend(g, span):
        first = first_of[m, g]
        rows = pl.ds(pl.multiple_of(g * BLK, BLK), tile)
        keys = pl.ds(pl.multiple_of(first * BLK, BLK), span)
        query, grad = q_buf[rows, :], g_buf[rows, :]
        key, value = k_buf[keys, :], v_buf[keys, :]
        after_g = jnp.minimum(g + 1, blocks - 1)
        second = (g + 1 < blocks) & (first_of[m, after_g] == first)
        scores = dot(query, key, 1, 1) * SCALE
        key_tok = first * BLK + lax.broadcasted_iota(jnp.int32, (tile, span), 1)
        query_tok = g * BLK + lax.broadcasted_iota(jnp.int32, (tile, span), 0)
        allowed = (key_tok <= query_tok) & (key_tok < end_of[m, g])
        scores = jnp.where(allowed, scores, -jnp.inf)
        exponent = jnp.exp(scores - jnp.max(scores, axis=1, keepdims=True))
        scale = 1.0 / jnp.sum(exponent, axis=1, keepdims=True)
        last_row = jnp.where(second, tile, BLK)
        row = lax.broadcasted_iota(jnp.int32, (tile, 1), 0)
        prob = exponent * jnp.where(row < last_row, scale, 0.0)
        prob_low = prob.astype(bf16)
        ctx = dot(prob_low, value, 1, 0).astype(bf16)
        prob_grad = dot(grad, value, 1, 1)
        delta = jnp.sum(prob * prob_grad, axis=1, keepdims=True)
        score_grad = (prob * (prob_grad - delta)).astype(bf16)
        dk_buf[keys, :] += dot(score_grad, query, 0, 0)
        dv_buf[keys, :] += dot(prob_low, grad, 0, 0)
        query_grad = dot(score_grad, key, 1, 0) * SCALE

        def put(block, lo):
            p, i = piece_of[m, block], inner_of[m, block]
            at = block - first
            ctx_ref[p, 0, i] = ctx[lo:lo + BLK]
            front = query_grad[lo:lo + BLK, 0:128]
            out_ref[p, 0, i, :, 0:128] = (
                front * cos_ref[at] - turned(front) * sin_ref[at]
            ).astype(bf16)
            out_ref[p, 0, i, :, 128:HD] = query_grad[lo:lo + BLK, 128:].astype(bf16)

        put(g, 0)
        pl.when(second)(lambda: put(after_g, BLK))

    def one_block(g, carry):
        at = g - first_of[m, g]
        for count in range(SEQ_MOST // 2):
            pl.when(at == 2 * count)(lambda: attend(g, (count + 1) * tile))
        return carry

    lax.fori_loop(0, blocks, one_block, 0)

    def store(g, carry):
        p, i = piece_of[m, g], inner_of[m, g]
        at = g - first_of[m, g]
        rows = block_rows(g)
        front = dk_buf[rows, 0:128] * SCALE
        out_ref[p, 0, i, :, HD:HD + 128] = (
            front * cos_ref[at] - turned(front) * sin_ref[at]
        ).astype(bf16)
        out_ref[p, 0, i, :, HD + 128:2 * HD] = (dk_buf[rows, 128:HD] * SCALE).astype(bf16)
        out_ref[p, 0, i, :, 2 * HD:] = dv_buf[rows, :].astype(bf16)
        return carry

    lax.fori_loop(0, blocks, store, 0)


def attention(tables, qkv, grad, cosine, sine):
    pieces, _, own = qkv.shape[:3]
    blocks = tables[0].shape[1]

    def part(width):
        return pl.BlockSpec((pieces, 1, own, BLK, width), lambda m, *_: (0, m, 0, 0, 0))

    whole = pl.BlockSpec((SEQ_MOST, BLK, 128), lambda m, *_: (0, 0, 0))
    rows = (blocks + 1) * BLK
    return pl.pallas_call(
        attention_kernel,
        grid_spec=pltpu.PrefetchScalarGridSpec(
            num_scalar_prefetch=4,
            grid=(MB,),
            in_specs=[part(3 * HD), part(HD), whole, whole],
            out_specs=[part(HD), part(3 * HD)],
            scratch_shapes=[
                pltpu.VMEM((rows, HD), bf16),
                pltpu.VMEM((rows, HD), bf16),
                pltpu.VMEM((rows, HD), bf16),
                pltpu.VMEM((rows, HD), bf16),
                pltpu.VMEM((rows, HD), f32),
                pltpu.VMEM((rows, HD), f32),
            ],
        ),
        out_shape=[
            jax.ShapeDtypeStruct((pieces, MB, own, BLK, HD), bf16),
            jax.ShapeDtypeStruct((pieces, MB, own, BLK, 3 * HD), bf16),
        ],
        compiler_params=params_of(),
        cost_estimate=cost(0),
    )(*tables, qkv, grad, cosine, sine)


def plus_low(a, b, index=None):
    shape = a.shape if index is None else a.shape[1:]
    if index is None:
        a, b, index = a[None], b[None], 0
    a, b = [x.reshape(x.shape[0], -1, x.shape[-1]) for x in (a, b)]
    rows, cols = a.shape[1:]
    block = spec((1, rows // 4, cols), lambda i: (index, i, 0))

    def body(a_ref, b_ref, out_ref):
        out_ref[...] = plus(a_ref[0], b_ref[0]).astype(bf16)

    return pl.pallas_call(
        body, grid=(4,), in_specs=[block, block],
        out_specs=spec((rows // 4, cols), lambda i: (i, 0)),
        out_shape=jax.ShapeDtypeStruct((rows, cols), bf16),
        compiler_params=params_of(32), cost_estimate=cost(0),
    )(a, b).reshape(shape)


def out_terms(owners, place, context, active, out_w, down_w, resid, came=None):
    rows, inner = active.shape
    n = resid.shape[0]
    cols = D // 8
    first = 4 if came is None else 0

    def terms(place_ref, refs):
        ctx, act = refs[0][...], refs[1][...]
        own = pl.program_id(0) == place_ref[0]
        return [
            dot(ctx, refs[2 + b][...], 1, 0)
            + dot(act, refs[6 + b][...], 1, 0)
            + jnp.where(own, refs[10 + b][...].astype(f32), 0.0)
            for b in range(4)
        ]

    def odd_body(owners_ref, place_ref, *refs):
        for b, part in enumerate(terms(place_ref, refs)):
            refs[14][b] = part.astype(bf16)

    def even_body(owners_ref, place_ref, *refs):
        got, send_one, keep_one, send_two, keep_two = refs[14:]
        parts = [(p + got[b].astype(f32)).astype(bf16) for b, p in enumerate(terms(place_ref, refs))]

        @pl.when(pl.program_id(0) < 4)
        def _():
            send_one[0], send_one[1] = parts[1], parts[3]
            keep_one[0], keep_one[1] = parts[0], parts[2]

        @pl.when(pl.program_id(0) >= 4)
        def _():
            send_two[0], send_two[1] = parts[2], parts[3]
            keep_two[0], keep_two[1] = parts[0], parts[1]

    def columns(height, b):
        return spec((height, cols), lambda i, o, p: (0, o[first + b]))

    in_specs = [
        spec((n, context.shape[1]), lambda i, o, p: (i, 0)),
        spec((n, inner), lambda i, o, p: (i, 0)),
        *[columns(context.shape[1], b) for b in range(4)],
        *[columns(inner, b) for b in range(4)],
        *[columns(n, b) for b in range(4)],
    ]
    args = [context, active, *[out_w] * 4, *[down_w] * 4, *[resid] * 4]
    if came is None:
        body = odd_body
        out_specs = spec((4, n, cols), lambda i, o, p: (0, i, 0))
        out_shape = jax.ShapeDtypeStruct((4, rows, cols), bf16)
    else:
        body = even_body
        in_specs.append(spec((4, n, cols), lambda i, o, p: (0, i, 0)))
        args.append(came)
        low = spec((2, n, cols), lambda i, o, p: (0, jnp.minimum(i, 3), 0))
        high = spec((2, n, cols), lambda i, o, p: (0, jnp.maximum(i - 4, 0), 0))
        out_specs = [low, low, high, high]
        out_shape = [jax.ShapeDtypeStruct((2, rows // 2, cols), bf16)] * 4
    return pl.pallas_call(
        body,
        grid_spec=pltpu.PrefetchScalarGridSpec(
            num_scalar_prefetch=2, grid=(8,), in_specs=in_specs, out_specs=out_specs
        ),
        out_shape=out_shape, compiler_params=params_of(), cost_estimate=cost(0),
    )(owners, place.reshape(1), *args)


def norm_terms(owners, mixed_grad, hidden_grad, qkv_w, up_w, came=None):
    rows = mixed_grad.shape[0]
    n = rows // 16
    first = 4 if came is None else 0

    def terms(refs):
        one, two, w_one, w_two = refs
        return dot(one[...], w_one[...], 1, 1) + dot(two[...], w_two[...], 1, 1)

    def odd_body(owners_ref, *refs):
        refs[4][0, 0] = terms(refs[:4]).astype(bf16)

    def even_body(owners_ref, *refs):
        got, send_one, keep_one, send_two, keep_two = refs[4:]
        sums = (terms(refs[:4]) + got[0, 0].astype(f32)).astype(bf16)
        i = pl.program_id(0)
        for ref, steps in (
            (keep_one, (0, 4)), (send_one, (2, 6)), (keep_two, (1, 3)), (send_two, (5, 7)),
        ):
            @pl.when((i == steps[0]) | (i == steps[1]))
            def _():
                ref[0] = sums

    def own_rows(i, o):
        return (o[first + i // 2] * 2 + i % 2, 0)

    in_specs = [
        spec((n, mixed_grad.shape[1]), own_rows),
        spec((n, hidden_grad.shape[1]), own_rows),
        spec(qkv_w.shape, lambda i, o: (0, 0)),
        spec(up_w.shape, lambda i, o: (0, 0)),
    ]
    args = [mixed_grad, hidden_grad, qkv_w, up_w]
    if came is None:
        body = odd_body
        out_specs = spec((1, 1, n, D), lambda i, o: (i // 2, i % 2, 0, 0))
        out_shape = jax.ShapeDtypeStruct((4, 2, n, D), bf16)
    else:
        body = even_body
        in_specs.append(spec((1, 1, n, D), lambda i, o: (i // 2, i % 2, 0, 0)))
        args.append(came)
        out_specs = [
            spec((1, n, D), lambda i, o: (i // 4, 0, 0)),
            spec((1, n, D), lambda i, o: (i // 4, 0, 0)),
            spec((1, n, D), lambda i, o: (jnp.maximum(i - 4, 0) // 2, 0, 0)),
            spec((1, n, D), lambda i, o: (jnp.minimum(i // 2, 1), 0, 0)),
        ]
        out_shape = [jax.ShapeDtypeStruct((2, n, D), bf16)] * 4
    return pl.pallas_call(
        body,
        grid_spec=pltpu.PrefetchScalarGridSpec(
            num_scalar_prefetch=1, grid=(8,), in_specs=in_specs, out_specs=out_specs
        ),
        out_shape=out_shape, compiler_params=params_of(), cost_estimate=cost(0),
    )(owners, *args)


def token_dot(left, right, part=0, parts=1):
    rows, width = left.shape[0], left.shape[1] // parts
    blocks, _, cols = right.shape
    step = 512 // cols

    def body(left_ref, right_ref, out_ref):
        for b in range(step):
            out_ref[:, b * cols:(b + 1) * cols] = dot(left_ref[...], right_ref[b], 0, 0).astype(bf16)

    return pl.pallas_call(
        body, grid=(blocks // step,),
        in_specs=[
            spec((rows, width), lambda i: (0, part)),
            spec((step, rows, cols), lambda i: (i, 0, 0)),
        ],
        out_specs=spec((width, step * cols), lambda i: (0, i)),
        out_shape=jax.ShapeDtypeStruct((width, blocks * cols), bf16),
        compiler_params=params_of(56), cost_estimate=cost(0),
    )(left, right)


def normed_dot(normed, right, sums=False, part=0, parts=1):
    rows, tile = normed.shape[0], 512

    def body(left_ref, right_ref, out_ref, *rest):
        out_ref[...] = dot(left_ref[...], right_ref[...], 0, 0).astype(bf16)
        if sums:
            @pl.when(pl.program_id(0) == 0)
            def _():
                rest[0][...] = jnp.sum(right_ref[...].astype(f32), axis=0, keepdims=True)

    width = right.shape[1] // parts
    out_specs = [spec((tile, width), lambda i: (i, 0))]
    out_shape = [jax.ShapeDtypeStruct((D, width), bf16)]
    if sums:
        out_specs.append(spec((1, width), lambda i: (0, 0)))
        out_shape.append(jax.ShapeDtypeStruct((1, width), f32))
    found = pl.pallas_call(
        body, grid=(D // tile,),
        in_specs=[spec((rows, tile), lambda i: (0, i)), spec((rows, width), lambda i: (0, part))],
        out_specs=out_specs, out_shape=out_shape,
        compiler_params=params_of(56), cost_estimate=cost(0),
    )(normed, right)
    return found if sums else found[0]


def whole_rows(ref):
    return jnp.concatenate([ref[b] for b in range(ref.shape[0])], axis=1)


def hidden_back(grad_out, down_w, slope):
    rows, wide = slope.shape
    n = rows // 8

    def body(grad_ref, w_ref, slope_ref, out_ref, sum_ref):
        active_grad = dot(whole_rows(grad_ref), w_ref[...], 1, 1).astype(bf16).astype(f32)
        value = (active_grad * slope_ref[...]).astype(bf16)
        out_ref[...] = value
        total = jnp.sum(value.astype(f32), axis=0, keepdims=True)

        @pl.when(pl.program_id(0) == 0)
        def _():
            sum_ref[...] = total

        @pl.when(pl.program_id(0) > 0)
        def _():
            sum_ref[...] += total

    return pl.pallas_call(
        body, grid=(8,),
        in_specs=[
            spec((grad_out.shape[0], n, grad_out.shape[2]), lambda i: (0, i, 0)),
            spec((wide, D), lambda i: (0, 0)),
            spec((n, wide), lambda i: (i, 0)),
        ],
        out_specs=[spec((n, wide), lambda i: (i, 0)), spec((1, wide), lambda i: (0, 0))],
        out_shape=[
            jax.ShapeDtypeStruct((rows, wide), bf16), jax.ShapeDtypeStruct((1, wide), f32),
        ],
        compiler_params=params_of(), cost_estimate=cost(0),
    )(grad_out, down_w, slope)


def head_back(grad_out, out_w):
    blocks, rows, cols = grad_out.shape
    n = rows // 8

    def body(grad_ref, w_ref, out_ref):
        out_ref[...] = dot(whole_rows(grad_ref), w_ref[...], 1, 1).astype(bf16)

    return pl.pallas_call(
        body, grid=(8,),
        in_specs=[
            spec((blocks, n, cols), lambda i: (0, i, 0)),
            spec((HD, D), lambda i: (0, 0)),
        ],
        out_specs=spec((n, HD), lambda i: (i, 0)),
        out_shape=jax.ShapeDtypeStruct((rows, HD), bf16),
        compiler_params=params_of(), cost_estimate=cost(0),
    )(grad_out, out_w)


def row_grads(inner, chunks):
    rows = [c[0].shape[0] for c in chunks]
    total, cols = sum(rows), 512

    def body(inner_ref, *refs):
        at = 0
        for c, n in enumerate(rows):
            one, two = refs[2 * c][...].astype(f32), refs[2 * c + 1][...].astype(f32)
            refs[-1][at:at + n, :] = jnp.where(inner_ref[0] == 1, one, two)
            at += n

    return pl.pallas_call(
        body,
        grid_spec=pltpu.PrefetchScalarGridSpec(
            num_scalar_prefetch=1, grid=(D // cols,),
            in_specs=[spec((n, cols), lambda i, *_: (0, i)) for n in rows for _ in range(2)],
            out_specs=spec((total, cols), lambda i, *_: (0, i)),
        ),
        out_shape=jax.ShapeDtypeStruct((total, D), f32),
        compiler_params=params_of(32), cost_estimate=cost(0),
    )(inner, *[a for c in chunks for a in c])


def column_grads(inner, chunks, weight, gain, shift, totals, run, step, by_run, token=None):
    rows, each = weight.shape[0], len(chunks[0])
    if by_run:
        groups, per = len(chunks), chunks[0][0].shape[0] // step
        steps = per
    else:
        groups, per = chunks[0][0].shape[2] // run, chunks[0][0].shape[0] // step
        steps = per * len(chunks)

    tokens = [] if token is None else [token]

    def body(inner_ref, *refs):
        pairs, refs = refs[:each * len(chunks)], refs[each * len(chunks) + len(tokens):]
        w_ref, t_ref, gain_ref, shift_ref, grads, gain_out, shift_out = refs[-7:]
        i, k = pl.program_id(0), pl.program_id(1)

        @pl.when((i == 0) & (k == 0))
        def _():
            gain_out[...] = jnp.zeros_like(gain_out)
            shift_out[...] = jnp.zeros_like(shift_out)

        for c in range(len(chunks)):
            @pl.when((k if by_run else i // per) == c)
            def _():
                for j in range(step):
                    value = pairs[each * c][j].astype(f32)
                    if each == 2:
                        other = pairs[2 * c + 1][j].astype(f32)
                        value = jnp.where(inner_ref[0] == 1, value, other)
                    at = slice(j * run, (j + 1) * run)
                    w, t = w_ref[:, at].astype(f32), t_ref[:, at]
                    grads[:, at] = gain_ref[...] * value + shift_ref[...] * t
                    for out, terms in ((gain_out, w * value), (shift_out, w * t)):
                        out[...] += sum(terms[:, lo:lo + 128] for lo in range(0, run, 128))

    def part_index(c):
        if by_run:
            return lambda i, k, *_: (i, 0, 0)
        return lambda i, k, *_: (jnp.clip(i - c * per, 0, per - 1), 0, k)

    def columns(i, k, *_):
        return (0, i * groups + k if by_run else k * steps + i)

    column = spec((rows, 1), lambda i, k, *_: (0, 0))
    wide_column = spec((rows, 128), lambda i, k, *_: (0, 0))
    grads, gain_grad, shift_grad = pl.pallas_call(
        body,
        grid_spec=pltpu.PrefetchScalarGridSpec(
            num_scalar_prefetch=1, grid=(steps, groups),
            in_specs=[spec((step, rows, run), part_index(c)) for c in range(len(chunks)) for _ in range(each)]
            + [pl.BlockSpec(memory_space=pl.ANY)] * len(tokens)
            + [spec((rows, step * run), columns), spec((1, step * run), columns), column, column],
            out_specs=[spec((rows, step * run), columns), wide_column, wide_column],
        ),
        out_shape=[
            jax.ShapeDtypeStruct(weight.shape, f32),
            jax.ShapeDtypeStruct((rows, 128), f32),
            jax.ShapeDtypeStruct((rows, 128), f32),
        ],
        compiler_params=params_of(32), cost_estimate=cost(0),
    )(
        inner, *[a for c in chunks for a in c], *tokens, weight, totals[None],
        gain.astype(f32)[:, None], shift.astype(f32)[:, None],
    )
    return grads, jnp.sum(gain_grad, axis=1), jnp.sum(shift_grad, axis=1)


def local(
    tokens, cotangent, seq_blocks, seq_pad, deal_order,
    ln1_gain, ln1_bias, ln2_gain, ln2_bias,
    qkv_weight, qkv_bias, out_weight, out_bias, up_weight, up_bias, down_weight, down_bias,
):
    shards = lax.axis_size("shard")
    place = lax.axis_index("shard")
    cube = shards == 8 and lax.axis_size("rep") == 4
    own = tokens.shape[1]
    blocks = deal_order.shape[2]
    own_rows = MB * own * BLK
    rows = shards * own_rows
    cols = D // shards
    wide = FF // shards
    split = shards // HEADS
    head, share = place // split, place % split
    share_cols = 3 * HD // split

    if cube:
        owners = jnp.bitwise_xor(place, jnp.array(ORDER, jnp.int32))
    deal = deal_order[:, 0, :]
    counts = seq_blocks[:, 0, :]
    pads = seq_pad[:, 0, :]
    ids = jnp.arange(blocks, dtype=jnp.int32)
    inverse = jnp.sum(
        jnp.where(deal[:, None, :] == ids[None, :, None], ids[None, None, :], 0), axis=-1
    )
    piece_of, inner_of = inverse // own, inverse % own
    ends = jnp.cumsum(counts, axis=1)
    starts = ends - counts
    inside = (ids[None, :, None] >= starts[:, None, :]) & (ids[None, :, None] < ends[:, None, :])
    first_of = jnp.sum(jnp.where(inside, starts[:, None, :], 0), axis=-1)
    valid = jnp.sum(jnp.where(inside, (counts * BLK - pads)[:, None, :], 0), axis=-1)
    tables = [t.astype(jnp.int32) for t in (piece_of, inner_of, first_of, first_of * BLK + valid)]
    given = deal.reshape(MB, shards, own)

    cot_own = jnp.stack([cotangent[m][given[m]] for m in range(MB)], axis=1)

    def swap(value):
        return lax.all_to_all(value, "shard", split_axis=0, concat_axis=0, tiled=True)

    token = jnp.zeros((8, 128), f32)

    def gate(*arrays):
        nonlocal token
        if cube:
            token = tick(token, *arrays)

    def late(value):
        nonlocal token
        if cube:
            value, token = tie(value, token)
        return value

    flat = tokens.reshape(own_rows, D).astype(f32)
    center = flat - jnp.mean(flat, axis=-1, keepdims=True)
    inv_std = lax.rsqrt(jnp.mean(center * center, axis=-1, keepdims=True) + EPS)
    normed_own = center * inv_std
    normed_low = normed_own.astype(bf16)
    normed = lax.all_gather(normed_low, "shard", axis=0, tiled=True)
    gate(normed_low)

    shares = lax.axis_size("rep") if cube else 1
    part_rows = cols // shares
    spot = lax.axis_index("rep") if cube else 0
    up_late, qkv_late = late((up_weight, qkv_weight))

    def part_of(array):
        return lax.dynamic_slice_in_dim(array, spot * part_rows, part_rows, 0).astype(f32)

    def with_shift(weight, gain, shift):
        high = lax.reduce_precision(shift, 8, 7)
        low = lax.reduce_precision(shift - high, 8, 7)
        tail = jnp.zeros((14, shift.shape[0]), bf16)
        scaled = (part_of(weight) * part_of(gain)[:, None]).astype(bf16)
        return jnp.concatenate([scaled, high.astype(bf16)[None], low.astype(bf16)[None], tail], axis=0)

    shift_up = jnp.sum(up_late.astype(f32) * ln2_bias.astype(f32)[:, None], axis=0)
    shift_qkv = jnp.sum(qkv_late.astype(f32) * ln1_bias.astype(f32)[:, None], axis=0)
    own_bias = lax.dynamic_slice_in_dim(shift_qkv, place * 3 * cols, 3 * cols) + qkv_bias.astype(f32)
    shift_qkv = lax.dynamic_update_slice_in_dim(shift_qkv, own_bias, place * 3 * cols, 0)
    sent_rows = part_rows + 16
    up_send = with_shift(up_late, ln2_gain, shift_up).reshape(sent_rows, shards, wide).transpose(1, 0, 2)
    qkv_send = with_shift(qkv_late, ln1_gain, shift_qkv).reshape(sent_rows, 3, HEADS, HD)
    qkv_send = qkv_send.transpose(2, 0, 1, 3).reshape(HEADS, sent_rows, 3 * HD)
    if split > 1:
        qkv_send = jnp.repeat(qkv_send, split, axis=0)
    found = swap(jnp.concatenate([up_send, qkv_send], axis=2))
    cot_late = late(cot_own)
    grad_out = lax.all_gather(cot_late.reshape(rows, cols), "shard", axis=0)
    gate(up_send, qkv_send, cot_late)
    found = late(found)
    biases = jnp.sum(found[:, part_rows:part_rows + 2].astype(f32), axis=(0, 1))
    bias_up, bias_qkv = biases[:wide] + up_bias.astype(f32), biases[wide:]

    def exchange(part):
        return [part] + [
            lax.ppermute(part, "rep", [(i, (i + k) % shares) for i in range(shares)])
            for k in range(1, shares)
        ]

    def whole(parts):
        if shares == 1:
            return parts[0].reshape(D, parts[0].shape[-1])
        width = parts[0].shape[-1]
        array = jnp.zeros((shards, shares, part_rows, width), bf16)
        for k, part in enumerate(parts):
            at = lax.rem(spot - k + shares, shares)
            array = lax.dynamic_update_slice(array, part[:, None], (0, at, 0, 0))
        return array.reshape(D, width)

    up_parts = exchange(found[:, :part_rows, :wide])
    gate(up_parts[0], biases)
    qkv_parts = exchange(late(found)[:, :part_rows, wide:])
    normed, up_parts = late((normed, up_parts))
    up_w = whole(up_parts)
    out_w, down_w, resid = out_weight, down_weight, tokens.reshape(own_rows, D)

    hidden = dot(normed, up_w, 1, 0) + bias_up
    cdf = 0.5 + 0.5 * lax.erf(hidden * (0.5 ** 0.5))
    density = jnp.exp(-0.5 * hidden * hidden) * 0.3989422804014327
    active = (hidden * cdf).astype(bf16)
    slope = cdf + hidden * density
    grad_out, active = tie(grad_out, active)

    def spread(grads):
        return swap(grads.reshape(shards, cols, grads.shape[-1]))

    down_parts = [token_dot(active, grad_out, 0, 2)]
    down_came = [rep_in(down_parts[0])]
    gate(down_parts[0])
    down_parts.append(token_dot(late(active), grad_out, 1, 2))
    grad_out, down_parts[1] = tie(grad_out, down_parts[1])
    hidden_grad, sum_hidden = hidden_back(grad_out, down_w, slope)
    up_terms = [normed_dot(normed, hidden_grad, False, 0, 2)]
    up_found = [spread(up_terms[0])]
    down_came[0], up_terms[0] = tie(down_came[0], up_terms[0])
    down_pair = [plus_low(down_parts[0], down_came[0])]
    down_other = [rep_over(down_pair[0])]
    down_came.append(rep_in(down_parts[1]))
    gate(down_pair[0], up_terms[0])

    context_w = out_w
    if split > 1:
        pairs = [list(range(h * split, (h + 1) * split)) for h in range(HEADS)]
        context_w = lax.all_gather(out_w, "shard", axis=0, tiled=True, axis_index_groups=pairs)
    up_terms.append(normed_dot(late(normed), hidden_grad, False, 1, 2))
    grad_out, up_terms[1] = tie(grad_out, up_terms[1])
    context_grad = head_back(grad_out, context_w)
    qkv_parts, context_grad = tie(qkv_parts, context_grad)
    qkv_w = whole(qkv_parts)
    mixed = dot(normed, qkv_w, 1, 0) + bias_qkv
    down_other[0], down_came[1], up_found[0], mixed = tie(down_other[0], down_came[1], up_found[0], mixed)
    down_total = [plus_low(down_pair[0], down_other[0])]
    down_back = [rep_out(down_total[0])]
    down_pair.append(plus_low(down_parts[1], down_came[1]))
    down_other.append(rep_over(down_pair[1]))
    up_came = [rep_in(up_found[0])]
    up_terms[1], up_found[0] = tie(up_terms[1], up_found[0])
    up_found.append(spread(up_terms[1]))
    gate(down_total[0], down_pair[1], up_found[0])
    cosine, sine = rotary_tables()
    context, mixed_grad = attention(
        tables,
        late(mixed).reshape(shards, MB, own, BLK, 3 * HD),
        context_grad.reshape(shards, MB, own, BLK, HD),
        cosine,
        sine,
    )
    context = context.reshape(rows, HD)
    mixed_grad = mixed_grad.reshape(rows, 3 * HD)
    down_back[0], down_other[1], up_came[0], up_found[1], context = tie(
        down_back[0], down_other[1], up_came[0], up_found[1], context
    )
    down_total.append(plus_low(down_pair[1], down_other[1]))
    down_back.append(rep_out(down_total[1]))
    up_pair = [plus_low(up_found[0], up_came[0])]
    up_other = [rep_over(up_pair[0])]
    up_came.append(rep_in(up_found[1]))
    gate(down_back[0], down_total[1], up_pair[0], up_found[1])
    mixed_grad = late(mixed_grad)
    if split > 1:
        context = lax.dynamic_slice_in_dim(context, share * (HD // split), HD // split, 1)
        mixed_grad = lax.dynamic_slice_in_dim(mixed_grad, share * share_cols, share_cols, 1)
        qkv_w = lax.dynamic_slice_in_dim(qkv_w, share * share_cols, share_cols, 1)
    qkv_terms, sum_mixed = normed_dot(normed, mixed_grad, True)
    qkv_found = spread(qkv_terms)
    sum_cot = jnp.sum(cot_own, axis=tuple(range(cot_own.ndim - 1)), dtype=f32)
    small = jnp.concatenate([sum_mixed[0], sum_hidden[0], sum_cot])

    def bias_grads(small):
        sum_qkv = small[:, :share_cols].reshape(HEADS, 3, HD).transpose(1, 0, 2).reshape(3 * D)
        sum_up = small[:, share_cols:share_cols + wide].reshape(FF)
        out_bias_grad = lax.dynamic_index_in_dim(small[:, share_cols + wide:], place, 0, keepdims=False)
        qkv_bias_grad = lax.dynamic_slice_in_dim(sum_qkv, place * 3 * cols, 3 * cols)
        up_bias_grad = lax.dynamic_slice_in_dim(sum_up, place * wide, wide)
        return sum_qkv, sum_up, out_bias_grad, qkv_bias_grad, up_bias_grad

    if cube:
        small_came = lax.ppermute(small, "rep", [(i, i ^ 1) for i in range(4)])
        context, qkv_terms = tie(context, qkv_terms)
        out_part = token_dot(context, grad_out)
        out_came = rep_in(out_part)

        context, out_part = tie(context, out_part)
        odd = out_terms(owners, place, context, active, out_w, down_w, resid)
        odd_came = flip(odd, 1)
        down_back[1], up_other[0], up_came[1], odd = tie(down_back[1], up_other[0], up_came[1], odd)
        up_total = [plus_low(up_pair[0], up_other[0])]
        up_back = [rep_out(up_total[0])]
        up_pair.append(plus_low(up_found[1], up_came[1]))
        up_other.append(rep_over(up_pair[1]))
        gate(down_back[1], up_total[0], up_pair[1], small, qkv_terms, odd)

        norm_odd = norm_terms(owners, late(mixed_grad), hidden_grad, qkv_w, up_w)
        norm_odd_came = flip(norm_odd, 1)
        odd_came, norm_odd = tie(odd_came, norm_odd)
        send_one, keep_one, send_two, keep_two = out_terms(
            owners, place, context, active, out_w, down_w, resid, odd_came
        )
        got_one, got_two = flip(send_one, 2), flip(send_two, 4)
        up_back[0], up_other[1], out_came, qkv_found, keep_one = tie(
            up_back[0], up_other[1], out_came, qkv_found, keep_one
        )
        up_total.append(plus_low(up_pair[1], up_other[1]))
        up_back.append(rep_out(up_total[1]))
        out_pair = plus_low(out_part, out_came)
        out_other = rep_over(out_pair)
        qkv_parts = [qkv_found[:shards // 2], qkv_found[shards // 2:]]
        qkv_came = [rep_in(part) for part in qkv_parts]
        gate(up_back[0], up_total[1], out_pair, *qkv_parts, norm_odd, send_one)

        norm_send_one, norm_keep_one, norm_send_two, norm_keep_two = norm_terms(
            owners, mixed_grad, hidden_grad, qkv_w, up_w, late(norm_odd_came)
        )
        norm_got_one, norm_got_two = flip(norm_send_one, 2), flip(norm_send_two, 4)

        out_other, qkv_came[0], norm_keep_one = tie(out_other, qkv_came[0], norm_keep_one)
        out_total = plus_low(out_pair, out_other)
        out_back = rep_out(out_total)
        qkv_pair = [plus_low(qkv_parts[0], qkv_came[0])]
        qkv_other = [rep_over(qkv_pair[0])]
        got_one, got_two, up_back[1], out_total, qkv_pair[0] = tie(
            got_one, got_two, up_back[1], out_total, qkv_pair[0]
        )
        last_one = plus_low(keep_one, got_one, 1)
        last_two = plus_low(keep_two, got_two, 1)
        qkv_came[1], last_one, last_two, up_back[1] = tie(qkv_came[1], last_one, last_two, up_back[1])
        last_one, last_two = flip(last_one, 4), flip(last_two, 2)
        qkv_pair.append(plus_low(qkv_parts[1], qkv_came[1]))
        qkv_other.append(rep_over(qkv_pair[1]))
        down_late, small_came, qkv_pair[1] = tie(
            list(zip(down_total, down_back)), small_came, qkv_pair[1]
        )
        inner = ((spot == 1) | (spot == 2)).astype(jnp.int32).reshape(1)
        down_grad = row_grads(inner, down_late)
        small_pair = small + small_came
        small_other = lax.ppermute(small_pair, "rep", [(i, i ^ 2) for i in range(4)])
        qkv_other[0], out_back, down_grad, small_pair = tie(qkv_other[0], out_back, down_grad, small_pair)
        qkv_total = [plus_low(qkv_pair[0], qkv_other[0])]
        qkv_back = [rep_out(qkv_total[0])]
        out_back, grad_late, qkv_total[0] = tie(out_back, grad_out, qkv_total[0])
        out_grad = row_grads(inner, [(out_total, out_back)])
        grad_rows = lax.dynamic_slice_in_dim(grad_late, place * own_rows, own_rows, 1)
        grad_rows = grad_rows.transpose(1, 0, 2).reshape(own_rows, D)
        norm_got_one, norm_got_two, out_grad, grad_rows = tie(
            norm_got_one, norm_got_two, out_grad, grad_rows
        )
        norm_last_one = plus_low(norm_keep_one, norm_got_one, 1)
        norm_last_two = plus_low(norm_keep_two, norm_got_two, 1)
        qkv_other[1], small_other, norm_last_one, norm_last_two = tie(
            qkv_other[1], small_other, norm_last_one, norm_last_two
        )
        norm_last_one, norm_last_two = flip(norm_last_one, 4), flip(norm_last_two, 2)
        qkv_total.append(plus_low(qkv_pair[1], qkv_other[1]))
        qkv_back.append(rep_out(qkv_total[1]))
        small_pair = small_pair + small_other
        small = swap(jnp.broadcast_to(small_pair[None], (shards,) + small_pair.shape))
        last_one, last_two, qkv_total[1], small_pair = tie(last_one, last_two, qkv_total[1], small_pair)
        out_own = jnp.concatenate(
            [
                plus(keep_one[0], got_one[0]) + last_one.astype(f32),
                plus(keep_two[0], got_two[0]) + last_two.astype(f32),
            ],
            axis=0,
        )
        norm_last_one, norm_last_two, qkv_back[0], out_own = tie(
            norm_last_one, norm_last_two, qkv_back[0], out_own
        )
        normed_grad = jnp.concatenate(
            [
                plus(norm_keep_one[0], norm_got_one[0]) + norm_last_one.astype(f32),
                plus(norm_keep_two[0], norm_got_two[0]) + norm_last_two.astype(f32),
            ],
            axis=0,
        )
    else:
        small = lax.all_gather(lax.psum(small, "rep"), "shard")
        sum_qkv, sum_up, out_bias_grad, qkv_bias_grad, up_bias_grad = bias_grads(small)
        out_sum, qkv_sum, up_sum, down_sum = lax.psum(
            (token_dot(context, grad_out), qkv_found, jnp.concatenate(up_found, axis=2), jnp.concatenate(down_parts)), "rep"
        )
        terms = dot(context, out_w, 1, 0) + dot(active, down_w, 1, 0)
        terms = lax.dynamic_update_slice_in_dim(
            terms,
            lax.dynamic_slice_in_dim(terms, place * own_rows, own_rows, 0) + resid.astype(f32),
            place * own_rows,
            0,
        )
        out_own = lax.psum_scatter(terms.astype(bf16), "shard", scatter_dimension=1, tiled=True)
        out_own = out_own.astype(f32)
        terms = dot(mixed_grad, qkv_w, 1, 1) + dot(hidden_grad, up_w, 1, 1)
        normed_grad = lax.psum_scatter(terms.astype(bf16), "shard", scatter_dimension=0, tiled=True)
        normed_grad = normed_grad.astype(f32)
        grad_rows = lax.dynamic_slice_in_dim(grad_out, place * own_rows, own_rows, 1)
        grad_rows = grad_rows.transpose(1, 0, 2).reshape(own_rows, D)

    out_own = out_own + (out_bias.astype(f32) + down_bias.astype(f32))
    out_own = out_own.astype(bf16).reshape(shards, MB, own, BLK, cols)
    out_given = jnp.stack([out_own[piece_of[m], m, inner_of[m]] for m in range(MB)])

    mean_grad = jnp.mean(normed_grad, axis=-1, keepdims=True)
    mean_proj = jnp.mean(normed_grad * normed_own, axis=-1, keepdims=True)
    tokens_grad = inv_std * (normed_grad - mean_grad - normed_own * mean_proj)
    tokens_grad = grad_rows.astype(f32) + tokens_grad
    tokens_grad = tokens_grad.astype(bf16).reshape(MB, own, BLK, D)

    if cube:
        small, tokens_grad = tie(small, tokens_grad)
        sum_qkv, sum_up, out_bias_grad, qkv_bias_grad, up_bias_grad = bias_grads(small)
        up_grad, gain_two_grad, shift_two_grad = column_grads(
            inner, list(zip(up_total, up_back)), up_weight, ln2_gain, ln2_bias, sum_up, wide // 2, 1, True
        )
        qkv_back, up_grad = tie(qkv_back, up_grad)
        qkv_grad, gain_one_grad, shift_one_grad = column_grads(
            inner, list(zip(qkv_total, qkv_back)), qkv_weight, ln1_gain, ln1_bias, sum_qkv, HD, 2, False, token
        )
    else:
        def finish(sums, weight, gain, shift, total):
            sums = sums.astype(f32)
            grads = gain.astype(f32)[:, None] * sums + shift.astype(f32)[:, None] * total
            weight = weight.astype(f32)
            return grads, jnp.sum(weight * sums, axis=1), jnp.sum(weight * total, axis=1)

        qkv_rows = qkv_sum.reshape(HEADS, split, cols, share_cols).transpose(2, 0, 1, 3)
        qkv_rows = qkv_rows.reshape(cols, HEADS, 3, HD).transpose(0, 2, 1, 3).reshape(cols, 3 * D)
        up_rows = up_sum.transpose(1, 0, 2).reshape(cols, FF)
        qkv_grad, gain_one_grad, shift_one_grad = finish(
            qkv_rows, qkv_weight, ln1_gain, ln1_bias, sum_qkv
        )
        out_grad = out_sum.astype(f32)
        down_grad = down_sum.astype(f32)
        up_grad, gain_two_grad, shift_two_grad = finish(
            up_rows, up_weight, ln2_gain, ln2_bias, sum_up
        )

    return (
        out_given,
        tokens_grad,
        gain_one_grad.reshape(cols),
        shift_one_grad.reshape(cols),
        gain_two_grad.reshape(cols),
        shift_two_grad.reshape(cols),
        qkv_grad,
        qkv_bias_grad,
        out_grad,
        out_bias_grad,
        up_grad,
        up_bias_grad,
        down_grad,
        out_bias_grad,
    )


def solution(mesh):
    in_specs = (
        P(None, ("rep", "shard"), None, None),
        P(None, "rep", None, "shard"),
        P(None, "rep", None),
        P(None, "rep", None),
        P(None, "rep", None),
        P("shard"),
        P("shard"),
        P("shard"),
        P("shard"),
        P("shard", None),
        P("shard"),
        P("shard", None),
        P("shard"),
        P("shard", None),
        P("shard"),
        P("shard", None),
        P("shard"),
    )
    out_specs = (
        P(None, "rep", None, "shard"),
        P(None, ("rep", "shard"), None, None),
        P("shard"),
        P("shard"),
        P("shard"),
        P("shard"),
        P("shard", None),
        P("shard"),
        P("shard", None),
        P("shard"),
        P("shard", None),
        P("shard"),
        P("shard", None),
        P("shard"),
    )
    return jax.shard_map(local, mesh=mesh, in_specs=in_specs, out_specs=out_specs, check_vma=False)
```

```python
import jax
import jax.numpy as jnp
from jax import lax
from jax.experimental import pallas as pl
from jax.experimental.pallas import tpu as pltpu
from jax.sharding import PartitionSpec as P

D = 2048
HEADS = 8
HD = 256
ROT = 64
FF = 8192
BLK = 128
SEQ_MOST = 8
MB = 2
EPS = 1e-05
SCALE = HD ** (-0.5)

bf16 = jnp.bfloat16
f32 = jnp.float32

ORDER = (0, 2, 4, 6, 1, 3, 5, 7)


def dot(a, b, ca, cb):
    return lax.dot_general(a, b, (((ca,), (cb,)), ((), ())), preferred_element_type=f32)


def flip(value, bit):
    return lax.ppermute(value, "shard", [(i, i ^ bit) for i in range(8)])


def tie(*values):
    return lax.optimization_barrier(values)


def plus(a, b):
    return a.astype(f32) + b.astype(f32)


def rep_in(value):
    return lax.ppermute(value, "rep", [(0, 1), (3, 2)])


def rep_over(value):
    return lax.ppermute(value, "rep", [(1, 2), (2, 1)])


def rep_out(value):
    return lax.ppermute(value, "rep", [(1, 0), (2, 3)])


def rotary_tables():
    half = ROT // 2
    freqs = 10000.0 ** (-2.0 * jnp.arange(half, dtype=f32) / ROT)
    angles = jnp.arange(SEQ_MOST * BLK, dtype=f32)[:, None] * freqs[None, :]
    rest = 128 - ROT
    cosine = jnp.concatenate(
        [jnp.cos(angles), jnp.cos(angles), jnp.ones((SEQ_MOST * BLK, rest), f32)], axis=-1
    )
    sine = jnp.concatenate(
        [-jnp.sin(angles), jnp.sin(angles), jnp.zeros((SEQ_MOST * BLK, rest), f32)], axis=-1
    )
    return cosine.reshape(SEQ_MOST, BLK, 128), sine.reshape(SEQ_MOST, BLK, 128)


def params_of(vmem=52):
    return pltpu.CompilerParams(vmem_limit_bytes=vmem * 2**20)


def cost(us):
    return pl.CostEstimate(flops=int(us * 1.1e9) + 1024, bytes_accessed=1024, transcendentals=0)


def tick(token, *arrays):
    def body(*refs):
        refs[-1][...] = refs[0][...]

    return pl.pallas_call(
        body,
        in_specs=[pl.BlockSpec(memory_space=pltpu.VMEM)] + [pl.BlockSpec(memory_space=pl.ANY)] * len(arrays),
        out_specs=pl.BlockSpec(memory_space=pltpu.VMEM),
        out_shape=jax.ShapeDtypeStruct(token.shape, token.dtype),
        compiler_params=params_of(16), cost_estimate=cost(2000),
    )(token, *arrays)


def spec(shape, index):
    return pl.BlockSpec(shape, index)


def attention_kernel(
    piece_of, inner_of, first_of, end_of,
    qkv_ref, grad_ref, cos_ref, sin_ref,
    ctx_ref, out_ref, sum_ref,
    q_buf, k_buf, v_buf, g_buf, dk_buf, dv_buf,
):
    m = pl.program_id(0)
    blocks = piece_of.shape[1]
    lane = lax.broadcasted_iota(jnp.int32, (BLK, 128), 1)
    tile = 2 * BLK

    def turned(x):
        return jnp.where(lane < ROT // 2, pltpu.roll(x, 128 - ROT // 2, 1), pltpu.roll(x, ROT // 2, 1))

    def store_part(p, i, start, value):
        low = value.astype(bf16)
        out_ref[p, 0, i, :, start:start + value.shape[1]] = low
        sum_ref[0, 0:1, start:start + value.shape[1]] += jnp.sum(low.astype(f32), axis=0, keepdims=True)

    def block_rows(g):
        return pl.ds(pl.multiple_of(g * BLK, BLK), BLK)

    def load(g, carry):
        p, i = piece_of[m, g], inner_of[m, g]
        at = g - first_of[m, g]
        cosine, sine = cos_ref[at], sin_ref[at]
        rows = block_rows(g)
        for buf, start in ((q_buf, 0), (k_buf, HD)):
            front = qkv_ref[p, 0, i, :, start:start + 128]
            buf[rows, 0:128] = (front * cosine + turned(front) * sine).astype(bf16)
            buf[rows, 128:HD] = qkv_ref[p, 0, i, :, start + 128:start + HD].astype(bf16)
        v_buf[rows, :] = qkv_ref[p, 0, i, :, 2 * HD:].astype(bf16)
        g_buf[rows, :] = grad_ref[p, 0, i]
        return carry

    lax.fori_loop(0, blocks, load, 0)
    for buf in (q_buf, k_buf, v_buf, g_buf):
        buf[blocks * BLK:, :] = jnp.zeros((BLK, HD), bf16)
    sum_ref[...] = jnp.zeros(sum_ref.shape, f32)
    dk_buf[...] = jnp.zeros(dk_buf.shape, f32)
    dv_buf[...] = jnp.zeros(dv_buf.shape, f32)

    def attend(g, span):
        first = first_of[m, g]
        rows = pl.ds(pl.multiple_of(g * BLK, BLK), tile)
        keys = pl.ds(pl.multiple_of(first * BLK, BLK), span)
        query, grad = q_buf[rows, :], g_buf[rows, :]
        key, value = k_buf[keys, :], v_buf[keys, :]
        after_g = jnp.minimum(g + 1, blocks - 1)
        second = (g + 1 < blocks) & (first_of[m, after_g] == first)
        scores = dot(query, key, 1, 1) * SCALE
        key_tok = first * BLK + lax.broadcasted_iota(jnp.int32, (tile, span), 1)
        query_tok = g * BLK + lax.broadcasted_iota(jnp.int32, (tile, span), 0)
        allowed = (key_tok <= query_tok) & (key_tok < end_of[m, g])
        scores = jnp.where(allowed, scores, -jnp.inf)
        exponent = jnp.exp(scores - jnp.max(scores, axis=1, keepdims=True))
        scale = 1.0 / jnp.sum(exponent, axis=1, keepdims=True)
        last_row = jnp.where(second, tile, BLK)
        row = lax.broadcasted_iota(jnp.int32, (tile, 1), 0)
        prob = exponent * jnp.where(row < last_row, scale, 0.0)
        prob_low = prob.astype(bf16)
        ctx = dot(prob_low, value, 1, 0).astype(bf16)
        prob_grad = dot(grad, value, 1, 1)
        delta = jnp.sum(prob * prob_grad, axis=1, keepdims=True)
        score_grad = (prob * (prob_grad - delta)).astype(bf16)
        dk_buf[keys, :] += dot(score_grad, query, 0, 0)
        dv_buf[keys, :] += dot(prob_low, grad, 0, 0)
        query_grad = dot(score_grad, key, 1, 0) * SCALE

        def put(block, lo):
            p, i = piece_of[m, block], inner_of[m, block]
            at = block - first
            ctx_ref[p, 0, i] = ctx[lo:lo + BLK]
            front = query_grad[lo:lo + BLK, 0:128]
            store_part(p, i, 0, front * cos_ref[at] - turned(front) * sin_ref[at])
            store_part(p, i, 128, query_grad[lo:lo + BLK, 128:])

        put(g, 0)
        pl.when(second)(lambda: put(after_g, BLK))

    def one_block(g, carry):
        at = g - first_of[m, g]
        for count in range(SEQ_MOST // 2):
            pl.when(at == 2 * count)(lambda: attend(g, (count + 1) * tile))
        return carry

    lax.fori_loop(0, blocks, one_block, 0)

    def store(g, carry):
        p, i = piece_of[m, g], inner_of[m, g]
        at = g - first_of[m, g]
        rows = block_rows(g)
        front = dk_buf[rows, 0:128] * SCALE
        store_part(p, i, HD, front * cos_ref[at] - turned(front) * sin_ref[at])
        store_part(p, i, HD + 128, dk_buf[rows, 128:HD] * SCALE)
        store_part(p, i, 2 * HD, dv_buf[rows, :])
        return carry

    lax.fori_loop(0, blocks, store, 0)


def attention(tables, qkv, grad, cosine, sine):
    pieces, _, own = qkv.shape[:3]
    blocks = tables[0].shape[1]

    def part(width):
        return pl.BlockSpec((pieces, 1, own, BLK, width), lambda m, *_: (0, m, 0, 0, 0))

    whole = pl.BlockSpec((SEQ_MOST, BLK, 128), lambda m, *_: (0, 0, 0))
    rows = (blocks + 1) * BLK
    return pl.pallas_call(
        attention_kernel,
        grid_spec=pltpu.PrefetchScalarGridSpec(
            num_scalar_prefetch=4,
            grid=(MB,),
            in_specs=[part(3 * HD), part(HD), whole, whole],
            out_specs=[part(HD), part(3 * HD), spec((1, 8, 3 * HD), lambda m, *_: (m, 0, 0))],
            scratch_shapes=[
                pltpu.VMEM((rows, HD), bf16),
                pltpu.VMEM((rows, HD), bf16),
                pltpu.VMEM((rows, HD), bf16),
                pltpu.VMEM((rows, HD), bf16),
                pltpu.VMEM((rows, HD), f32),
                pltpu.VMEM((rows, HD), f32),
            ],
        ),
        out_shape=[
            jax.ShapeDtypeStruct((pieces, MB, own, BLK, HD), bf16),
            jax.ShapeDtypeStruct((pieces, MB, own, BLK, 3 * HD), bf16),
            jax.ShapeDtypeStruct((MB, 8, 3 * HD), f32),
        ],
        compiler_params=params_of(),
        cost_estimate=cost(0),
    )(*tables, qkv, grad, cosine, sine)


def plus_low(a, b, index=None):
    shape = a.shape if index is None else a.shape[1:]
    if index is None:
        a, b, index = a[None], b[None], 0
    a, b = [x.reshape(x.shape[0], -1, x.shape[-1]) for x in (a, b)]
    rows, cols = a.shape[1:]
    steps = 2 if rows % 32 == 0 else 1
    block = spec((1, rows // steps, cols), lambda i: (index, i, 0))

    def body(a_ref, b_ref, out_ref):
        out_ref[...] = plus(a_ref[0], b_ref[0]).astype(bf16)

    return pl.pallas_call(
        body, grid=(steps,), in_specs=[block, block],
        out_specs=spec((rows // steps, cols), lambda i: (i, 0)),
        out_shape=jax.ShapeDtypeStruct((rows, cols), bf16),
        compiler_params=params_of(32), cost_estimate=cost(0),
    )(a, b).reshape(shape)


def out_terms(owners, place, context, active, out_w, down_w, resid, came=None):
    rows, inner = active.shape
    n = resid.shape[0]
    cols = D // 8
    first = 4 if came is None else 0

    def terms(place_ref, refs):
        ctx, act = refs[0][...], refs[1][...]
        own = pl.program_id(0) == place_ref[0]
        return [
            dot(ctx, refs[2 + b][...], 1, 0)
            + dot(act, refs[6 + b][...], 1, 0)
            + jnp.where(own, refs[10 + b][...].astype(f32), 0.0)
            for b in range(4)
        ]

    def odd_body(owners_ref, place_ref, *refs):
        for b, part in enumerate(terms(place_ref, refs)):
            refs[14][b] = part.astype(bf16)

    def even_body(owners_ref, place_ref, *refs):
        got, send_one, keep_one, send_two, keep_two = refs[14:]
        parts = [(p + got[b].astype(f32)).astype(bf16) for b, p in enumerate(terms(place_ref, refs))]

        @pl.when(pl.program_id(0) < 4)
        def _():
            send_one[0], send_one[1] = parts[1], parts[3]
            keep_one[0], keep_one[1] = parts[0], parts[2]

        @pl.when(pl.program_id(0) >= 4)
        def _():
            send_two[0], send_two[1] = parts[2], parts[3]
            keep_two[0], keep_two[1] = parts[0], parts[1]

    def columns(height, b):
        return spec((height, cols), lambda i, o, p: (0, o[first + b]))

    in_specs = [
        spec((n, context.shape[1]), lambda i, o, p: (i, 0)),
        spec((n, inner), lambda i, o, p: (i, 0)),
        *[columns(context.shape[1], b) for b in range(4)],
        *[columns(inner, b) for b in range(4)],
        *[columns(n, b) for b in range(4)],
    ]
    args = [context, active, *[out_w] * 4, *[down_w] * 4, *[resid] * 4]
    if came is None:
        body = odd_body
        out_specs = spec((4, n, cols), lambda i, o, p: (0, i, 0))
        out_shape = jax.ShapeDtypeStruct((4, rows, cols), bf16)
    else:
        body = even_body
        in_specs.append(spec((4, n, cols), lambda i, o, p: (0, i, 0)))
        args.append(came)
        low = spec((2, n, cols), lambda i, o, p: (0, jnp.minimum(i, 3), 0))
        high = spec((2, n, cols), lambda i, o, p: (0, jnp.maximum(i - 4, 0), 0))
        out_specs = [low, low, high, high]
        out_shape = [jax.ShapeDtypeStruct((2, rows // 2, cols), bf16)] * 4
    return pl.pallas_call(
        body,
        grid_spec=pltpu.PrefetchScalarGridSpec(
            num_scalar_prefetch=2, grid=(8,), in_specs=in_specs, out_specs=out_specs
        ),
        out_shape=out_shape, compiler_params=params_of(), cost_estimate=cost(0),
    )(owners, place.reshape(1), *args)


def norm_terms(owners, mixed_grad, hidden_grad, qkv_w, up_w, came=None):
    rows = mixed_grad.shape[0]
    n = rows // 16
    first = 4 if came is None else 0

    def terms(refs):
        one, two, w_one, w_two = refs
        return dot(one[...], w_one[...], 1, 1) + dot(two[...], w_two[...], 1, 1)

    def odd_body(owners_ref, *refs):
        refs[4][0, 0] = terms(refs[:4]).astype(bf16)

    def even_body(owners_ref, *refs):
        got, send_one, keep_one, send_two, keep_two = refs[4:]
        sums = (terms(refs[:4]) + got[0, 0].astype(f32)).astype(bf16)
        i = pl.program_id(0)
        for ref, steps in (
            (keep_one, (0, 4)), (send_one, (2, 6)), (keep_two, (1, 3)), (send_two, (5, 7)),
        ):
            @pl.when((i == steps[0]) | (i == steps[1]))
            def _():
                ref[0] = sums

    def own_rows(i, o):
        return (o[first + i // 2] * 2 + i % 2, 0)

    in_specs = [
        spec((n, mixed_grad.shape[1]), own_rows),
        spec((n, hidden_grad.shape[1]), own_rows),
        spec(qkv_w.shape, lambda i, o: (0, 0)),
        spec(up_w.shape, lambda i, o: (0, 0)),
    ]
    args = [mixed_grad, hidden_grad, qkv_w, up_w]
    if came is None:
        body = odd_body
        out_specs = spec((1, 1, n, D), lambda i, o: (i // 2, i % 2, 0, 0))
        out_shape = jax.ShapeDtypeStruct((4, 2, n, D), bf16)
    else:
        body = even_body
        in_specs.append(spec((1, 1, n, D), lambda i, o: (i // 2, i % 2, 0, 0)))
        args.append(came)
        out_specs = [
            spec((1, n, D), lambda i, o: (i // 4, 0, 0)),
            spec((1, n, D), lambda i, o: (i // 4, 0, 0)),
            spec((1, n, D), lambda i, o: (jnp.maximum(i - 4, 0) // 2, 0, 0)),
            spec((1, n, D), lambda i, o: (jnp.minimum(i // 2, 1), 0, 0)),
        ]
        out_shape = [jax.ShapeDtypeStruct((2, n, D), bf16)] * 4
    return pl.pallas_call(
        body,
        grid_spec=pltpu.PrefetchScalarGridSpec(
            num_scalar_prefetch=1, grid=(8,), in_specs=in_specs, out_specs=out_specs
        ),
        out_shape=out_shape, compiler_params=params_of(), cost_estimate=cost(0),
    )(owners, *args)


def token_dot(left, right, part=0, parts=1, extra=None):
    rows, width = left.shape[0], left.shape[1] // parts
    blocks, _, cols = right.shape
    step = 512 // cols
    more = [] if extra is None else [extra]
    total = width + sum(m.shape[0] for m in more)

    def body(left_ref, right_ref, *refs):
        out_ref = refs[-1]
        for b in range(step):
            at = slice(b * cols, (b + 1) * cols)
            out_ref[0:width, at] = dot(left_ref[...], right_ref[b], 0, 0).astype(bf16)
        if more:
            out_ref[width:, :] = refs[0][...]

    return pl.pallas_call(
        body, grid=(blocks // step,),
        in_specs=[
            spec((rows, width), lambda i: (0, part)),
            spec((step, rows, cols), lambda i: (i, 0, 0)),
        ] + [spec((m.shape[0], step * cols), lambda i: (0, i)) for m in more],
        out_specs=spec((total, step * cols), lambda i: (0, i)),
        out_shape=jax.ShapeDtypeStruct((total, blocks * cols), bf16),
        compiler_params=params_of(56), cost_estimate=cost(0),
    )(left, right, *more)


EXTRA = 16


def normed_dot(spot, shards, normed, right, sums, part=0, parts=1):
    rows, tile = normed.shape[0], 512
    cols, width = D // shards, right.shape[1] // parts
    per = tile // cols

    def body(spot_ref, left_ref, right_ref, sum_ref, out_ref):
        sums = dot(left_ref[...], right_ref[...], 0, 0).astype(bf16)
        high = sum_ref[...]
        first = high.astype(bf16).astype(f32)
        second = (high - first).astype(bf16).astype(f32)
        third = high - first - second
        row = lax.broadcasted_iota(jnp.int32, (EXTRA, width), 0) - 3 * spot_ref[0]
        extra = jnp.where(row == 0, first, jnp.where(row == 1, second, jnp.where(row == 2, third, 0.0)))
        for b in range(per):
            out_ref[b, 0:cols, :] = sums[b * cols:(b + 1) * cols]
            out_ref[b, cols:, :] = extra.astype(bf16)

    return pl.pallas_call(
        body,
        grid_spec=pltpu.PrefetchScalarGridSpec(
            num_scalar_prefetch=1, grid=(D // tile,),
            in_specs=[
                spec((rows, tile), lambda i, z: (0, i)),
                spec((rows, width), lambda i, z: (0, part)),
                spec((1, width), lambda i, z: (0, part)),
            ],
            out_specs=spec((per, cols + EXTRA, width), lambda i, z: (i, 0, 0)),
        ),
        out_shape=jax.ShapeDtypeStruct((shards, cols + EXTRA, width), bf16),
        compiler_params=params_of(56), cost_estimate=cost(0),
    )(spot, normed, right, sums)


def whole_rows(ref):
    return jnp.concatenate([ref[b] for b in range(ref.shape[0])], axis=1)


def out_blocks(piece_of, inner_of, own, parts, bias):
    blocks = piece_of.shape[1]
    half, cols = parts[0][2].shape

    def body(piece_ref, inner_ref, *refs):
        bias_ref, out_ref, all_rows = refs[6:]
        m = pl.program_id(0)

        @pl.when(m == 0)
        def _():
            for h in range(2):
                keep, came, last = refs[3 * h:3 * h + 3]
                sums = plus(keep[0], came[0]) + last[...].astype(f32) + bias_ref[...]
                all_rows[h * half:(h + 1) * half, :] = sums.astype(bf16)

        def one(g, carry):
            row = ((piece_ref[m, g] * MB + m) * own + inner_ref[m, g]) * BLK
            out_ref[0, g] = all_rows[pl.ds(pl.multiple_of(row, BLK), BLK), :]
            return carry

        lax.fori_loop(0, blocks, one, 0)

    first = spec((1, half, cols), lambda m, *_: (0, 0, 0))
    whole = spec((half, cols), lambda m, *_: (0, 0))
    return pl.pallas_call(
        body,
        grid_spec=pltpu.PrefetchScalarGridSpec(
            num_scalar_prefetch=2, grid=(MB,),
            in_specs=[first, first, whole] * 2 + [spec((1, cols), lambda m, *_: (0, 0))],
            out_specs=spec((1, blocks, BLK, cols), lambda m, *_: (m, 0, 0, 0)),
            scratch_shapes=[pltpu.VMEM((2 * half, cols), bf16)],
        ),
        out_shape=jax.ShapeDtypeStruct((MB, blocks, BLK, cols), bf16),
        compiler_params=params_of(), cost_estimate=cost(0),
    )(piece_of, inner_of, *parts[0], *parts[1], bias[None])


def token_grads(tokens, grad_rows, parts):
    rows = tokens.shape[0]
    n = rows // 4

    def body(tokens_ref, grad_ref, *refs):
        out_ref = refs[6]
        x = tokens_ref[...].astype(f32)
        center = x - jnp.mean(x, axis=1, keepdims=True)
        inv_std = lax.rsqrt(jnp.mean(center * center, axis=1, keepdims=True) + EPS)
        normed = center * inv_std

        def finish(keep, came, last):
            grad = plus(keep[0], came[0]) + last[...].astype(f32)
            mean = jnp.mean(grad, axis=1, keepdims=True)
            proj = jnp.mean(grad * normed, axis=1, keepdims=True)
            grad = inv_std * (grad - mean - normed * proj)
            out_ref[...] = (grad_ref[...].astype(f32) + grad).astype(bf16)

        pl.when(pl.program_id(0) < 2)(lambda: finish(*refs[0:3]))
        pl.when(pl.program_id(0) >= 2)(lambda: finish(*refs[3:6]))

    own = spec((n, D), lambda i: (i, 0))
    in_specs = [own, own]
    for at in (lambda i: jnp.minimum(i, 1), lambda i: jnp.maximum(i - 2, 0)):
        first = spec((1, n, D), lambda i, at=at: (0, at(i), 0))
        in_specs += [first, first, spec((n, D), lambda i, at=at: (at(i), 0))]
    return pl.pallas_call(
        body, grid=(4,), in_specs=in_specs, out_specs=own,
        out_shape=jax.ShapeDtypeStruct((rows, D), bf16),
        compiler_params=params_of(), cost_estimate=cost(0),
    )(tokens, grad_rows, *parts[0], *parts[1])


def sum_rows(vector, spot):
    thirds, left = [], vector
    for _ in range(3):
        thirds.append(lax.reduce_precision(left, 8, 7))
        left = left - thirds[-1]
    mine = jnp.arange(4)[:, None, None] == spot
    values = jnp.where(mine, jnp.stack(thirds)[None], 0.0).reshape(-1)
    return jnp.pad(values, (0, 16 * D - values.shape[0])).reshape(16, D).astype(bf16)


def sums_of(found, size):
    return jnp.sum(found.astype(f32).reshape(-1)[:12 * size].reshape(12, size), axis=0)


def hidden_back(grad_out, down_w, slope):
    rows, wide = slope.shape
    n = rows // 8

    def body(grad_ref, w_ref, slope_ref, out_ref, sum_ref):
        active_grad = dot(whole_rows(grad_ref), w_ref[...], 1, 1).astype(bf16).astype(f32)
        value = (active_grad * slope_ref[...]).astype(bf16)
        out_ref[...] = value
        total = jnp.sum(value.astype(f32), axis=0, keepdims=True)

        @pl.when(pl.program_id(0) == 0)
        def _():
            sum_ref[...] = total

        @pl.when(pl.program_id(0) > 0)
        def _():
            sum_ref[...] += total

    return pl.pallas_call(
        body, grid=(8,),
        in_specs=[
            spec((grad_out.shape[0], n, grad_out.shape[2]), lambda i: (0, i, 0)),
            spec((wide, D), lambda i: (0, 0)),
            spec((n, wide), lambda i: (i, 0)),
        ],
        out_specs=[spec((n, wide), lambda i: (i, 0)), spec((1, wide), lambda i: (0, 0))],
        out_shape=[
            jax.ShapeDtypeStruct((rows, wide), bf16), jax.ShapeDtypeStruct((1, wide), f32),
        ],
        compiler_params=params_of(), cost_estimate=cost(0),
    )(grad_out, down_w, slope)


def head_back(grad_out, out_w):
    blocks, rows, cols = grad_out.shape
    n = rows // 8

    def body(grad_ref, w_ref, out_ref):
        out_ref[...] = dot(whole_rows(grad_ref), w_ref[...], 1, 1).astype(bf16)

    return pl.pallas_call(
        body, grid=(8,),
        in_specs=[
            spec((blocks, n, cols), lambda i: (0, i, 0)),
            spec((HD, D), lambda i: (0, 0)),
        ],
        out_specs=spec((n, HD), lambda i: (i, 0)),
        out_shape=jax.ShapeDtypeStruct((rows, HD), bf16),
        compiler_params=params_of(), cost_estimate=cost(0),
    )(grad_out, out_w)


def row_grads(inner, chunks, count=None):
    rows = [count or c[0].shape[0] for c in chunks]
    total, cols = sum(rows), 512

    def body(inner_ref, *refs):
        at = 0
        for c, n in enumerate(rows):
            one, two = refs[2 * c][...].astype(f32), refs[2 * c + 1][...].astype(f32)
            refs[-1][at:at + n, :] = jnp.where(inner_ref[0] == 1, one, two)
            at += n

    return pl.pallas_call(
        body,
        grid_spec=pltpu.PrefetchScalarGridSpec(
            num_scalar_prefetch=1, grid=(D // cols,),
            in_specs=[spec((n, cols), lambda i, *_: (0, i)) for n in rows for _ in range(2)],
            out_specs=spec((total, cols), lambda i, *_: (0, i)),
        ),
        out_shape=jax.ShapeDtypeStruct((total, D), f32),
        compiler_params=params_of(32), cost_estimate=cost(0),
    )(inner, *[a for c in chunks for a in c])


def column_grads(inner, chunks, weight, gain, shift, run, step, by_run, token=None):
    rows, each = weight.shape[0], len(chunks[0])
    if by_run:
        groups, per = len(chunks), chunks[0][0].shape[0] // step
        steps = per
    else:
        groups, per = chunks[0][0].shape[2] // run, chunks[0][0].shape[0] // step
        steps = per * len(chunks)

    tokens = [] if token is None else [token]

    def body(inner_ref, *refs):
        pairs, refs = refs[:each * len(chunks)], refs[each * len(chunks) + len(tokens):]
        w_ref, gain_ref, shift_ref, grads, gain_out, shift_out, t_out = refs
        i, k = pl.program_id(0), pl.program_id(1)

        @pl.when((i == 0) & (k == 0))
        def _():
            gain_out[...] = jnp.zeros_like(gain_out)
            shift_out[...] = jnp.zeros_like(shift_out)

        for c in range(len(chunks)):
            @pl.when((k if by_run else i // per) == c)
            def _():
                for j in range(step):
                    value = pairs[each * c][j].astype(f32)
                    if each == 2:
                        other = pairs[2 * c + 1][j].astype(f32)
                        value = jnp.where(inner_ref[0] == 1, value, other)
                    at = slice(j * run, (j + 1) * run)
                    t = jnp.sum(value[rows:], axis=0, keepdims=True)
                    value, w = value[:rows], w_ref[:, at].astype(f32)
                    t_out[:, at] = t
                    grads[:, at] = gain_ref[...] * value + shift_ref[...] * t
                    for out, terms in ((gain_out, w * value), (shift_out, w * t)):
                        out[...] += sum(terms[:, lo:lo + 128] for lo in range(0, run, 128))

    def part_index(c):
        if by_run:
            return lambda i, k, *_: (i, 0, 0)
        return lambda i, k, *_: (jnp.clip(i - c * per, 0, per - 1), 0, k)

    def columns(i, k, *_):
        return (0, i * groups + k if by_run else k * steps + i)

    column = spec((rows, 1), lambda i, k, *_: (0, 0))
    wide_column = spec((rows, 128), lambda i, k, *_: (0, 0))
    grads, gain_grad, shift_grad, totals = pl.pallas_call(
        body,
        grid_spec=pltpu.PrefetchScalarGridSpec(
            num_scalar_prefetch=1, grid=(steps, groups),
            in_specs=[spec((step, rows + EXTRA, run), part_index(c)) for c in range(len(chunks)) for _ in range(each)]
            + [pl.BlockSpec(memory_space=pl.ANY)] * len(tokens)
            + [spec((rows, step * run), columns), column, column],
            out_specs=[
                spec((rows, step * run), columns), wide_column, wide_column,
                spec((1, step * run), columns),
            ],
        ),
        out_shape=[
            jax.ShapeDtypeStruct(weight.shape, f32),
            jax.ShapeDtypeStruct((rows, 128), f32),
            jax.ShapeDtypeStruct((rows, 128), f32),
            jax.ShapeDtypeStruct((1, weight.shape[1]), f32),
        ],
        compiler_params=params_of(32), cost_estimate=cost(0),
    )(
        inner, *[a for c in chunks for a in c], *tokens, weight,
        gain.astype(f32)[:, None], shift.astype(f32)[:, None],
    )
    return grads, jnp.sum(gain_grad, axis=1), jnp.sum(shift_grad, axis=1), totals[0]


def local(
    tokens, cotangent, seq_blocks, seq_pad, deal_order,
    ln1_gain, ln1_bias, ln2_gain, ln2_bias,
    qkv_weight, qkv_bias, out_weight, out_bias, up_weight, up_bias, down_weight, down_bias,
):
    shards = lax.axis_size("shard")
    place = lax.axis_index("shard")
    cube = shards == 8 and lax.axis_size("rep") == 4
    own = tokens.shape[1]
    blocks = deal_order.shape[2]
    own_rows = MB * own * BLK
    rows = shards * own_rows
    cols = D // shards
    wide = FF // shards
    split = shards // HEADS
    head, share = place // split, place % split
    share_cols = 3 * HD // split

    if cube:
        owners = jnp.bitwise_xor(place, jnp.array(ORDER, jnp.int32))
    deal = deal_order[:, 0, :]
    counts = seq_blocks[:, 0, :]
    pads = seq_pad[:, 0, :]
    ids = jnp.arange(blocks, dtype=jnp.int32)
    inverse = jnp.sum(
        jnp.where(deal[:, None, :] == ids[None, :, None], ids[None, None, :], 0), axis=-1
    )
    piece_of, inner_of = inverse // own, inverse % own
    ends = jnp.cumsum(counts, axis=1)
    starts = ends - counts
    inside = (ids[None, :, None] >= starts[:, None, :]) & (ids[None, :, None] < ends[:, None, :])
    first_of = jnp.sum(jnp.where(inside, starts[:, None, :], 0), axis=-1)
    valid = jnp.sum(jnp.where(inside, (counts * BLK - pads)[:, None, :], 0), axis=-1)
    tables = [t.astype(jnp.int32) for t in (piece_of, inner_of, first_of, first_of * BLK + valid)]
    given = deal.reshape(MB, shards, own)

    cot_own = jnp.stack([cotangent[m][given[m]] for m in range(MB)], axis=1)

    def swap(value):
        return lax.all_to_all(value, "shard", split_axis=0, concat_axis=0, tiled=True)

    token = jnp.zeros((8, 128), f32)

    def gate(*arrays):
        nonlocal token
        if cube:
            token = tick(token, *arrays)

    def late(value):
        nonlocal token
        if cube:
            value, token = tie(value, token)
        return value

    flat = tokens.reshape(own_rows, D).astype(f32)
    center = flat - jnp.mean(flat, axis=-1, keepdims=True)
    inv_std = lax.rsqrt(jnp.mean(center * center, axis=-1, keepdims=True) + EPS)
    normed_own = center * inv_std
    normed_low = normed_own.astype(bf16)
    normed = lax.all_gather(normed_low, "shard", axis=0, tiled=True)
    gate(normed_low)

    shares = lax.axis_size("rep") if cube else 1
    part_rows = cols // shares
    spot = lax.axis_index("rep") if cube else 0
    up_late, qkv_late = late((up_weight, qkv_weight))

    def part_of(array):
        return lax.dynamic_slice_in_dim(array, spot * part_rows, part_rows, 0).astype(f32)

    def with_shift(weight, gain, shift):
        high = lax.reduce_precision(shift, 8, 7)
        low = lax.reduce_precision(shift - high, 8, 7)
        tail = jnp.zeros((14, shift.shape[0]), bf16)
        scaled = (part_of(weight) * part_of(gain)[:, None]).astype(bf16)
        return jnp.concatenate([scaled, high.astype(bf16)[None], low.astype(bf16)[None], tail], axis=0)

    shift_up = jnp.sum(up_late.astype(f32) * ln2_bias.astype(f32)[:, None], axis=0)
    shift_qkv = jnp.sum(qkv_late.astype(f32) * ln1_bias.astype(f32)[:, None], axis=0)
    own_bias = lax.dynamic_slice_in_dim(shift_qkv, place * 3 * cols, 3 * cols) + qkv_bias.astype(f32)
    shift_qkv = lax.dynamic_update_slice_in_dim(shift_qkv, own_bias, place * 3 * cols, 0)
    sent_rows = part_rows + 16
    up_send = with_shift(up_late, ln2_gain, shift_up).reshape(sent_rows, shards, wide).transpose(1, 0, 2)
    qkv_send = with_shift(qkv_late, ln1_gain, shift_qkv).reshape(sent_rows, 3, HEADS, HD)
    qkv_send = qkv_send.transpose(2, 0, 1, 3).reshape(HEADS, sent_rows, 3 * HD)
    if split > 1:
        qkv_send = jnp.repeat(qkv_send, split, axis=0)
    found = swap(jnp.concatenate([up_send, qkv_send], axis=2))
    cot_late = late(cot_own)
    grad_out = lax.all_gather(cot_late.reshape(rows, cols), "shard", axis=0)
    gate(up_send, qkv_send, cot_late)
    found = late(found)
    biases = jnp.sum(found[:, part_rows:part_rows + 2].astype(f32), axis=(0, 1))

    def exchange(part):
        return [part] + [
            lax.ppermute(part, "rep", [(i, (i + k) % shares) for i in range(shares)])
            for k in range(1, shares)
        ]

    def whole(parts):
        if shares == 1:
            return parts[0].reshape(D, parts[0].shape[-1])
        width = parts[0].shape[-1]
        array = jnp.zeros((shards, shares, part_rows, width), bf16)
        for k, part in enumerate(parts):
            at = lax.rem(spot - k + shares, shares)
            array = lax.dynamic_update_slice(array, part[:, None], (0, at, 0, 0))
        return array.reshape(D, width)

    up_parts = exchange(found[:, :part_rows, :wide])
    normed, up_parts, biases = tie(normed, up_parts, biases)
    up_w = whole(up_parts)
    found, up_w = tie(found, up_w)
    qkv_parts = exchange(found[:, :part_rows, wide:])
    bias_up, bias_qkv = biases[:wide] + up_bias.astype(f32), biases[wide:]
    out_w, down_w, resid = out_weight, down_weight, tokens.reshape(own_rows, D)

    hidden = dot(normed, up_w, 1, 0) + bias_up
    cdf = 0.5 + 0.5 * lax.erf(hidden * (0.5 ** 0.5))
    density = jnp.exp(-0.5 * hidden * hidden) * 0.3989422804014327
    active = (hidden * cdf).astype(bf16)
    slope = cdf + hidden * density
    grad_out, active = tie(grad_out, active)

    where_rep = jnp.asarray(spot, jnp.int32).reshape(1)

    down_parts = [token_dot(active, grad_out, 0, 2)]
    down_came = [rep_in(down_parts[0])]
    gate(down_parts[0])
    hidden_grad, sum_hidden = hidden_back(late(grad_out), down_w, slope)
    sum_cot = jnp.sum(cot_own, axis=tuple(range(cot_own.ndim - 1)), dtype=f32)
    extra = sum_rows(sum_cot, spot) if cube else None
    down_parts.append(token_dot(active, grad_out, 1, 2, extra))
    hidden_grad, down_parts[1] = tie(hidden_grad, down_parts[1])
    up_terms = [normed_dot(where_rep, shards, normed, hidden_grad, sum_hidden, 0, 2)]
    up_found = [swap(up_terms[0])]
    down_came[0], up_terms[0] = tie(down_came[0], up_terms[0])
    down_pair = [plus_low(down_parts[0], down_came[0])]
    down_other = [rep_over(down_pair[0])]
    down_came.append(rep_in(down_parts[1]))
    gate(down_pair[0], up_terms[0])

    context_w = out_w
    if split > 1:
        pairs = [list(range(h * split, (h + 1) * split)) for h in range(HEADS)]
        context_w = lax.all_gather(out_w, "shard", axis=0, tiled=True, axis_index_groups=pairs)
    up_terms.append(normed_dot(where_rep, shards, late(normed), hidden_grad, sum_hidden, 1, 2))
    grad_out, up_terms[1] = tie(grad_out, up_terms[1])
    context_grad = head_back(grad_out, context_w)
    qkv_parts, context_grad = tie(qkv_parts, context_grad)
    qkv_w = whole(qkv_parts)
    mixed = dot(normed, qkv_w, 1, 0) + bias_qkv
    down_other[0], down_came[1], up_found[0], mixed = tie(down_other[0], down_came[1], up_found[0], mixed)
    down_total = [plus_low(down_pair[0], down_other[0])]
    down_back = [rep_out(down_total[0])]
    down_pair.append(plus_low(down_parts[1], down_came[1]))
    down_other.append(rep_over(down_pair[1]))
    up_came = [rep_in(up_found[0])]
    up_terms[1], up_found[0] = tie(up_terms[1], up_found[0])
    up_found.append(swap(up_terms[1]))
    gate(down_total[0], down_pair[1], up_found[0])
    cosine, sine = rotary_tables()
    context, mixed_grad, sum_mixed = attention(
        tables,
        late(mixed).reshape(shards, MB, own, BLK, 3 * HD),
        context_grad.reshape(shards, MB, own, BLK, HD),
        cosine,
        sine,
    )
    context = context.reshape(rows, HD)
    mixed_grad = mixed_grad.reshape(rows, 3 * HD)
    down_back[0], down_other[1], up_came[0], up_found[1], context = tie(
        down_back[0], down_other[1], up_came[0], up_found[1], context
    )
    down_total.append(plus_low(down_pair[1], down_other[1]))
    down_back.append(rep_out(down_total[1]))
    up_pair = [plus_low(up_found[0], up_came[0])]
    up_other = [rep_over(up_pair[0])]
    up_came.append(rep_in(up_found[1]))
    gate(down_back[0], down_total[1], up_pair[0], up_found[1])
    mixed_grad = late(mixed_grad)
    if split > 1:
        context = lax.dynamic_slice_in_dim(context, share * (HD // split), HD // split, 1)
        mixed_grad = lax.dynamic_slice_in_dim(mixed_grad, share * share_cols, share_cols, 1)
        qkv_w = lax.dynamic_slice_in_dim(qkv_w, share * share_cols, share_cols, 1)
        sum_mixed = lax.dynamic_slice_in_dim(sum_mixed, share * share_cols, share_cols, 2)
    sum_mixed = jnp.sum(sum_mixed, axis=(0, 1))[None]
    qkv_terms = normed_dot(where_rep, shards, normed, mixed_grad, sum_mixed)
    qkv_found = swap(qkv_terms)
    if cube:
        context, qkv_terms = tie(context, qkv_terms)
        out_part = token_dot(context, grad_out)
        out_came = rep_in(out_part)

        context, out_part = tie(context, out_part)
        odd = out_terms(owners, place, context, active, out_w, down_w, resid)
        odd_came = flip(odd, 1)
        down_back[1], up_other[0], up_came[1], odd = tie(down_back[1], up_other[0], up_came[1], odd)
        up_total = [plus_low(up_pair[0], up_other[0])]
        up_back = [rep_out(up_total[0])]
        up_pair.append(plus_low(up_found[1], up_came[1]))
        up_other.append(rep_over(up_pair[1]))
        gate(down_back[1], up_total[0], up_pair[1], qkv_terms, odd)

        norm_odd = norm_terms(owners, late(mixed_grad), hidden_grad, qkv_w, up_w)
        norm_odd_came = flip(norm_odd, 1)
        odd_came, norm_odd = tie(odd_came, norm_odd)
        send_one, keep_one, send_two, keep_two = out_terms(
            owners, place, context, active, out_w, down_w, resid, odd_came
        )
        got_one, got_two = flip(send_one, 2), flip(send_two, 4)
        up_back[0], up_other[1], out_came, qkv_found, keep_one = tie(
            up_back[0], up_other[1], out_came, qkv_found, keep_one
        )
        up_total.append(plus_low(up_pair[1], up_other[1]))
        up_back.append(rep_out(up_total[1]))
        qkv_parts = [qkv_found[:shards // 2], qkv_found[shards // 2:]]
        qkv_came = [rep_in(qkv_parts[0])]
        gate(up_back[0], up_total[1], out_came, *qkv_parts, norm_odd, send_one)

        norm_send_one, norm_keep_one, norm_send_two, norm_keep_two = norm_terms(
            owners, mixed_grad, hidden_grad, qkv_w, up_w, late(norm_odd_came)
        )
        norm_got_one, norm_got_two = flip(norm_send_one, 2), flip(norm_send_two, 4)

        qkv_came[0], norm_keep_one = tie(qkv_came[0], norm_keep_one)
        qkv_pair = [plus_low(qkv_parts[0], qkv_came[0])]
        qkv_other = [rep_over(qkv_pair[0])]
        qkv_parts[1], out_came, qkv_pair[0] = tie(qkv_parts[1], out_came, qkv_pair[0])
        qkv_came.append(rep_in(qkv_parts[1]))
        got_one, got_two, out_came = tie(got_one, got_two, out_came)
        out_pair = plus_low(out_part, out_came)
        out_other = rep_over(out_pair)
        keep_one, keep_two, out_pair = tie(keep_one, keep_two, out_pair)
        last_one = plus_low(keep_one, got_one, 1)
        last_two = plus_low(keep_two, got_two, 1)
        down_late, grad_late, last_one, last_two = tie(
            list(zip(down_total, down_back)), grad_out, last_one, last_two
        )
        inner = ((spot == 1) | (spot == 2)).astype(jnp.int32).reshape(1)
        down_grad = row_grads(inner, down_late, wide // 2)
        grad_rows = lax.dynamic_slice_in_dim(grad_late, place * own_rows, own_rows, 1)
        grad_rows = grad_rows.transpose(1, 0, 2).reshape(own_rows, D)
        qkv_other[0], down_grad, grad_rows = tie(qkv_other[0], down_grad, grad_rows)
        qkv_total = [plus_low(qkv_pair[0], qkv_other[0])]
        qkv_back = [rep_out(qkv_total[0])]
        qkv_came[1], qkv_total[0] = tie(qkv_came[1], qkv_total[0])
        qkv_pair.append(plus_low(qkv_parts[1], qkv_came[1]))
        qkv_other.append(rep_over(qkv_pair[1]))
        up_back[1], qkv_pair[1] = tie(up_back[1], qkv_pair[1])
        up_grad, gain_two_grad, shift_two_grad, sum_up = column_grads(
            inner, list(zip(up_total, up_back)), up_weight, ln2_gain, ln2_bias, wide // 2, 1, True
        )
        norm_got_one, norm_got_two, up_grad = tie(norm_got_one, norm_got_two, up_grad)
        norm_last_one = plus_low(norm_keep_one, norm_got_one, 1)
        norm_last_two = plus_low(norm_keep_two, norm_got_two, 1)
        qkv_other[1], qkv_back[0], norm_last_one, norm_last_two = tie(
            qkv_other[1], qkv_back[0], norm_last_one, norm_last_two
        )
        norm_last_one, norm_last_two = flip(norm_last_one, 4), flip(norm_last_two, 2)
        qkv_total.append(plus_low(qkv_pair[1], qkv_other[1]))
        qkv_back.append(rep_out(qkv_total[1]))
        out_other, last_one, last_two, qkv_total[1] = tie(out_other, last_one, last_two, qkv_total[1])
        last_one, last_two = flip(last_one, 4), flip(last_two, 2)
        out_total = plus_low(out_pair, out_other)
        out_back = rep_out(out_total)
        norm_last_one, norm_last_two, out_total = tie(norm_last_one, norm_last_two, out_total)
        tokens_grad = token_grads(
            resid, grad_rows,
            [(norm_keep_one, norm_got_one, norm_last_one), (norm_keep_two, norm_got_two, norm_last_two)],
        )
        last_one, last_two, tokens_grad = tie(last_one, last_two, tokens_grad)
        out_given = out_blocks(
            tables[0], tables[1], own, [(keep_one, got_one, last_one), (keep_two, got_two, last_two)],
            out_bias.astype(f32) + down_bias.astype(f32),
        )
        found = jnp.where(inner == 1, down_total[1][wide // 2:], down_back[1][wide // 2:])
        out_bias_grad = sums_of(found, cols)
        qkv_back, out_given = tie(qkv_back, out_given)
    else:
        sums = jnp.concatenate([sum_mixed[0], sum_hidden[0]])
        sums, out_bias_grad = lax.psum((sums, sum_cot), "rep")
        sums = lax.all_gather(sums, "shard")
        sum_qkv = sums[:, :share_cols].reshape(HEADS, 3, HD).transpose(1, 0, 2).reshape(3 * D)
        sum_up = sums[:, share_cols:].reshape(FF)
        qkv_found, up_found = qkv_found[:, :cols], [found[:, :cols] for found in up_found]
        out_sum, qkv_sum, up_sum, down_sum = lax.psum(
            (token_dot(context, grad_out), qkv_found, jnp.concatenate(up_found, axis=2), jnp.concatenate(down_parts)), "rep"
        )
        terms = dot(context, out_w, 1, 0) + dot(active, down_w, 1, 0)
        terms = lax.dynamic_update_slice_in_dim(
            terms,
            lax.dynamic_slice_in_dim(terms, place * own_rows, own_rows, 0) + resid.astype(f32),
            place * own_rows,
            0,
        )
        out_own = lax.psum_scatter(terms.astype(bf16), "shard", scatter_dimension=1, tiled=True)
        out_own = out_own.astype(f32)
        terms = dot(mixed_grad, qkv_w, 1, 1) + dot(hidden_grad, up_w, 1, 1)
        normed_grad = lax.psum_scatter(terms.astype(bf16), "shard", scatter_dimension=0, tiled=True)
        normed_grad = normed_grad.astype(f32)
        grad_rows = lax.dynamic_slice_in_dim(grad_out, place * own_rows, own_rows, 1)
        grad_rows = grad_rows.transpose(1, 0, 2).reshape(own_rows, D)

        out_own = out_own + (out_bias.astype(f32) + down_bias.astype(f32))
        out_own = out_own.astype(bf16).reshape(shards, MB, own, BLK, cols)
        out_given = jnp.stack([out_own[piece_of[m], m, inner_of[m]] for m in range(MB)])
        mean_grad = jnp.mean(normed_grad, axis=-1, keepdims=True)
        mean_proj = jnp.mean(normed_grad * normed_own, axis=-1, keepdims=True)
        tokens_grad = inv_std * (normed_grad - mean_grad - normed_own * mean_proj)
        tokens_grad = (grad_rows.astype(f32) + tokens_grad).astype(bf16)
    tokens_grad = tokens_grad.reshape(MB, own, BLK, D)

    if cube:
        qkv_grad, gain_one_grad, shift_one_grad, sum_qkv = column_grads(
            inner, list(zip(qkv_total, qkv_back)), qkv_weight, ln1_gain, ln1_bias, HD, 2, False, token
        )
        out_back, qkv_grad = tie(out_back, qkv_grad)
        out_grad = row_grads(inner, [(out_total, out_back)])
    else:
        def finish(sums, weight, gain, shift, total):
            sums = sums.astype(f32)
            grads = gain.astype(f32)[:, None] * sums + shift.astype(f32)[:, None] * total
            weight = weight.astype(f32)
            return grads, jnp.sum(weight * sums, axis=1), jnp.sum(weight * total, axis=1)

        qkv_rows = qkv_sum.reshape(HEADS, split, cols, share_cols).transpose(2, 0, 1, 3)
        qkv_rows = qkv_rows.reshape(cols, HEADS, 3, HD).transpose(0, 2, 1, 3).reshape(cols, 3 * D)
        up_rows = up_sum.transpose(1, 0, 2).reshape(cols, FF)
        qkv_grad, gain_one_grad, shift_one_grad = finish(
            qkv_rows, qkv_weight, ln1_gain, ln1_bias, sum_qkv
        )
        out_grad = out_sum.astype(f32)
        down_grad = down_sum.astype(f32)
        up_grad, gain_two_grad, shift_two_grad = finish(
            up_rows, up_weight, ln2_gain, ln2_bias, sum_up
        )

    qkv_bias_grad = lax.dynamic_slice_in_dim(sum_qkv, place * 3 * cols, 3 * cols)
    up_bias_grad = lax.dynamic_slice_in_dim(sum_up, place * wide, wide)
    return (
        out_given,
        tokens_grad,
        gain_one_grad.reshape(cols),
        shift_one_grad.reshape(cols),
        gain_two_grad.reshape(cols),
        shift_two_grad.reshape(cols),
        qkv_grad,
        qkv_bias_grad,
        out_grad,
        out_bias_grad,
        up_grad,
        up_bias_grad,
        down_grad,
        out_bias_grad,
    )


def solution(mesh):
    in_specs = (
        P(None, ("rep", "shard"), None, None),
        P(None, "rep", None, "shard"),
        P(None, "rep", None),
        P(None, "rep", None),
        P(None, "rep", None),
        P("shard"),
        P("shard"),
        P("shard"),
        P("shard"),
        P("shard", None),
        P("shard"),
        P("shard", None),
        P("shard"),
        P("shard", None),
        P("shard"),
        P("shard", None),
        P("shard"),
    )
    out_specs = (
        P(None, "rep", None, "shard"),
        P(None, ("rep", "shard"), None, None),
        P("shard"),
        P("shard"),
        P("shard"),
        P("shard"),
        P("shard", None),
        P("shard"),
        P("shard", None),
        P("shard"),
        P("shard", None),
        P("shard"),
        P("shard", None),
        P("shard"),
    )
    return jax.shard_map(local, mesh=mesh, in_specs=in_specs, out_specs=out_specs, check_vma=False)
```

```python
import jax
import jax.numpy as jnp
from jax import lax
from jax.experimental import pallas as pl
from jax.experimental.pallas import tpu as pltpu
from jax.sharding import PartitionSpec as P

D = 2048
HEADS = 8
HD = 256
ROT = 64
FF = 8192
BLK = 128
SEQ_MOST = 8
MB = 2
EPS = 1e-05
SCALE = HD ** (-0.5)

bf16 = jnp.bfloat16
f32 = jnp.float32

ORDER = (0, 2, 4, 6, 1, 3, 5, 7)


def dot(a, b, ca, cb):
    return lax.dot_general(a, b, (((ca,), (cb,)), ((), ())), preferred_element_type=f32)


def flip(value, bit):
    return lax.ppermute(value, "shard", [(i, i ^ bit) for i in range(8)])


def tie(*values):
    return lax.optimization_barrier(values)


def plus(a, b):
    return a.astype(f32) + b.astype(f32)


def rep_move(value, pairs):
    return lax.ppermute(value, "rep", pairs) if lax.axis_size("rep") == 4 else value


def rep_in(value):
    return rep_move(value, [(0, 1), (3, 2)])


def rep_over(value):
    return rep_move(value, [(1, 2), (2, 1)])


def rep_out(value):
    return rep_move(value, [(1, 0), (2, 3)])


def rotary_tables():
    half = ROT // 2
    freqs = 10000.0 ** (-2.0 * jnp.arange(half, dtype=f32) / ROT)
    angles = jnp.arange(SEQ_MOST * BLK, dtype=f32)[:, None] * freqs[None, :]
    rest = 128 - ROT
    cosine = jnp.concatenate(
        [jnp.cos(angles), jnp.cos(angles), jnp.ones((SEQ_MOST * BLK, rest), f32)], axis=-1
    )
    sine = jnp.concatenate(
        [-jnp.sin(angles), jnp.sin(angles), jnp.zeros((SEQ_MOST * BLK, rest), f32)], axis=-1
    )
    return cosine.reshape(SEQ_MOST, BLK, 128), sine.reshape(SEQ_MOST, BLK, 128)


def params_of(vmem=52):
    return pltpu.CompilerParams(vmem_limit_bytes=vmem * 2**20)


def cost(us):
    return pl.CostEstimate(flops=int(us * 1.1e9) + 1024, bytes_accessed=1024, transcendentals=0)


def tick(token, *arrays):
    def body(*refs):
        refs[-1][...] = refs[0][...]

    return pl.pallas_call(
        body,
        in_specs=[pl.BlockSpec(memory_space=pltpu.VMEM)] + [pl.BlockSpec(memory_space=pl.ANY)] * len(arrays),
        out_specs=pl.BlockSpec(memory_space=pltpu.VMEM),
        out_shape=jax.ShapeDtypeStruct(token.shape, token.dtype),
        compiler_params=params_of(16), cost_estimate=cost(2000),
    )(token, *arrays)


def spec(shape, index):
    return pl.BlockSpec(shape, index)


def attention_kernel(
    piece_of, inner_of, first_of, end_of,
    qkv_ref, grad_ref, cos_ref, sin_ref,
    ctx_ref, out_ref, sum_ref,
    q_buf, k_buf, v_buf, g_buf, dk_buf, dv_buf,
):
    m = pl.program_id(0)
    blocks = piece_of.shape[1]
    lane = lax.broadcasted_iota(jnp.int32, (BLK, 128), 1)
    tile = 2 * BLK

    def turned(x):
        return jnp.where(lane < ROT // 2, pltpu.roll(x, 128 - ROT // 2, 1), pltpu.roll(x, ROT // 2, 1))

    def store_part(p, i, start, value):
        low = value.astype(bf16)
        out_ref[p, 0, i, :, start:start + value.shape[1]] = low
        sum_ref[0, 0:1, start:start + value.shape[1]] += jnp.sum(low.astype(f32), axis=0, keepdims=True)

    def block_rows(g):
        return pl.ds(pl.multiple_of(g * BLK, BLK), BLK)

    def load(g, carry):
        p, i = piece_of[m, g], inner_of[m, g]
        at = g - first_of[m, g]
        cosine, sine = cos_ref[at], sin_ref[at]
        rows = block_rows(g)
        for buf, start in ((q_buf, 0), (k_buf, HD)):
            front = qkv_ref[p, 0, i, :, start:start + 128]
            buf[rows, 0:128] = (front * cosine + turned(front) * sine).astype(bf16)
            buf[rows, 128:HD] = qkv_ref[p, 0, i, :, start + 128:start + HD].astype(bf16)
        v_buf[rows, :] = qkv_ref[p, 0, i, :, 2 * HD:].astype(bf16)
        g_buf[rows, :] = grad_ref[p, 0, i]
        return carry

    lax.fori_loop(0, blocks, load, 0, unroll=4)
    for buf in (q_buf, k_buf, v_buf, g_buf):
        buf[blocks * BLK:, :] = jnp.zeros((BLK, HD), bf16)
    sum_ref[...] = jnp.zeros(sum_ref.shape, f32)
    dk_buf[...] = jnp.zeros(dk_buf.shape, f32)
    dv_buf[...] = jnp.zeros(dv_buf.shape, f32)

    def attend(g, span):
        first = first_of[m, g]
        rows = pl.ds(pl.multiple_of(g * BLK, BLK), tile)
        keys = pl.ds(pl.multiple_of(first * BLK, BLK), span)
        query, grad = q_buf[rows, :], g_buf[rows, :]
        key, value = k_buf[keys, :], v_buf[keys, :]
        after_g = jnp.minimum(g + 1, blocks - 1)
        second = (g + 1 < blocks) & (first_of[m, after_g] == first)
        scores = dot(query, key, 1, 1) * SCALE
        key_tok = first * BLK + lax.broadcasted_iota(jnp.int32, (tile, span), 1)
        query_tok = g * BLK + lax.broadcasted_iota(jnp.int32, (tile, span), 0)
        allowed = (key_tok <= query_tok) & (key_tok < end_of[m, g])
        scores = jnp.where(allowed, scores, -jnp.inf)
        exponent = jnp.exp(scores - jnp.max(scores, axis=1, keepdims=True))
        scale = 1.0 / jnp.sum(exponent, axis=1, keepdims=True)
        last_row = jnp.where(second, tile, BLK)
        row = lax.broadcasted_iota(jnp.int32, (tile, 1), 0)
        prob = exponent * jnp.where(row < last_row, scale, 0.0)
        prob_low = prob.astype(bf16)
        ctx = dot(prob_low, value, 1, 0).astype(bf16)
        prob_grad = dot(grad, value, 1, 1)
        delta = jnp.sum(prob * prob_grad, axis=1, keepdims=True)
        score_grad = (prob * (prob_grad - delta)).astype(bf16)
        dk_buf[keys, :] += dot(score_grad, query, 0, 0)
        dv_buf[keys, :] += dot(prob_low, grad, 0, 0)
        query_grad = dot(score_grad, key, 1, 0) * SCALE

        def put(block, lo):
            p, i = piece_of[m, block], inner_of[m, block]
            at = block - first
            ctx_ref[p, 0, i] = ctx[lo:lo + BLK]
            front = query_grad[lo:lo + BLK, 0:128]
            store_part(p, i, 0, front * cos_ref[at] - turned(front) * sin_ref[at])
            store_part(p, i, 128, query_grad[lo:lo + BLK, 128:])

        put(g, 0)
        pl.when(second)(lambda: put(after_g, BLK))

    def one_block(g, carry):
        at = g - first_of[m, g]
        for count in range(SEQ_MOST // 2):
            pl.when(at == 2 * count)(lambda: attend(g, (count + 1) * tile))
        return carry

    lax.fori_loop(0, blocks, one_block, 0)

    def store(g, carry):
        p, i = piece_of[m, g], inner_of[m, g]
        at = g - first_of[m, g]
        rows = block_rows(g)
        front = dk_buf[rows, 0:128] * SCALE
        store_part(p, i, HD, front * cos_ref[at] - turned(front) * sin_ref[at])
        store_part(p, i, HD + 128, dk_buf[rows, 128:HD] * SCALE)
        store_part(p, i, 2 * HD, dv_buf[rows, :])
        return carry

    lax.fori_loop(0, blocks, store, 0, unroll=4)


def attention(tables, qkv, grad, cosine, sine):
    pieces, _, own = qkv.shape[:3]
    blocks = tables[0].shape[1]

    def part(width):
        return pl.BlockSpec((pieces, 1, own, BLK, width), lambda m, *_: (0, m, 0, 0, 0))

    whole = pl.BlockSpec((SEQ_MOST, BLK, 128), lambda m, *_: (0, 0, 0))
    rows = (blocks + 1) * BLK
    return pl.pallas_call(
        attention_kernel,
        grid_spec=pltpu.PrefetchScalarGridSpec(
            num_scalar_prefetch=4,
            grid=(MB,),
            in_specs=[part(3 * HD), part(HD), whole, whole],
            out_specs=[part(HD), part(3 * HD), spec((1, 8, 3 * HD), lambda m, *_: (m, 0, 0))],
            scratch_shapes=[
                pltpu.VMEM((rows, HD), bf16),
                pltpu.VMEM((rows, HD), bf16),
                pltpu.VMEM((rows, HD), bf16),
                pltpu.VMEM((rows, HD), bf16),
                pltpu.VMEM((rows, HD), f32),
                pltpu.VMEM((rows, HD), f32),
            ],
        ),
        out_shape=[
            jax.ShapeDtypeStruct((pieces, MB, own, BLK, HD), bf16),
            jax.ShapeDtypeStruct((pieces, MB, own, BLK, 3 * HD), bf16),
            jax.ShapeDtypeStruct((MB, 8, 3 * HD), f32),
        ],
        compiler_params=params_of(),
        cost_estimate=cost(0),
    )(*tables, qkv, grad, cosine, sine)


def plus_low(a, b, index=None, needed=None):
    shape = a.shape if index is None else a.shape[1:]
    if index is None:
        a, b, index = a[None], b[None], 0
    if needed is None:
        needed = jnp.ones((1,), jnp.int32)
    a, b = [x.reshape(x.shape[0], -1, x.shape[-1]) for x in (a, b)]
    rows, cols = a.shape[1:]
    steps = next(n for n in (2, 3, 1) if rows % (16 * n) == 0)
    block = spec((1, rows // steps, cols), lambda i, needed_ref: (index, i * needed_ref[0], 0))

    def body(needed_ref, a_ref, b_ref, out_ref):
        @pl.when((needed_ref[0] == 1) | (pl.program_id(0) == 0))
        def _():
            out_ref[...] = plus(a_ref[0], b_ref[0]).astype(bf16)

    return pl.pallas_call(
        body,
        grid_spec=pltpu.PrefetchScalarGridSpec(
            num_scalar_prefetch=1, grid=(steps,), in_specs=[block, block],
            out_specs=spec((rows // steps, cols), lambda i, needed_ref: (i * needed_ref[0], 0)),
        ),
        out_shape=jax.ShapeDtypeStruct((rows, cols), bf16),
        compiler_params=params_of(32), cost_estimate=cost(0),
    )(needed, a, b).reshape(shape)


def out_terms(owners, place, context, active, out_w, down_w, resid, came=None):
    rows, inner = active.shape
    n = resid.shape[0]
    cols = D // 8
    first = 4 if came is None else 0

    def terms(place_ref, refs):
        ctx, act = refs[0][...], refs[1][...]
        own = pl.program_id(0) == place_ref[0]
        return [
            dot(ctx, refs[2 + b][...], 1, 0)
            + dot(act, refs[6 + b][...], 1, 0)
            + jnp.where(own, refs[10 + b][...].astype(f32), 0.0)
            for b in range(4)
        ]

    def odd_body(owners_ref, place_ref, *refs):
        for b, part in enumerate(terms(place_ref, refs)):
            refs[14][b] = part.astype(bf16)

    def even_body(owners_ref, place_ref, *refs):
        got, send_one, keep_one, send_two, keep_two = refs[14:]
        parts = [(p + got[b].astype(f32)).astype(bf16) for b, p in enumerate(terms(place_ref, refs))]

        @pl.when(pl.program_id(0) < 4)
        def _():
            send_one[0], send_one[1] = parts[1], parts[3]
            keep_one[0], keep_one[1] = parts[0], parts[2]

        @pl.when(pl.program_id(0) >= 4)
        def _():
            send_two[0], send_two[1] = parts[2], parts[3]
            keep_two[0], keep_two[1] = parts[0], parts[1]

    def columns(height, b):
        return spec((height, cols), lambda i, o, p: (0, o[first + b]))

    in_specs = [
        spec((n, context.shape[1]), lambda i, o, p: (i, 0)),
        spec((n, inner), lambda i, o, p: (i, 0)),
        *[columns(context.shape[1], b) for b in range(4)],
        *[columns(inner, b) for b in range(4)],
        *[columns(n, b) for b in range(4)],
    ]
    args = [context, active, *[out_w] * 4, *[down_w] * 4, *[resid] * 4]
    if came is None:
        body = odd_body
        out_specs = spec((4, n, cols), lambda i, o, p: (0, i, 0))
        out_shape = jax.ShapeDtypeStruct((4, rows, cols), bf16)
    else:
        body = even_body
        in_specs.append(spec((4, n, cols), lambda i, o, p: (0, i, 0)))
        args.append(came)
        low = spec((2, n, cols), lambda i, o, p: (0, jnp.minimum(i, 3), 0))
        high = spec((2, n, cols), lambda i, o, p: (0, jnp.maximum(i - 4, 0), 0))
        out_specs = [low, low, high, high]
        out_shape = [jax.ShapeDtypeStruct((2, rows // 2, cols), bf16)] * 4
    return pl.pallas_call(
        body,
        grid_spec=pltpu.PrefetchScalarGridSpec(
            num_scalar_prefetch=2, grid=(8,), in_specs=in_specs, out_specs=out_specs
        ),
        out_shape=out_shape, compiler_params=params_of(), cost_estimate=cost(0),
    )(owners, place.reshape(1), *args)


def norm_terms(owners, mixed_grad, hidden_grad, qkv_w, up_w, came=None):
    rows = mixed_grad.shape[0]
    n = rows // 16
    first = 4 if came is None else 0

    def terms(refs):
        one, two, w_one, w_two = refs
        return dot(one[...], w_one[...], 1, 1) + dot(two[...], w_two[...], 1, 1)

    def odd_body(owners_ref, *refs):
        refs[4][0, 0] = terms(refs[:4]).astype(bf16)

    def even_body(owners_ref, *refs):
        got, send_one, keep_one, send_two, keep_two = refs[4:]
        sums = (terms(refs[:4]) + got[0, 0].astype(f32)).astype(bf16)
        i = pl.program_id(0)
        for ref, steps in (
            (keep_one, (0, 4)), (send_one, (2, 6)), (keep_two, (1, 3)), (send_two, (5, 7)),
        ):
            @pl.when((i == steps[0]) | (i == steps[1]))
            def _():
                ref[0] = sums

    def own_rows(i, o):
        return (o[first + i // 2] * 2 + i % 2, 0)

    in_specs = [
        spec((n, mixed_grad.shape[1]), own_rows),
        spec((n, hidden_grad.shape[1]), own_rows),
        spec(qkv_w.shape, lambda i, o: (0, 0)),
        spec(up_w.shape, lambda i, o: (0, 0)),
    ]
    args = [mixed_grad, hidden_grad, qkv_w, up_w]
    if came is None:
        body = odd_body
        out_specs = spec((1, 1, n, D), lambda i, o: (i // 2, i % 2, 0, 0))
        out_shape = jax.ShapeDtypeStruct((4, 2, n, D), bf16)
    else:
        body = even_body
        in_specs.append(spec((1, 1, n, D), lambda i, o: (i // 2, i % 2, 0, 0)))
        args.append(came)
        out_specs = [
            spec((1, n, D), lambda i, o: (i // 4, 0, 0)),
            spec((1, n, D), lambda i, o: (i // 4, 0, 0)),
            spec((1, n, D), lambda i, o: (jnp.maximum(i - 4, 0) // 2, 0, 0)),
            spec((1, n, D), lambda i, o: (jnp.minimum(i // 2, 1), 0, 0)),
        ]
        out_shape = [jax.ShapeDtypeStruct((2, n, D), bf16)] * 4
    return pl.pallas_call(
        body,
        grid_spec=pltpu.PrefetchScalarGridSpec(
            num_scalar_prefetch=1, grid=(8,), in_specs=in_specs, out_specs=out_specs
        ),
        out_shape=out_shape, compiler_params=params_of(), cost_estimate=cost(0),
    )(owners, *args)


def token_dot(left, right, part=0, parts=1, extra=None):
    rows, width = left.shape[0], left.shape[1] // parts
    blocks, _, cols = right.shape
    step = 512 // cols
    more = [] if extra is None else [extra]
    total = width + sum(m.shape[0] for m in more)

    def body(left_ref, right_ref, *refs):
        out_ref = refs[-1]
        for b in range(step):
            at = slice(b * cols, (b + 1) * cols)
            out_ref[0:width, at] = dot(left_ref[...], right_ref[b], 0, 0).astype(bf16)
        if more:
            out_ref[width:, :] = refs[0][...]

    return pl.pallas_call(
        body, grid=(blocks // step,),
        in_specs=[
            spec((rows, width), lambda i: (0, part)),
            spec((step, rows, cols), lambda i: (i, 0, 0)),
        ] + [spec((m.shape[0], step * cols), lambda i: (0, i)) for m in more],
        out_specs=spec((total, step * cols), lambda i: (0, i)),
        out_shape=jax.ShapeDtypeStruct((total, blocks * cols), bf16),
        compiler_params=params_of(56), cost_estimate=cost(0),
    )(left, right, *more)


EXTRA = 16


def normed_dot(spot, shards, normed, right, sums, part=0, parts=1):
    rows, tile = normed.shape[0], 512
    cols, width = D // shards, right.shape[1] // parts
    per = tile // cols

    def body(spot_ref, left_ref, right_ref, sum_ref, out_ref):
        sums = dot(left_ref[...], right_ref[...], 0, 0).astype(bf16)
        high = sum_ref[...]
        first = high.astype(bf16).astype(f32)
        second = (high - first).astype(bf16).astype(f32)
        third = high - first - second
        row = lax.broadcasted_iota(jnp.int32, (EXTRA, width), 0) - 3 * spot_ref[0]
        extra = jnp.where(row == 0, first, jnp.where(row == 1, second, jnp.where(row == 2, third, 0.0)))
        for b in range(per):
            out_ref[b, 0:cols, :] = sums[b * cols:(b + 1) * cols]
            out_ref[b, cols:, :] = extra.astype(bf16)

    return pl.pallas_call(
        body,
        grid_spec=pltpu.PrefetchScalarGridSpec(
            num_scalar_prefetch=1, grid=(D // tile,),
            in_specs=[
                spec((rows, tile), lambda i, z: (0, i)),
                spec((rows, width), lambda i, z: (0, part)),
                spec((1, width), lambda i, z: (0, part)),
            ],
            out_specs=spec((per, cols + EXTRA, width), lambda i, z: (i, 0, 0)),
        ),
        out_shape=jax.ShapeDtypeStruct((shards, cols + EXTRA, width), bf16),
        compiler_params=params_of(56), cost_estimate=cost(0),
    )(spot, normed, right, sums)


def whole_rows(ref):
    return jnp.concatenate([ref[b] for b in range(ref.shape[0])], axis=1)


def out_blocks(piece_of, inner_of, own, parts, bias):
    blocks = piece_of.shape[1]
    half, cols = parts[0][2].shape

    def body(piece_ref, inner_ref, *refs):
        bias_ref, out_ref, all_rows = refs[6:]
        m = pl.program_id(0)

        @pl.when(m == 0)
        def _():
            for h in range(2):
                keep, came, last = refs[3 * h:3 * h + 3]
                sums = plus(keep[0], came[0]) + last[...].astype(f32) + bias_ref[...]
                all_rows[h * half:(h + 1) * half, :] = sums.astype(bf16)

        def one(g, carry):
            row = ((piece_ref[m, g] * MB + m) * own + inner_ref[m, g]) * BLK
            out_ref[0, g] = all_rows[pl.ds(pl.multiple_of(row, BLK), BLK), :]
            return carry

        lax.fori_loop(0, blocks, one, 0)

    first = spec((1, half, cols), lambda m, *_: (0, 0, 0))
    whole = spec((half, cols), lambda m, *_: (0, 0))
    return pl.pallas_call(
        body,
        grid_spec=pltpu.PrefetchScalarGridSpec(
            num_scalar_prefetch=2, grid=(MB,),
            in_specs=[first, first, whole] * 2 + [spec((1, cols), lambda m, *_: (0, 0))],
            out_specs=spec((1, blocks, BLK, cols), lambda m, *_: (m, 0, 0, 0)),
            scratch_shapes=[pltpu.VMEM((2 * half, cols), bf16)],
        ),
        out_shape=jax.ShapeDtypeStruct((MB, blocks, BLK, cols), bf16),
        compiler_params=params_of(), cost_estimate=cost(0),
    )(piece_of, inner_of, *parts[0], *parts[1], bias[None])


def token_grads(tokens, grad_rows, parts):
    rows = tokens.shape[0]
    n = rows // 4

    def body(tokens_ref, grad_ref, *refs):
        out_ref = refs[6]
        x = tokens_ref[...].astype(f32)
        center = x - jnp.mean(x, axis=1, keepdims=True)
        inv_std = lax.rsqrt(jnp.mean(center * center, axis=1, keepdims=True) + EPS)
        normed = center * inv_std

        def finish(keep, came, last):
            grad = plus(keep[0], came[0]) + last[...].astype(f32)
            mean = jnp.mean(grad, axis=1, keepdims=True)
            proj = jnp.mean(grad * normed, axis=1, keepdims=True)
            grad = inv_std * (grad - mean - normed * proj)
            out_ref[...] = (grad_ref[...].astype(f32) + grad).astype(bf16)

        pl.when(pl.program_id(0) < 2)(lambda: finish(*refs[0:3]))
        pl.when(pl.program_id(0) >= 2)(lambda: finish(*refs[3:6]))

    own = spec((n, D), lambda i: (i, 0))
    in_specs = [own, own]
    for at in (lambda i: jnp.minimum(i, 1), lambda i: jnp.maximum(i - 2, 0)):
        first = spec((1, n, D), lambda i, at=at: (0, at(i), 0))
        in_specs += [first, first, spec((n, D), lambda i, at=at: (at(i), 0))]
    return pl.pallas_call(
        body, grid=(4,), in_specs=in_specs, out_specs=own,
        out_shape=jax.ShapeDtypeStruct((rows, D), bf16),
        compiler_params=params_of(), cost_estimate=cost(0),
    )(tokens, grad_rows, *parts[0], *parts[1])


def sum_rows(vector, spot):
    thirds, left = [], vector
    for _ in range(3):
        thirds.append(lax.reduce_precision(left, 8, 7))
        left = left - thirds[-1]
    mine = jnp.arange(4)[:, None, None] == spot
    values = jnp.where(mine, jnp.stack(thirds)[None], 0.0).reshape(-1)
    return jnp.pad(values, (0, 16 * D - values.shape[0])).reshape(16, D).astype(bf16)


def sums_of(found, size):
    return jnp.sum(found.astype(f32).reshape(-1)[:12 * size].reshape(12, size), axis=0)


def hidden_back(grad_out, down_w, slope):
    rows, wide = slope.shape
    n = rows // 8

    def body(grad_ref, w_ref, slope_ref, out_ref, sum_ref):
        active_grad = dot(whole_rows(grad_ref), w_ref[...], 1, 1).astype(bf16).astype(f32)
        value = (active_grad * slope_ref[...]).astype(bf16)
        out_ref[...] = value
        total = jnp.sum(value.astype(f32), axis=0, keepdims=True)

        @pl.when(pl.program_id(0) == 0)
        def _():
            sum_ref[...] = total

        @pl.when(pl.program_id(0) > 0)
        def _():
            sum_ref[...] += total

    return pl.pallas_call(
        body, grid=(8,),
        in_specs=[
            spec((grad_out.shape[0], n, grad_out.shape[2]), lambda i: (0, i, 0)),
            spec((wide, D), lambda i: (0, 0)),
            spec((n, wide), lambda i: (i, 0)),
        ],
        out_specs=[spec((n, wide), lambda i: (i, 0)), spec((1, wide), lambda i: (0, 0))],
        out_shape=[
            jax.ShapeDtypeStruct((rows, wide), bf16), jax.ShapeDtypeStruct((1, wide), f32),
        ],
        compiler_params=params_of(), cost_estimate=cost(0),
    )(grad_out, down_w, slope)


def head_back(grad_out, out_w):
    blocks, rows, cols = grad_out.shape
    n = rows // 8

    def body(grad_ref, w_ref, out_ref):
        out_ref[...] = dot(whole_rows(grad_ref), w_ref[...], 1, 1).astype(bf16)

    return pl.pallas_call(
        body, grid=(8,),
        in_specs=[
            spec((blocks, n, cols), lambda i: (0, i, 0)),
            spec((HD, D), lambda i: (0, 0)),
        ],
        out_specs=spec((n, HD), lambda i: (i, 0)),
        out_shape=jax.ShapeDtypeStruct((rows, HD), bf16),
        compiler_params=params_of(), cost_estimate=cost(0),
    )(grad_out, out_w)


def row_grads(inner, chunks, count=None):
    rows = [count or c[0].shape[0] for c in chunks]
    total, cols = sum(rows), 512

    def body(inner_ref, *refs):
        at = 0
        for c, n in enumerate(rows):
            one, two = refs[2 * c][...].astype(f32), refs[2 * c + 1][...].astype(f32)
            refs[-1][at:at + n, :] = jnp.where(inner_ref[0] == 1, one, two)
            at += n

    return pl.pallas_call(
        body,
        grid_spec=pltpu.PrefetchScalarGridSpec(
            num_scalar_prefetch=1, grid=(D // cols,),
            in_specs=[spec((n, cols), lambda i, *_: (0, i)) for n in rows for _ in range(2)],
            out_specs=spec((total, cols), lambda i, *_: (0, i)),
        ),
        out_shape=jax.ShapeDtypeStruct((total, D), f32),
        compiler_params=params_of(32), cost_estimate=cost(0),
    )(inner, *[a for c in chunks for a in c])


def column_grads(inner, chunks, weight, gain, shift, run, step, by_run, token=None):
    rows, each = weight.shape[0], len(chunks[0])
    if by_run:
        groups, per = len(chunks), chunks[0][0].shape[0] // step
        steps = per
    else:
        groups, per = chunks[0][0].shape[2] // run, chunks[0][0].shape[0] // step
        steps = per * len(chunks)

    tokens = [] if token is None else [token]

    def body(inner_ref, *refs):
        pairs, refs = refs[:each * len(chunks)], refs[each * len(chunks) + len(tokens):]
        w_ref, gain_ref, shift_ref, grads, gain_out, shift_out, t_out = refs
        i, k = pl.program_id(0), pl.program_id(1)

        @pl.when((i == 0) & (k == 0))
        def _():
            gain_out[...] = jnp.zeros_like(gain_out)
            shift_out[...] = jnp.zeros_like(shift_out)

        for c in range(len(chunks)):
            @pl.when((k if by_run else i // per) == c)
            def _():
                for j in range(step):
                    value = pairs[each * c][j].astype(f32)
                    if each == 2:
                        other = pairs[2 * c + 1][j].astype(f32)
                        value = jnp.where(inner_ref[0] == 1, value, other)
                    at = slice(j * run, (j + 1) * run)
                    t = jnp.sum(value[rows:], axis=0, keepdims=True)
                    value, w = value[:rows], w_ref[:, at].astype(f32)
                    t_out[:, at] = t
                    grads[:, at] = gain_ref[...] * value + shift_ref[...] * t
                    for out, terms in ((gain_out, w * value), (shift_out, w * t)):
                        out[...] += sum(terms[:, lo:lo + 128] for lo in range(0, run, 128))

    def part_index(c):
        if by_run:
            return lambda i, k, *_: (i, 0, 0)
        return lambda i, k, *_: (jnp.clip(i - c * per, 0, per - 1), 0, k)

    def columns(i, k, *_):
        return (0, i * groups + k if by_run else k * steps + i)

    column = spec((rows, 1), lambda i, k, *_: (0, 0))
    wide_column = spec((rows, 128), lambda i, k, *_: (0, 0))
    grads, gain_grad, shift_grad, totals = pl.pallas_call(
        body,
        grid_spec=pltpu.PrefetchScalarGridSpec(
            num_scalar_prefetch=1, grid=(steps, groups),
            in_specs=[spec((step, rows + EXTRA, run), part_index(c)) for c in range(len(chunks)) for _ in range(each)]
            + [pl.BlockSpec(memory_space=pl.ANY)] * len(tokens)
            + [spec((rows, step * run), columns), column, column],
            out_specs=[
                spec((rows, step * run), columns), wide_column, wide_column,
                spec((1, step * run), columns),
            ],
        ),
        out_shape=[
            jax.ShapeDtypeStruct(weight.shape, f32),
            jax.ShapeDtypeStruct((rows, 128), f32),
            jax.ShapeDtypeStruct((rows, 128), f32),
            jax.ShapeDtypeStruct((1, weight.shape[1]), f32),
        ],
        compiler_params=params_of(32), cost_estimate=cost(0),
    )(
        inner, *[a for c in chunks for a in c], *tokens, weight,
        gain.astype(f32)[:, None], shift.astype(f32)[:, None],
    )
    return grads, jnp.sum(gain_grad, axis=1), jnp.sum(shift_grad, axis=1), totals[0]


def local(
    tokens, cotangent, seq_blocks, seq_pad, deal_order,
    ln1_gain, ln1_bias, ln2_gain, ln2_bias,
    qkv_weight, qkv_bias, out_weight, out_bias, up_weight, up_bias, down_weight, down_bias,
):
    shards = lax.axis_size("shard")
    place = lax.axis_index("shard")
    cube = shards == 8 and lax.axis_size("rep") == 4
    own = tokens.shape[1]
    blocks = deal_order.shape[2]
    own_rows = MB * own * BLK
    rows = shards * own_rows
    cols = D // shards
    wide = FF // shards
    split = shards // HEADS
    head, share = place // split, place % split
    share_cols = 3 * HD // split

    if cube:
        owners = jnp.bitwise_xor(place, jnp.array(ORDER, jnp.int32))
    deal = deal_order[:, 0, :]
    counts = seq_blocks[:, 0, :]
    pads = seq_pad[:, 0, :]
    ids = jnp.arange(blocks, dtype=jnp.int32)
    inverse = jnp.sum(
        jnp.where(deal[:, None, :] == ids[None, :, None], ids[None, None, :], 0), axis=-1
    )
    piece_of, inner_of = inverse // own, inverse % own
    ends = jnp.cumsum(counts, axis=1)
    starts = ends - counts
    inside = (ids[None, :, None] >= starts[:, None, :]) & (ids[None, :, None] < ends[:, None, :])
    first_of = jnp.sum(jnp.where(inside, starts[:, None, :], 0), axis=-1)
    valid = jnp.sum(jnp.where(inside, (counts * BLK - pads)[:, None, :], 0), axis=-1)
    tables = [t.astype(jnp.int32) for t in (piece_of, inner_of, first_of, first_of * BLK + valid)]
    given = deal.reshape(MB, shards, own)

    cot_own = jnp.stack([cotangent[m][given[m]] for m in range(MB)], axis=1)

    def swap(value):
        return lax.all_to_all(value, "shard", split_axis=0, concat_axis=0, tiled=True)

    token = jnp.zeros((8, 128), f32)

    def gate(*arrays):
        nonlocal token
        if cube:
            token = tick(token, *arrays)

    def late(value):
        nonlocal token
        if cube:
            value, token = tie(value, token)
        return value

    flat = tokens.reshape(own_rows, D).astype(f32)
    center = flat - jnp.mean(flat, axis=-1, keepdims=True)
    inv_std = lax.rsqrt(jnp.mean(center * center, axis=-1, keepdims=True) + EPS)
    normed_own = center * inv_std
    normed_low = normed_own.astype(bf16)
    normed = lax.all_gather(normed_low, "shard", axis=0, tiled=True)
    gate(normed_low)

    shares = lax.axis_size("rep") if cube else 1
    part_rows = cols // shares
    spot = lax.axis_index("rep") if cube else 0
    up_late, qkv_late = late((up_weight, qkv_weight))

    def part_of(array):
        return lax.dynamic_slice_in_dim(array, spot * part_rows, part_rows, 0).astype(f32)

    def with_shift(weight, gain, shift):
        high = lax.reduce_precision(shift, 8, 7)
        low = lax.reduce_precision(shift - high, 8, 7)
        tail = jnp.zeros((14, shift.shape[0]), bf16)
        scaled = (part_of(weight) * part_of(gain)[:, None]).astype(bf16)
        return jnp.concatenate([scaled, high.astype(bf16)[None], low.astype(bf16)[None], tail], axis=0)

    shift_up = jnp.sum(up_late.astype(f32) * ln2_bias.astype(f32)[:, None], axis=0)
    shift_qkv = jnp.sum(qkv_late.astype(f32) * ln1_bias.astype(f32)[:, None], axis=0)
    own_bias = lax.dynamic_slice_in_dim(shift_qkv, place * 3 * cols, 3 * cols) + qkv_bias.astype(f32)
    shift_qkv = lax.dynamic_update_slice_in_dim(shift_qkv, own_bias, place * 3 * cols, 0)
    sent_rows = part_rows + 16
    up_send = with_shift(up_late, ln2_gain, shift_up).reshape(sent_rows, shards, wide).transpose(1, 0, 2)
    qkv_send = with_shift(qkv_late, ln1_gain, shift_qkv).reshape(sent_rows, 3, HEADS, HD)
    qkv_send = qkv_send.transpose(2, 0, 1, 3).reshape(HEADS, sent_rows, 3 * HD)
    if split > 1:
        qkv_send = jnp.repeat(qkv_send, split, axis=0)
    found = swap(jnp.concatenate([up_send, qkv_send], axis=2))
    cot_late = late(cot_own)
    grad_out = lax.all_gather(cot_late.reshape(rows, cols), "shard", axis=0)
    gate(up_send, qkv_send, cot_late)
    found = late(found)
    biases = jnp.sum(found[:, part_rows:part_rows + 2].astype(f32), axis=(0, 1))

    def exchange(part):
        return [part] + [
            lax.ppermute(part, "rep", [(i, (i + k) % shares) for i in range(shares)])
            for k in range(1, shares)
        ]

    def whole(parts):
        if shares == 1:
            return parts[0].reshape(D, parts[0].shape[-1])
        width = parts[0].shape[-1]
        array = jnp.zeros((shards, shares, part_rows, width), bf16)
        for k, part in enumerate(parts):
            at = lax.rem(spot - k + shares, shares)
            array = lax.dynamic_update_slice(array, part[:, None], (0, at, 0, 0))
        return array.reshape(D, width)

    up_parts = exchange(found[:, :part_rows, :wide])
    normed, up_parts, biases = tie(normed, up_parts, biases)
    up_w = whole(up_parts)
    found, up_w = tie(found, up_w)
    qkv_parts = exchange(found[:, :part_rows, wide:])
    bias_up, bias_qkv = biases[:wide] + up_bias.astype(f32), biases[wide:]
    out_w, down_w, resid = out_weight, down_weight, tokens.reshape(own_rows, D)

    hidden = dot(normed, up_w, 1, 0) + bias_up
    cdf = 0.5 + 0.5 * lax.erf(hidden * (0.5 ** 0.5))
    density = jnp.exp(-0.5 * hidden * hidden) * 0.3989422804014327
    active = (hidden * cdf).astype(bf16)
    slope = cdf + hidden * density
    grad_out, active = tie(grad_out, active)

    where_rep = jnp.asarray(spot, jnp.int32).reshape(1)
    inner = ((where_rep == 1) | (where_rep == 2)).astype(jnp.int32)

    down_parts = [token_dot(active, grad_out, 0, 2)]
    down_came = [rep_in(down_parts[0])]
    gate(down_parts[0])
    hidden_grad, sum_hidden = hidden_back(late(grad_out), down_w, slope)
    sum_cot = jnp.sum(cot_own, axis=tuple(range(cot_own.ndim - 1)), dtype=f32)
    extra = sum_rows(sum_cot, spot) if cube else None
    down_parts.append(token_dot(active, grad_out, 1, 2, extra))
    hidden_grad, down_parts[1] = tie(hidden_grad, down_parts[1])
    up_terms = [normed_dot(where_rep, shards, normed, hidden_grad, sum_hidden, 0, 2)]
    up_found = [swap(up_terms[0])]
    down_came[0], up_terms[0] = tie(down_came[0], up_terms[0])
    down_pair = [plus_low(down_parts[0], down_came[0], needed=inner)]
    down_other = [rep_over(down_pair[0])]
    down_came.append(rep_in(down_parts[1]))
    gate(down_pair[0], up_terms[0])

    context_w = out_w
    if split > 1:
        pairs = [list(range(h * split, (h + 1) * split)) for h in range(HEADS)]
        context_w = lax.all_gather(out_w, "shard", axis=0, tiled=True, axis_index_groups=pairs)
    up_terms.append(normed_dot(where_rep, shards, late(normed), hidden_grad, sum_hidden, 1, 2))
    grad_out, up_terms[1] = tie(grad_out, up_terms[1])
    context_grad = head_back(grad_out, context_w)
    qkv_parts, context_grad = tie(qkv_parts, context_grad)
    qkv_w = whole(qkv_parts)
    mixed = dot(normed, qkv_w, 1, 0) + bias_qkv
    down_other[0], down_came[1], up_found[0], mixed = tie(down_other[0], down_came[1], up_found[0], mixed)
    down_total = [plus_low(down_pair[0], down_other[0], needed=inner)]
    down_back = [rep_out(down_total[0])]
    down_pair.append(plus_low(down_parts[1], down_came[1], needed=inner))
    down_other.append(rep_over(down_pair[1]))
    up_came = [rep_in(up_found[0])]
    up_terms[1], up_found[0] = tie(up_terms[1], up_found[0])
    up_found.append(swap(up_terms[1]))
    gate(down_total[0], down_pair[1], up_found[0])
    cosine, sine = rotary_tables()
    context, mixed_grad, sum_mixed = attention(
        tables,
        late(mixed).reshape(shards, MB, own, BLK, 3 * HD),
        context_grad.reshape(shards, MB, own, BLK, HD),
        cosine,
        sine,
    )
    context = context.reshape(rows, HD)
    mixed_grad = mixed_grad.reshape(rows, 3 * HD)
    down_back[0], down_other[1], up_came[0], up_found[1], context = tie(
        down_back[0], down_other[1], up_came[0], up_found[1], context
    )
    down_total.append(plus_low(down_pair[1], down_other[1], needed=inner))
    down_back.append(rep_out(down_total[1]))
    up_pair = [plus_low(up_found[0], up_came[0], needed=inner)]
    up_other = [rep_over(up_pair[0])]
    up_came.append(rep_in(up_found[1]))
    gate(down_back[0], down_total[1], up_pair[0], up_found[1])
    mixed_grad = late(mixed_grad)
    if split > 1:
        context = lax.dynamic_slice_in_dim(context, share * (HD // split), HD // split, 1)
        mixed_grad = lax.dynamic_slice_in_dim(mixed_grad, share * share_cols, share_cols, 1)
        qkv_w = lax.dynamic_slice_in_dim(qkv_w, share * share_cols, share_cols, 1)
        sum_mixed = lax.dynamic_slice_in_dim(sum_mixed, share * share_cols, share_cols, 2)
    sum_mixed = jnp.sum(sum_mixed, axis=(0, 1))[None]
    qkv_terms = normed_dot(where_rep, shards, normed, mixed_grad, sum_mixed)
    qkv_found = swap(qkv_terms)
    if cube:
        context, qkv_terms = tie(context, qkv_terms)
        out_part = token_dot(context, grad_out)
        out_came = rep_in(out_part)

        context, out_part = tie(context, out_part)
        odd = out_terms(owners, place, context, active, out_w, down_w, resid)
        odd_came = flip(odd, 1)
        down_back[1], up_other[0], up_came[1], odd = tie(down_back[1], up_other[0], up_came[1], odd)
        up_total = [plus_low(up_pair[0], up_other[0], needed=inner)]
        up_back = [rep_out(up_total[0])]
        up_pair.append(plus_low(up_found[1], up_came[1], needed=inner))
        up_other.append(rep_over(up_pair[1]))
        gate(down_back[1], up_total[0], up_pair[1], qkv_terms, odd)

        norm_odd = norm_terms(owners, late(mixed_grad), hidden_grad, qkv_w, up_w)
        norm_odd_came = flip(norm_odd, 1)
        odd_came, norm_odd = tie(odd_came, norm_odd)
        send_one, keep_one, send_two, keep_two = out_terms(
            owners, place, context, active, out_w, down_w, resid, odd_came
        )
        got_one, got_two = flip(send_one, 2), flip(send_two, 4)
        up_back[0], up_other[1], out_came, qkv_found, keep_one = tie(
            up_back[0], up_other[1], out_came, qkv_found, keep_one
        )
        up_total.append(plus_low(up_pair[1], up_other[1], needed=inner))
        up_back.append(rep_out(up_total[1]))
        qkv_parts = [qkv_found[:shards // 2], qkv_found[shards // 2:]]
        qkv_came = [rep_in(part) for part in qkv_parts]
        gate(up_back[0], up_total[1], out_came, *qkv_parts, norm_odd, send_one)

        norm_send_one, norm_keep_one, norm_send_two, norm_keep_two = norm_terms(
            owners, mixed_grad, hidden_grad, qkv_w, up_w, late(norm_odd_came)
        )
        norm_got_one, norm_got_two = flip(norm_send_one, 2), flip(norm_send_two, 4)

        qkv_came[0], norm_keep_one = tie(qkv_came[0], norm_keep_one)
        qkv_pair = [plus_low(qkv_parts[0], qkv_came[0], needed=inner)]
        qkv_other = [rep_over(qkv_pair[0])]
        out_came, qkv_pair[0] = tie(out_came, qkv_pair[0])
        got_one, got_two, out_came = tie(got_one, got_two, out_came)
        out_pair = plus_low(out_part, out_came, needed=inner)
        out_other = rep_over(out_pair)
        keep_one, keep_two, out_pair = tie(keep_one, keep_two, out_pair)
        last_one = plus_low(keep_one, got_one, 1)
        last_two = plus_low(keep_two, got_two, 1)
        qkv_came[1], last_one, last_two = tie(qkv_came[1], last_one, last_two)
        qkv_pair.append(plus_low(qkv_parts[1], qkv_came[1], needed=inner))
        qkv_other.append(rep_over(qkv_pair[1]))
        down_late, grad_late, qkv_pair[1] = tie(list(zip(down_total, down_back)), grad_out, qkv_pair[1])
        down_grad = row_grads(inner, down_late, wide // 2)
        found = jnp.where(inner == 1, down_late[1][0][wide // 2:], down_late[1][1][wide // 2:])
        out_bias_grad = sums_of(found, cols)
        grad_rows = lax.dynamic_slice_in_dim(grad_late, place * own_rows, own_rows, 1)
        grad_rows = grad_rows.transpose(1, 0, 2).reshape(own_rows, D)
        qkv_other[0], down_grad, grad_rows, out_bias_grad = tie(
            qkv_other[0], down_grad, grad_rows, out_bias_grad
        )
        qkv_total = [plus_low(qkv_pair[0], qkv_other[0], needed=inner)]
        qkv_back = [rep_out(qkv_total[0])]
        norm_got_one, norm_got_two, qkv_total[0] = tie(norm_got_one, norm_got_two, qkv_total[0])
        norm_last_one = plus_low(norm_keep_one, norm_got_one, 1)
        norm_last_two = plus_low(norm_keep_two, norm_got_two, 1)
        up_back[1], norm_last_one, norm_last_two = tie(up_back[1], norm_last_one, norm_last_two)
        norm_last_one, norm_last_two = flip(norm_last_one, 4), flip(norm_last_two, 2)
        up_grad, gain_two_grad, shift_two_grad, sum_up = column_grads(
            inner, list(zip(up_total, up_back)), up_weight, ln2_gain, ln2_bias, wide // 2, 1, True
        )
        qkv_other[1], up_grad = tie(qkv_other[1], up_grad)
        qkv_total.append(plus_low(qkv_pair[1], qkv_other[1], needed=inner))
        qkv_back.append(rep_out(qkv_total[1]))
        out_other, qkv_back[0], norm_last_one, norm_last_two, last_one, last_two, qkv_total[1] = tie(
            out_other, qkv_back[0], norm_last_one, norm_last_two, last_one, last_two, qkv_total[1]
        )
        last_one, last_two = flip(last_one, 4), flip(last_two, 2)
        out_total = plus_low(out_pair, out_other, needed=inner)
        out_back = rep_out(out_total)
        norm_last_one, norm_last_two, out_total = tie(norm_last_one, norm_last_two, out_total)
        tokens_grad = token_grads(
            resid, grad_rows,
            [(norm_keep_one, norm_got_one, norm_last_one), (norm_keep_two, norm_got_two, norm_last_two)],
        )
        qkv_back, tokens_grad = tie(qkv_back, tokens_grad)
        qkv_grad, gain_one_grad, shift_one_grad, sum_qkv = column_grads(
            inner, list(zip(qkv_total, qkv_back)), qkv_weight, ln1_gain, ln1_bias, HD, 2, False, token
        )
        last_one, last_two, qkv_grad = tie(last_one, last_two, qkv_grad)
        out_given = out_blocks(
            tables[0], tables[1], own, [(keep_one, got_one, last_one), (keep_two, got_two, last_two)],
            out_bias.astype(f32) + down_bias.astype(f32),
        )
        out_back, out_given = tie(out_back, out_given)
        out_grad = row_grads(inner, [(out_total, out_back)])
    else:
        sums = jnp.concatenate([sum_mixed[0], sum_hidden[0]])
        sums, out_bias_grad = lax.psum((sums, sum_cot), "rep")
        sums = lax.all_gather(sums, "shard")
        sum_qkv = sums[:, :share_cols].reshape(HEADS, 3, HD).transpose(1, 0, 2).reshape(3 * D)
        sum_up = sums[:, share_cols:].reshape(FF)
        qkv_found, up_found = qkv_found[:, :cols], [found[:, :cols] for found in up_found]
        out_sum, qkv_sum, up_sum, down_sum = lax.psum(
            (token_dot(context, grad_out), qkv_found, jnp.concatenate(up_found, axis=2), jnp.concatenate(down_parts)), "rep"
        )
        terms = dot(context, out_w, 1, 0) + dot(active, down_w, 1, 0)
        terms = lax.dynamic_update_slice_in_dim(
            terms,
            lax.dynamic_slice_in_dim(terms, place * own_rows, own_rows, 0) + resid.astype(f32),
            place * own_rows,
            0,
        )
        out_own = lax.psum_scatter(terms.astype(bf16), "shard", scatter_dimension=1, tiled=True)
        out_own = out_own.astype(f32)
        terms = dot(mixed_grad, qkv_w, 1, 1) + dot(hidden_grad, up_w, 1, 1)
        normed_grad = lax.psum_scatter(terms.astype(bf16), "shard", scatter_dimension=0, tiled=True)
        normed_grad = normed_grad.astype(f32)
        grad_rows = lax.dynamic_slice_in_dim(grad_out, place * own_rows, own_rows, 1)
        grad_rows = grad_rows.transpose(1, 0, 2).reshape(own_rows, D)

        out_own = out_own + (out_bias.astype(f32) + down_bias.astype(f32))
        out_own = out_own.astype(bf16).reshape(shards, MB, own, BLK, cols)
        out_given = jnp.stack([out_own[piece_of[m], m, inner_of[m]] for m in range(MB)])
        mean_grad = jnp.mean(normed_grad, axis=-1, keepdims=True)
        mean_proj = jnp.mean(normed_grad * normed_own, axis=-1, keepdims=True)
        tokens_grad = inv_std * (normed_grad - mean_grad - normed_own * mean_proj)
        tokens_grad = (grad_rows.astype(f32) + tokens_grad).astype(bf16)
    tokens_grad = tokens_grad.reshape(MB, own, BLK, D)

    if not cube:
        def finish(sums, weight, gain, shift, total):
            sums = sums.astype(f32)
            grads = gain.astype(f32)[:, None] * sums + shift.astype(f32)[:, None] * total
            weight = weight.astype(f32)
            return grads, jnp.sum(weight * sums, axis=1), jnp.sum(weight * total, axis=1)

        qkv_rows = qkv_sum.reshape(HEADS, split, cols, share_cols).transpose(2, 0, 1, 3)
        qkv_rows = qkv_rows.reshape(cols, HEADS, 3, HD).transpose(0, 2, 1, 3).reshape(cols, 3 * D)
        up_rows = up_sum.transpose(1, 0, 2).reshape(cols, FF)
        qkv_grad, gain_one_grad, shift_one_grad = finish(
            qkv_rows, qkv_weight, ln1_gain, ln1_bias, sum_qkv
        )
        out_grad = out_sum.astype(f32)
        down_grad = down_sum.astype(f32)
        up_grad, gain_two_grad, shift_two_grad = finish(
            up_rows, up_weight, ln2_gain, ln2_bias, sum_up
        )

    qkv_bias_grad = lax.dynamic_slice_in_dim(sum_qkv, place * 3 * cols, 3 * cols)
    up_bias_grad = lax.dynamic_slice_in_dim(sum_up, place * wide, wide)
    return (
        out_given,
        tokens_grad,
        gain_one_grad.reshape(cols),
        shift_one_grad.reshape(cols),
        gain_two_grad.reshape(cols),
        shift_two_grad.reshape(cols),
        qkv_grad,
        qkv_bias_grad,
        out_grad,
        out_bias_grad,
        up_grad,
        up_bias_grad,
        down_grad,
        out_bias_grad,
    )


def solution(mesh):
    in_specs = (
        P(None, ("rep", "shard"), None, None),
        P(None, "rep", None, "shard"),
        P(None, "rep", None),
        P(None, "rep", None),
        P(None, "rep", None),
        P("shard"),
        P("shard"),
        P("shard"),
        P("shard"),
        P("shard", None),
        P("shard"),
        P("shard", None),
        P("shard"),
        P("shard", None),
        P("shard"),
        P("shard", None),
        P("shard"),
    )
    out_specs = (
        P(None, "rep", None, "shard"),
        P(None, ("rep", "shard"), None, None),
        P("shard"),
        P("shard"),
        P("shard"),
        P("shard"),
        P("shard", None),
        P("shard"),
        P("shard", None),
        P("shard"),
        P("shard", None),
        P("shard"),
        P("shard", None),
        P("shard"),
    )
    return jax.shard_map(local, mesh=mesh, in_specs=in_specs, out_specs=out_specs, check_vma=False)
```

```python
import jax
import jax.numpy as jnp
from jax import lax
from jax.experimental import pallas as pl
from jax.experimental.pallas import tpu as pltpu
from jax.sharding import PartitionSpec as P

D = 2048
HEADS = 8
HD = 256
ROT = 64
FF = 8192
BLK = 128
SEQ_MOST = 8
MB = 2
EPS = 1e-05
SCALE = HD ** (-0.5)

bf16 = jnp.bfloat16
f32 = jnp.float32

ORDER = (0, 2, 4, 6, 1, 3, 5, 7)


def dot(a, b, ca, cb):
    return lax.dot_general(a, b, (((ca,), (cb,)), ((), ())), preferred_element_type=f32)


def flip(value, bit):
    return lax.ppermute(value, "shard", [(i, i ^ bit) for i in range(8)])


def tie(*values):
    return lax.optimization_barrier(values)


def plus(a, b):
    return a.astype(f32) + b.astype(f32)


def rep_move(value, pairs):
    return lax.ppermute(value, "rep", pairs) if lax.axis_size("rep") == 4 else value


def rep_in(value):
    return rep_move(value, [(0, 1), (3, 2)])


def rep_over(value):
    return rep_move(value, [(1, 2), (2, 1)])


def rep_out(value):
    return rep_move(value, [(1, 0), (2, 3)])


def rotary_tables():
    half = ROT // 2
    freqs = 10000.0 ** (-2.0 * jnp.arange(half, dtype=f32) / ROT)
    angles = jnp.arange(SEQ_MOST * BLK, dtype=f32)[:, None] * freqs[None, :]
    rest = 128 - ROT
    cosine = jnp.concatenate(
        [jnp.cos(angles), jnp.cos(angles), jnp.ones((SEQ_MOST * BLK, rest), f32)], axis=-1
    )
    sine = jnp.concatenate(
        [-jnp.sin(angles), jnp.sin(angles), jnp.zeros((SEQ_MOST * BLK, rest), f32)], axis=-1
    )
    return cosine.reshape(SEQ_MOST, BLK, 128), sine.reshape(SEQ_MOST, BLK, 128)


def params_of(vmem=52):
    return pltpu.CompilerParams(vmem_limit_bytes=vmem * 2**20)


def cost(us):
    return pl.CostEstimate(flops=int(us * 1.1e9) + 1024, bytes_accessed=1024, transcendentals=0)


def tick(token, *arrays):
    def body(*refs):
        refs[-1][...] = refs[0][...]

    return pl.pallas_call(
        body,
        in_specs=[pl.BlockSpec(memory_space=pltpu.VMEM)] + [pl.BlockSpec(memory_space=pl.ANY)] * len(arrays),
        out_specs=pl.BlockSpec(memory_space=pltpu.VMEM),
        out_shape=jax.ShapeDtypeStruct(token.shape, token.dtype),
        compiler_params=params_of(16), cost_estimate=cost(2000),
    )(token, *arrays)


def spec(shape, index):
    return pl.BlockSpec(shape, index)


def attention_kernel(
    piece_of, inner_of, first_of, end_of,
    qkv_ref, grad_ref, cos_ref, sin_ref,
    ctx_ref, out_ref, sum_ref,
    q_buf, k_buf, v_buf, g_buf, dk_buf, dv_buf,
):
    m = pl.program_id(0)
    blocks = piece_of.shape[1]
    lane = lax.broadcasted_iota(jnp.int32, (BLK, 128), 1)
    tile = 2 * BLK

    def turned(x):
        return jnp.where(lane < ROT // 2, pltpu.roll(x, 128 - ROT // 2, 1), pltpu.roll(x, ROT // 2, 1))

    def store_part(p, i, start, value):
        low = value.astype(bf16)
        out_ref[p, 0, i, :, start:start + value.shape[1]] = low
        sum_ref[0, 0:1, start:start + value.shape[1]] += jnp.sum(low.astype(f32), axis=0, keepdims=True)

    def block_rows(g):
        return pl.ds(pl.multiple_of(g * BLK, BLK), BLK)

    def load(g, carry):
        p, i = piece_of[m, g], inner_of[m, g]
        at = g - first_of[m, g]
        cosine, sine = cos_ref[at], sin_ref[at]
        rows = block_rows(g)
        for buf, start in ((q_buf, 0), (k_buf, HD)):
            front = qkv_ref[p, 0, i, :, start:start + 128]
            buf[rows, 0:128] = (front * cosine + turned(front) * sine).astype(bf16)
            buf[rows, 128:HD] = qkv_ref[p, 0, i, :, start + 128:start + HD].astype(bf16)
        v_buf[rows, :] = qkv_ref[p, 0, i, :, 2 * HD:].astype(bf16)
        g_buf[rows, :] = grad_ref[p, 0, i]
        return carry

    lax.fori_loop(0, blocks, load, 0, unroll=4)
    for buf in (q_buf, k_buf, v_buf, g_buf):
        buf[blocks * BLK:, :] = jnp.zeros((BLK, HD), bf16)
    sum_ref[...] = jnp.zeros(sum_ref.shape, f32)
    dk_buf[...] = jnp.zeros(dk_buf.shape, f32)
    dv_buf[...] = jnp.zeros(dv_buf.shape, f32)

    def attend(g, span):
        first = first_of[m, g]
        rows = pl.ds(pl.multiple_of(g * BLK, BLK), tile)
        keys = pl.ds(pl.multiple_of(first * BLK, BLK), span)
        query, grad = q_buf[rows, :], g_buf[rows, :]
        key, value = k_buf[keys, :], v_buf[keys, :]
        after_g = jnp.minimum(g + 1, blocks - 1)
        second = (g + 1 < blocks) & (first_of[m, after_g] == first)
        scores = dot(query, key, 1, 1) * SCALE
        key_tok = first * BLK + lax.broadcasted_iota(jnp.int32, (tile, span), 1)
        query_tok = g * BLK + lax.broadcasted_iota(jnp.int32, (tile, span), 0)
        allowed = (key_tok <= query_tok) & (key_tok < end_of[m, g])
        scores = jnp.where(allowed, scores, -jnp.inf)
        exponent = jnp.exp(scores - jnp.max(scores, axis=1, keepdims=True))
        scale = 1.0 / jnp.sum(exponent, axis=1, keepdims=True)
        last_row = jnp.where(second, tile, BLK)
        row = lax.broadcasted_iota(jnp.int32, (tile, 1), 0)
        prob = exponent * jnp.where(row < last_row, scale, 0.0)
        prob_low = prob.astype(bf16)
        ctx = dot(prob_low, value, 1, 0).astype(bf16)
        prob_grad = dot(grad, value, 1, 1)
        delta = jnp.sum(prob * prob_grad, axis=1, keepdims=True)
        score_grad = (prob * (prob_grad - delta)).astype(bf16)
        dk_buf[keys, :] += dot(score_grad, query, 0, 0)
        dv_buf[keys, :] += dot(prob_low, grad, 0, 0)
        query_grad = dot(score_grad, key, 1, 0) * SCALE

        def put(block, lo):
            p, i = piece_of[m, block], inner_of[m, block]
            at = block - first
            ctx_ref[p, 0, i] = ctx[lo:lo + BLK]
            front = query_grad[lo:lo + BLK, 0:128]
            store_part(p, i, 0, front * cos_ref[at] - turned(front) * sin_ref[at])
            store_part(p, i, 128, query_grad[lo:lo + BLK, 128:])

        put(g, 0)
        pl.when(second)(lambda: put(after_g, BLK))

    def one_block(g, carry):
        at = g - first_of[m, g]
        for count in range(SEQ_MOST // 2):
            pl.when(at == 2 * count)(lambda: attend(g, (count + 1) * tile))
        return carry

    lax.fori_loop(0, blocks, one_block, 0)

    def store(g, carry):
        p, i = piece_of[m, g], inner_of[m, g]
        at = g - first_of[m, g]
        rows = block_rows(g)
        front = dk_buf[rows, 0:128] * SCALE
        store_part(p, i, HD, front * cos_ref[at] - turned(front) * sin_ref[at])
        store_part(p, i, HD + 128, dk_buf[rows, 128:HD] * SCALE)
        store_part(p, i, 2 * HD, dv_buf[rows, :])
        return carry

    lax.fori_loop(0, blocks, store, 0, unroll=4)


def attention(tables, qkv, grad, cosine, sine):
    pieces, _, own = qkv.shape[:3]
    blocks = tables[0].shape[1]

    def part(width):
        return pl.BlockSpec((pieces, 1, own, BLK, width), lambda m, *_: (0, m, 0, 0, 0))

    whole = pl.BlockSpec((SEQ_MOST, BLK, 128), lambda m, *_: (0, 0, 0))
    rows = (blocks + 1) * BLK
    return pl.pallas_call(
        attention_kernel,
        grid_spec=pltpu.PrefetchScalarGridSpec(
            num_scalar_prefetch=4,
            grid=(MB,),
            in_specs=[part(3 * HD), part(HD), whole, whole],
            out_specs=[part(HD), part(3 * HD), spec((1, 8, 3 * HD), lambda m, *_: (m, 0, 0))],
            scratch_shapes=[
                pltpu.VMEM((rows, HD), bf16),
                pltpu.VMEM((rows, HD), bf16),
                pltpu.VMEM((rows, HD), bf16),
                pltpu.VMEM((rows, HD), bf16),
                pltpu.VMEM((rows, HD), f32),
                pltpu.VMEM((rows, HD), f32),
            ],
        ),
        out_shape=[
            jax.ShapeDtypeStruct((pieces, MB, own, BLK, HD), bf16),
            jax.ShapeDtypeStruct((pieces, MB, own, BLK, 3 * HD), bf16),
            jax.ShapeDtypeStruct((MB, 8, 3 * HD), f32),
        ],
        compiler_params=params_of(),
        cost_estimate=cost(0),
    )(*tables, qkv, grad, cosine, sine)


def plus_low(a, b, index=None, needed=None):
    shape = a.shape if index is None else a.shape[1:]
    if index is None:
        a, b, index = a[None], b[None], 0
    if needed is None:
        needed = jnp.ones((1,), jnp.int32)
    a, b = [x.reshape(x.shape[0], -1, x.shape[-1]) for x in (a, b)]
    rows, cols = a.shape[1:]
    steps = next(n for n in (2, 3, 1) if rows % (16 * n) == 0)
    block = spec((1, rows // steps, cols), lambda i, needed_ref: (index, i * needed_ref[0], 0))

    def body(needed_ref, a_ref, b_ref, out_ref):
        @pl.when((needed_ref[0] == 1) | (pl.program_id(0) == 0))
        def _():
            out_ref[...] = plus(a_ref[0], b_ref[0]).astype(bf16)

    return pl.pallas_call(
        body,
        grid_spec=pltpu.PrefetchScalarGridSpec(
            num_scalar_prefetch=1, grid=(steps,), in_specs=[block, block],
            out_specs=spec((rows // steps, cols), lambda i, needed_ref: (i * needed_ref[0], 0)),
        ),
        out_shape=jax.ShapeDtypeStruct((rows, cols), bf16),
        compiler_params=params_of(32), cost_estimate=cost(0),
    )(needed, a, b).reshape(shape)


def out_terms(owners, place, context, active, out_w, down_w, resid, came=None):
    rows, inner = active.shape
    n = resid.shape[0]
    cols = D // 8
    first = 4 if came is None else 0

    def terms(place_ref, refs):
        ctx, act = refs[0][...], refs[1][...]
        own = pl.program_id(0) == place_ref[0]
        return [
            dot(ctx, refs[2 + b][...], 1, 0)
            + dot(act, refs[6 + b][...], 1, 0)
            + jnp.where(own, refs[10 + b][...].astype(f32), 0.0)
            for b in range(4)
        ]

    def odd_body(owners_ref, place_ref, *refs):
        for b, part in enumerate(terms(place_ref, refs)):
            refs[14][b] = part.astype(bf16)

    def even_body(owners_ref, place_ref, *refs):
        got, send_one, keep_one, send_two, keep_two = refs[14:]
        parts = [(p + got[b].astype(f32)).astype(bf16) for b, p in enumerate(terms(place_ref, refs))]

        @pl.when(pl.program_id(0) < 4)
        def _():
            send_one[0], send_one[1] = parts[1], parts[3]
            keep_one[0], keep_one[1] = parts[0], parts[2]

        @pl.when(pl.program_id(0) >= 4)
        def _():
            send_two[0], send_two[1] = parts[2], parts[3]
            keep_two[0], keep_two[1] = parts[0], parts[1]

    def columns(height, b):
        return spec((height, cols), lambda i, o, p: (0, o[first + b]))

    in_specs = [
        spec((n, context.shape[1]), lambda i, o, p: (i, 0)),
        spec((n, inner), lambda i, o, p: (i, 0)),
        *[columns(context.shape[1], b) for b in range(4)],
        *[columns(inner, b) for b in range(4)],
        *[columns(n, b) for b in range(4)],
    ]
    args = [context, active, *[out_w] * 4, *[down_w] * 4, *[resid] * 4]
    if came is None:
        body = odd_body
        out_specs = spec((4, n, cols), lambda i, o, p: (0, i, 0))
        out_shape = jax.ShapeDtypeStruct((4, rows, cols), bf16)
    else:
        body = even_body
        in_specs.append(spec((4, n, cols), lambda i, o, p: (0, i, 0)))
        args.append(came)
        low = spec((2, n, cols), lambda i, o, p: (0, jnp.minimum(i, 3), 0))
        high = spec((2, n, cols), lambda i, o, p: (0, jnp.maximum(i - 4, 0), 0))
        out_specs = [low, low, high, high]
        out_shape = [jax.ShapeDtypeStruct((2, rows // 2, cols), bf16)] * 4
    return pl.pallas_call(
        body,
        grid_spec=pltpu.PrefetchScalarGridSpec(
            num_scalar_prefetch=2, grid=(8,), in_specs=in_specs, out_specs=out_specs
        ),
        out_shape=out_shape, compiler_params=params_of(), cost_estimate=cost(0),
    )(owners, place.reshape(1), *args)


def norm_terms(owners, mixed_grad, hidden_grad, qkv_w, up_w, came=None):
    rows = mixed_grad.shape[0]
    n = rows // 16
    first = 4 if came is None else 0

    def terms(refs):
        one, two, w_one, w_two = refs
        return dot(one[...], w_one[...], 1, 1) + dot(two[...], w_two[...], 1, 1)

    def odd_body(owners_ref, *refs):
        refs[4][0, 0] = terms(refs[:4]).astype(bf16)

    def even_body(owners_ref, *refs):
        got, send_one, keep_one, send_two, keep_two = refs[4:]
        sums = (terms(refs[:4]) + got[0, 0].astype(f32)).astype(bf16)
        i = pl.program_id(0)
        for ref, steps in (
            (keep_one, (0, 4)), (send_one, (2, 6)), (keep_two, (1, 3)), (send_two, (5, 7)),
        ):
            @pl.when((i == steps[0]) | (i == steps[1]))
            def _():
                ref[0] = sums

    def own_rows(i, o):
        return (o[first + i // 2] * 2 + i % 2, 0)

    in_specs = [
        spec((n, mixed_grad.shape[1]), own_rows),
        spec((n, hidden_grad.shape[1]), own_rows),
        spec(qkv_w.shape, lambda i, o: (0, 0)),
        spec(up_w.shape, lambda i, o: (0, 0)),
    ]
    args = [mixed_grad, hidden_grad, qkv_w, up_w]
    if came is None:
        body = odd_body
        out_specs = spec((1, 1, n, D), lambda i, o: (i // 2, i % 2, 0, 0))
        out_shape = jax.ShapeDtypeStruct((4, 2, n, D), bf16)
    else:
        body = even_body
        in_specs.append(spec((1, 1, n, D), lambda i, o: (i // 2, i % 2, 0, 0)))
        args.append(came)
        out_specs = [
            spec((1, n, D), lambda i, o: (i // 4, 0, 0)),
            spec((1, n, D), lambda i, o: (i // 4, 0, 0)),
            spec((1, n, D), lambda i, o: (jnp.maximum(i - 4, 0) // 2, 0, 0)),
            spec((1, n, D), lambda i, o: (jnp.minimum(i // 2, 1), 0, 0)),
        ]
        out_shape = [jax.ShapeDtypeStruct((2, n, D), bf16)] * 4
    return pl.pallas_call(
        body,
        grid_spec=pltpu.PrefetchScalarGridSpec(
            num_scalar_prefetch=1, grid=(8,), in_specs=in_specs, out_specs=out_specs
        ),
        out_shape=out_shape, compiler_params=params_of(), cost_estimate=cost(0),
    )(owners, *args)


def token_dot(left, right, part=0, parts=1, extra=None):
    rows, width = left.shape[0], left.shape[1] // parts
    blocks, _, cols = right.shape
    step = 512 // cols
    more = [] if extra is None else [extra]
    total = width + sum(m.shape[0] for m in more)

    def body(left_ref, right_ref, *refs):
        out_ref = refs[-1]
        for b in range(step):
            at = slice(b * cols, (b + 1) * cols)
            out_ref[0:width, at] = dot(left_ref[...], right_ref[b], 0, 0).astype(bf16)
        if more:
            out_ref[width:, :] = refs[0][...]

    return pl.pallas_call(
        body, grid=(blocks // step,),
        in_specs=[
            spec((rows, width), lambda i: (0, part)),
            spec((step, rows, cols), lambda i: (i, 0, 0)),
        ] + [spec((m.shape[0], step * cols), lambda i: (0, i)) for m in more],
        out_specs=spec((total, step * cols), lambda i: (0, i)),
        out_shape=jax.ShapeDtypeStruct((total, blocks * cols), bf16),
        compiler_params=params_of(56), cost_estimate=cost(0),
    )(left, right, *more)


EXTRA = 16


def normed_dot(spot, shards, normed, right, sums, part=0, parts=1):
    rows, tile = normed.shape[0], 512
    cols, width = D // shards, right.shape[1] // parts
    per = tile // cols

    def body(spot_ref, left_ref, right_ref, sum_ref, out_ref):
        sums = dot(left_ref[...], right_ref[...], 0, 0).astype(bf16)
        high = sum_ref[...]
        first = high.astype(bf16).astype(f32)
        second = (high - first).astype(bf16).astype(f32)
        third = high - first - second
        row = lax.broadcasted_iota(jnp.int32, (EXTRA, width), 0) - 3 * spot_ref[0]
        extra = jnp.where(row == 0, first, jnp.where(row == 1, second, jnp.where(row == 2, third, 0.0)))
        for b in range(per):
            out_ref[b, 0:cols, :] = sums[b * cols:(b + 1) * cols]
            out_ref[b, cols:, :] = extra.astype(bf16)

    return pl.pallas_call(
        body,
        grid_spec=pltpu.PrefetchScalarGridSpec(
            num_scalar_prefetch=1, grid=(D // tile,),
            in_specs=[
                spec((rows, tile), lambda i, z: (0, i)),
                spec((rows, width), lambda i, z: (0, part)),
                spec((1, width), lambda i, z: (0, part)),
            ],
            out_specs=spec((per, cols + EXTRA, width), lambda i, z: (i, 0, 0)),
        ),
        out_shape=jax.ShapeDtypeStruct((shards, cols + EXTRA, width), bf16),
        compiler_params=params_of(56), cost_estimate=cost(0),
    )(spot, normed, right, sums)


def whole_rows(ref):
    return jnp.concatenate([ref[b] for b in range(ref.shape[0])], axis=1)


def out_blocks(piece_of, inner_of, own, parts, bias):
    blocks = piece_of.shape[1]
    half, cols = parts[0][2].shape

    def body(piece_ref, inner_ref, *refs):
        bias_ref, out_ref, all_rows = refs[6:]
        m = pl.program_id(0)

        @pl.when(m == 0)
        def _():
            for h in range(2):
                keep, came, last = refs[3 * h:3 * h + 3]
                sums = plus(keep[0], came[0]) + last[...].astype(f32) + bias_ref[...]
                all_rows[h * half:(h + 1) * half, :] = sums.astype(bf16)

        def one(g, carry):
            row = ((piece_ref[m, g] * MB + m) * own + inner_ref[m, g]) * BLK
            out_ref[0, g] = all_rows[pl.ds(pl.multiple_of(row, BLK), BLK), :]
            return carry

        lax.fori_loop(0, blocks, one, 0)

    first = spec((1, half, cols), lambda m, *_: (0, 0, 0))
    whole = spec((half, cols), lambda m, *_: (0, 0))
    return pl.pallas_call(
        body,
        grid_spec=pltpu.PrefetchScalarGridSpec(
            num_scalar_prefetch=2, grid=(MB,),
            in_specs=[first, first, whole] * 2 + [spec((1, cols), lambda m, *_: (0, 0))],
            out_specs=spec((1, blocks, BLK, cols), lambda m, *_: (m, 0, 0, 0)),
            scratch_shapes=[pltpu.VMEM((2 * half, cols), bf16)],
        ),
        out_shape=jax.ShapeDtypeStruct((MB, blocks, BLK, cols), bf16),
        compiler_params=params_of(), cost_estimate=cost(0),
    )(piece_of, inner_of, *parts[0], *parts[1], bias[None])


def token_grads(tokens, grad_rows, parts):
    rows = tokens.shape[0]
    n = rows // 4

    def body(tokens_ref, grad_ref, *refs):
        out_ref = refs[6]
        x = tokens_ref[...].astype(f32)
        center = x - jnp.mean(x, axis=1, keepdims=True)
        inv_std = lax.rsqrt(jnp.mean(center * center, axis=1, keepdims=True) + EPS)
        normed = center * inv_std

        def finish(keep, came, last):
            grad = plus(keep[0], came[0]) + last[...].astype(f32)
            mean = jnp.mean(grad, axis=1, keepdims=True)
            proj = jnp.mean(grad * normed, axis=1, keepdims=True)
            grad = inv_std * (grad - mean - normed * proj)
            out_ref[...] = (grad_ref[...].astype(f32) + grad).astype(bf16)

        pl.when(pl.program_id(0) < 2)(lambda: finish(*refs[0:3]))
        pl.when(pl.program_id(0) >= 2)(lambda: finish(*refs[3:6]))

    own = spec((n, D), lambda i: (i, 0))
    in_specs = [own, own]
    for at in (lambda i: jnp.minimum(i, 1), lambda i: jnp.maximum(i - 2, 0)):
        first = spec((1, n, D), lambda i, at=at: (0, at(i), 0))
        in_specs += [first, first, spec((n, D), lambda i, at=at: (at(i), 0))]
    return pl.pallas_call(
        body, grid=(4,), in_specs=in_specs, out_specs=own,
        out_shape=jax.ShapeDtypeStruct((rows, D), bf16),
        compiler_params=params_of(), cost_estimate=cost(0),
    )(tokens, grad_rows, *parts[0], *parts[1])


def sum_rows(vector, spot):
    thirds, left = [], vector
    for _ in range(3):
        thirds.append(lax.reduce_precision(left, 8, 7))
        left = left - thirds[-1]
    mine = jnp.arange(4)[:, None, None] == spot
    values = jnp.where(mine, jnp.stack(thirds)[None], 0.0).reshape(-1)
    return jnp.pad(values, (0, 16 * D - values.shape[0])).reshape(16, D).astype(bf16)


def sums_of(found, size):
    return jnp.sum(found.astype(f32).reshape(-1)[:12 * size].reshape(12, size), axis=0)


def hidden_back(grad_out, down_w, slope):
    rows, wide = slope.shape
    n = rows // 8

    def body(grad_ref, w_ref, slope_ref, out_ref, sum_ref):
        active_grad = dot(whole_rows(grad_ref), w_ref[...], 1, 1).astype(bf16).astype(f32)
        value = (active_grad * slope_ref[...]).astype(bf16)
        out_ref[...] = value
        total = jnp.sum(value.astype(f32), axis=0, keepdims=True)

        @pl.when(pl.program_id(0) == 0)
        def _():
            sum_ref[...] = total

        @pl.when(pl.program_id(0) > 0)
        def _():
            sum_ref[...] += total

    return pl.pallas_call(
        body, grid=(8,),
        in_specs=[
            spec((grad_out.shape[0], n, grad_out.shape[2]), lambda i: (0, i, 0)),
            spec((wide, D), lambda i: (0, 0)),
            spec((n, wide), lambda i: (i, 0)),
        ],
        out_specs=[spec((n, wide), lambda i: (i, 0)), spec((1, wide), lambda i: (0, 0))],
        out_shape=[
            jax.ShapeDtypeStruct((rows, wide), bf16), jax.ShapeDtypeStruct((1, wide), f32),
        ],
        compiler_params=params_of(), cost_estimate=cost(0),
    )(grad_out, down_w, slope)


def head_back(grad_out, out_w):
    blocks, rows, cols = grad_out.shape
    n = rows // 8

    def body(grad_ref, w_ref, out_ref):
        out_ref[...] = dot(whole_rows(grad_ref), w_ref[...], 1, 1).astype(bf16)

    return pl.pallas_call(
        body, grid=(8,),
        in_specs=[
            spec((blocks, n, cols), lambda i: (0, i, 0)),
            spec((HD, D), lambda i: (0, 0)),
        ],
        out_specs=spec((n, HD), lambda i: (i, 0)),
        out_shape=jax.ShapeDtypeStruct((rows, HD), bf16),
        compiler_params=params_of(), cost_estimate=cost(0),
    )(grad_out, out_w)


def row_grads(inner, chunks, count=None):
    rows = [count or c[0].shape[0] for c in chunks]
    total, cols = sum(rows), 512

    def body(inner_ref, *refs):
        at = 0
        for c, n in enumerate(rows):
            one, two = refs[2 * c][...].astype(f32), refs[2 * c + 1][...].astype(f32)
            refs[-1][at:at + n, :] = jnp.where(inner_ref[0] == 1, one, two)
            at += n

    return pl.pallas_call(
        body,
        grid_spec=pltpu.PrefetchScalarGridSpec(
            num_scalar_prefetch=1, grid=(D // cols,),
            in_specs=[spec((n, cols), lambda i, *_: (0, i)) for n in rows for _ in range(2)],
            out_specs=spec((total, cols), lambda i, *_: (0, i)),
        ),
        out_shape=jax.ShapeDtypeStruct((total, D), f32),
        compiler_params=params_of(32), cost_estimate=cost(0),
    )(inner, *[a for c in chunks for a in c])


def column_grads(inner, chunks, weight, gain, shift, run, step, by_run, token=None):
    rows, each = weight.shape[0], len(chunks[0])
    if by_run:
        groups, per = len(chunks), chunks[0][0].shape[0] // step
        steps = per
    else:
        groups, per = chunks[0][0].shape[2] // run, chunks[0][0].shape[0] // step
        steps = per * len(chunks)

    tokens = [] if token is None else [token]

    def body(inner_ref, *refs):
        pairs, refs = refs[:each * len(chunks)], refs[each * len(chunks) + len(tokens):]
        w_ref, gain_ref, shift_ref, grads, gain_out, shift_out, t_out = refs
        i, k = pl.program_id(0), pl.program_id(1)

        @pl.when((i == 0) & (k == 0))
        def _():
            gain_out[...] = jnp.zeros_like(gain_out)
            shift_out[...] = jnp.zeros_like(shift_out)

        for c in range(len(chunks)):
            @pl.when((k if by_run else i // per) == c)
            def _():
                for j in range(step):
                    value = pairs[each * c][j].astype(f32)
                    if each == 2:
                        other = pairs[2 * c + 1][j].astype(f32)
                        value = jnp.where(inner_ref[0] == 1, value, other)
                    at = slice(j * run, (j + 1) * run)
                    t = jnp.sum(value[rows:], axis=0, keepdims=True)
                    value, w = value[:rows], w_ref[:, at].astype(f32)
                    t_out[:, at] = t
                    grads[:, at] = gain_ref[...] * value + shift_ref[...] * t
                    for out, terms in ((gain_out, w * value), (shift_out, w * t)):
                        out[...] += sum(terms[:, lo:lo + 128] for lo in range(0, run, 128))

    def part_index(c):
        if by_run:
            return lambda i, k, *_: (i, 0, 0)
        return lambda i, k, *_: (jnp.clip(i - c * per, 0, per - 1), 0, k)

    def columns(i, k, *_):
        return (0, i * groups + k if by_run else k * steps + i)

    column = spec((rows, 1), lambda i, k, *_: (0, 0))
    wide_column = spec((rows, 128), lambda i, k, *_: (0, 0))
    grads, gain_grad, shift_grad, totals = pl.pallas_call(
        body,
        grid_spec=pltpu.PrefetchScalarGridSpec(
            num_scalar_prefetch=1, grid=(steps, groups),
            in_specs=[spec((step, rows + EXTRA, run), part_index(c)) for c in range(len(chunks)) for _ in range(each)]
            + [pl.BlockSpec(memory_space=pl.ANY)] * len(tokens)
            + [spec((rows, step * run), columns), column, column],
            out_specs=[
                spec((rows, step * run), columns), wide_column, wide_column,
                spec((1, step * run), columns),
            ],
        ),
        out_shape=[
            jax.ShapeDtypeStruct(weight.shape, f32),
            jax.ShapeDtypeStruct((rows, 128), f32),
            jax.ShapeDtypeStruct((rows, 128), f32),
            jax.ShapeDtypeStruct((1, weight.shape[1]), f32),
        ],
        compiler_params=params_of(32), cost_estimate=cost(0),
    )(
        inner, *[a for c in chunks for a in c], *tokens, weight,
        gain.astype(f32)[:, None], shift.astype(f32)[:, None],
    )
    return grads, jnp.sum(gain_grad, axis=1), jnp.sum(shift_grad, axis=1), totals[0]


def local(
    tokens, cotangent, seq_blocks, seq_pad, deal_order,
    ln1_gain, ln1_bias, ln2_gain, ln2_bias,
    qkv_weight, qkv_bias, out_weight, out_bias, up_weight, up_bias, down_weight, down_bias,
):
    shards = lax.axis_size("shard")
    place = lax.axis_index("shard")
    cube = shards == 8 and lax.axis_size("rep") == 4
    own = tokens.shape[1]
    blocks = deal_order.shape[2]
    own_rows = MB * own * BLK
    rows = shards * own_rows
    cols = D // shards
    wide = FF // shards
    split = shards // HEADS
    head, share = place // split, place % split
    share_cols = 3 * HD // split

    if cube:
        owners = jnp.bitwise_xor(place, jnp.array(ORDER, jnp.int32))
    deal = deal_order[:, 0, :]
    counts = seq_blocks[:, 0, :]
    pads = seq_pad[:, 0, :]
    ids = jnp.arange(blocks, dtype=jnp.int32)
    inverse = jnp.sum(
        jnp.where(deal[:, None, :] == ids[None, :, None], ids[None, None, :], 0), axis=-1
    )
    piece_of, inner_of = inverse // own, inverse % own
    ends = jnp.cumsum(counts, axis=1)
    starts = ends - counts
    inside = (ids[None, :, None] >= starts[:, None, :]) & (ids[None, :, None] < ends[:, None, :])
    first_of = jnp.sum(jnp.where(inside, starts[:, None, :], 0), axis=-1)
    valid = jnp.sum(jnp.where(inside, (counts * BLK - pads)[:, None, :], 0), axis=-1)
    tables = [t.astype(jnp.int32) for t in (piece_of, inner_of, first_of, first_of * BLK + valid)]
    given = deal.reshape(MB, shards, own)

    cot_own = jnp.stack([cotangent[m][given[m]] for m in range(MB)], axis=1)

    def swap(value):
        return lax.all_to_all(value, "shard", split_axis=0, concat_axis=0, tiled=True)

    token = jnp.zeros((8, 128), f32)

    def gate(*arrays):
        nonlocal token
        if cube:
            token = tick(token, *arrays)

    def late(value):
        nonlocal token
        if cube:
            value, token = tie(value, token)
        return value

    flat = tokens.reshape(own_rows, D).astype(f32)
    center = flat - jnp.mean(flat, axis=-1, keepdims=True)
    inv_std = lax.rsqrt(jnp.mean(center * center, axis=-1, keepdims=True) + EPS)
    normed_own = center * inv_std
    normed_low = normed_own.astype(bf16)
    normed = lax.all_gather(normed_low, "shard", axis=0, tiled=True)
    gate(normed_low)

    shares = lax.axis_size("rep") if cube else 1
    part_rows = cols // shares
    spot = lax.axis_index("rep") if cube else 0
    up_late, qkv_late = late((up_weight, qkv_weight))

    def part_of(array):
        return lax.dynamic_slice_in_dim(array, spot * part_rows, part_rows, 0).astype(f32)

    def with_shift(weight, gain, shift):
        high = lax.reduce_precision(shift, 8, 7)
        low = lax.reduce_precision(shift - high, 8, 7)
        tail = jnp.zeros((14, shift.shape[0]), bf16)
        scaled = (part_of(weight) * part_of(gain)[:, None]).astype(bf16)
        return jnp.concatenate([scaled, high.astype(bf16)[None], low.astype(bf16)[None], tail], axis=0)

    shift_up = jnp.sum(up_late.astype(f32) * ln2_bias.astype(f32)[:, None], axis=0)
    shift_qkv = jnp.sum(qkv_late.astype(f32) * ln1_bias.astype(f32)[:, None], axis=0)
    own_bias = lax.dynamic_slice_in_dim(shift_qkv, place * 3 * cols, 3 * cols) + qkv_bias.astype(f32)
    shift_qkv = lax.dynamic_update_slice_in_dim(shift_qkv, own_bias, place * 3 * cols, 0)
    sent_rows = part_rows + 16
    up_send = with_shift(up_late, ln2_gain, shift_up).reshape(sent_rows, shards, wide).transpose(1, 0, 2)
    qkv_send = with_shift(qkv_late, ln1_gain, shift_qkv).reshape(sent_rows, 3, HEADS, HD)
    qkv_send = qkv_send.transpose(2, 0, 1, 3).reshape(HEADS, sent_rows, 3 * HD)
    if split > 1:
        qkv_send = jnp.repeat(qkv_send, split, axis=0)
    found = swap(jnp.concatenate([up_send, qkv_send], axis=2))
    cot_late = late(cot_own)
    grad_out = lax.all_gather(cot_late.reshape(rows, cols), "shard", axis=0)
    gate(up_send, qkv_send, cot_late)
    found = late(found)
    biases = jnp.sum(found[:, part_rows:part_rows + 2].astype(f32), axis=(0, 1))

    def exchange(part):
        return [part] + [
            lax.ppermute(part, "rep", [(i, (i + k) % shares) for i in range(shares)])
            for k in range(1, shares)
        ]

    def whole(parts):
        if shares == 1:
            return parts[0].reshape(D, parts[0].shape[-1])
        width = parts[0].shape[-1]
        array = jnp.zeros((shards, shares, part_rows, width), bf16)
        for k, part in enumerate(parts):
            at = lax.rem(spot - k + shares, shares)
            array = lax.dynamic_update_slice(array, part[:, None], (0, at, 0, 0))
        return array.reshape(D, width)

    up_parts = exchange(found[:, :part_rows, :wide])
    normed, up_parts, biases = tie(normed, up_parts, biases)
    up_w = whole(up_parts)
    found, up_w = tie(found, up_w)
    qkv_parts = exchange(found[:, :part_rows, wide:])
    bias_up, bias_qkv = biases[:wide] + up_bias.astype(f32), biases[wide:]
    out_w, down_w, resid = out_weight, down_weight, tokens.reshape(own_rows, D)

    hidden = dot(normed, up_w, 1, 0) + bias_up
    cdf = 0.5 + 0.5 * lax.erf(hidden * (0.5 ** 0.5))
    density = jnp.exp(-0.5 * hidden * hidden) * 0.3989422804014327
    active = (hidden * cdf).astype(bf16)
    slope = cdf + hidden * density
    grad_out, active = tie(grad_out, active)

    where_rep = jnp.asarray(spot, jnp.int32).reshape(1)
    inner = ((where_rep == 1) | (where_rep == 2)).astype(jnp.int32)

    down_parts = [token_dot(active, grad_out, 0, 2)]
    down_came = [rep_in(down_parts[0])]
    gate(down_parts[0])
    hidden_grad, sum_hidden = hidden_back(late(grad_out), down_w, slope)
    sum_cot = jnp.sum(cot_own, axis=tuple(range(cot_own.ndim - 1)), dtype=f32)
    extra = sum_rows(sum_cot, spot) if cube else None
    down_parts.append(token_dot(active, grad_out, 1, 2, extra))
    hidden_grad, down_parts[1] = tie(hidden_grad, down_parts[1])
    up_terms = [normed_dot(where_rep, shards, normed, hidden_grad, sum_hidden, 0, 2)]
    up_found = [swap(up_terms[0])]
    down_came[0], up_terms[0] = tie(down_came[0], up_terms[0])
    down_pair = [plus_low(down_parts[0], down_came[0], needed=inner)]
    down_other = [rep_over(down_pair[0])]
    down_came.append(rep_in(down_parts[1]))
    gate(down_pair[0], up_terms[0])

    context_w = out_w
    if split > 1:
        pairs = [list(range(h * split, (h + 1) * split)) for h in range(HEADS)]
        context_w = lax.all_gather(out_w, "shard", axis=0, tiled=True, axis_index_groups=pairs)
    up_terms.append(normed_dot(where_rep, shards, late(normed), hidden_grad, sum_hidden, 1, 2))
    grad_out, up_terms[1] = tie(grad_out, up_terms[1])
    context_grad = head_back(grad_out, context_w)
    qkv_parts, context_grad = tie(qkv_parts, context_grad)
    qkv_w = whole(qkv_parts)
    mixed = dot(normed, qkv_w, 1, 0) + bias_qkv
    down_other[0], down_came[1], up_found[0], mixed = tie(down_other[0], down_came[1], up_found[0], mixed)
    down_total = [plus_low(down_pair[0], down_other[0], needed=inner)]
    down_back = [rep_out(down_total[0])]
    down_pair.append(plus_low(down_parts[1], down_came[1], needed=inner))
    down_other.append(rep_over(down_pair[1]))
    up_came = [rep_in(up_found[0])]
    up_terms[1], up_found[0] = tie(up_terms[1], up_found[0])
    up_found.append(swap(up_terms[1]))
    gate(down_total[0], down_pair[1], up_found[0])
    cosine, sine = rotary_tables()
    context, mixed_grad, sum_mixed = attention(
        tables,
        late(mixed).reshape(shards, MB, own, BLK, 3 * HD),
        context_grad.reshape(shards, MB, own, BLK, HD),
        cosine,
        sine,
    )
    context = context.reshape(rows, HD)
    mixed_grad = mixed_grad.reshape(rows, 3 * HD)
    down_back[0], down_other[1], up_came[0], up_found[1], context = tie(
        down_back[0], down_other[1], up_came[0], up_found[1], context
    )
    down_total.append(plus_low(down_pair[1], down_other[1], needed=inner))
    down_back.append(rep_out(down_total[1]))
    up_pair = [plus_low(up_found[0], up_came[0], needed=inner)]
    up_other = [rep_over(up_pair[0])]
    up_came.append(rep_in(up_found[1]))
    gate(down_back[0], down_total[1], up_pair[0], up_found[1])
    mixed_grad = late(mixed_grad)
    if split > 1:
        context = lax.dynamic_slice_in_dim(context, share * (HD // split), HD // split, 1)
        mixed_grad = lax.dynamic_slice_in_dim(mixed_grad, share * share_cols, share_cols, 1)
        qkv_w = lax.dynamic_slice_in_dim(qkv_w, share * share_cols, share_cols, 1)
        sum_mixed = lax.dynamic_slice_in_dim(sum_mixed, share * share_cols, share_cols, 2)
    sum_mixed = jnp.sum(sum_mixed, axis=(0, 1))[None]
    qkv_terms = normed_dot(where_rep, shards, normed, mixed_grad, sum_mixed)
    qkv_found = swap(qkv_terms)
    if cube:
        context, qkv_terms = tie(context, qkv_terms)
        out_part = token_dot(context, grad_out)
        out_came = rep_in(out_part)

        context, out_part = tie(context, out_part)
        odd = out_terms(owners, place, context, active, out_w, down_w, resid)
        odd_came = flip(odd, 1)
        down_back[1], up_other[0], up_came[1], odd = tie(down_back[1], up_other[0], up_came[1], odd)
        up_total = [plus_low(up_pair[0], up_other[0], needed=inner)]
        up_back = [rep_out(up_total[0])]
        up_pair.append(plus_low(up_found[1], up_came[1], needed=inner))
        up_other.append(rep_over(up_pair[1]))
        gate(down_back[1], up_total[0], up_pair[1], qkv_terms, odd)

        norm_odd = norm_terms(owners, late(mixed_grad), hidden_grad, qkv_w, up_w)
        norm_odd_came = flip(norm_odd, 1)
        odd_came, norm_odd = tie(odd_came, norm_odd)
        send_one, keep_one, send_two, keep_two = out_terms(
            owners, place, context, active, out_w, down_w, resid, odd_came
        )
        got_one, got_two = flip(send_one, 2), flip(send_two, 4)
        up_back[0], up_other[1], out_came, qkv_found, keep_one = tie(
            up_back[0], up_other[1], out_came, qkv_found, keep_one
        )
        up_total.append(plus_low(up_pair[1], up_other[1], needed=inner))
        up_back.append(rep_out(up_total[1]))
        qkv_parts = [qkv_found[:shards // 2], qkv_found[shards // 2:]]
        qkv_came = [rep_in(part) for part in qkv_parts]
        gate(up_back[0], up_total[1], out_came, *qkv_parts, norm_odd, send_one)

        norm_send_one, norm_keep_one, norm_send_two, norm_keep_two = norm_terms(
            owners, mixed_grad, hidden_grad, qkv_w, up_w, late(norm_odd_came)
        )
        norm_got_one, norm_got_two = flip(norm_send_one, 2), flip(norm_send_two, 4)

        qkv_came[0], norm_keep_one = tie(qkv_came[0], norm_keep_one)
        qkv_pair = [plus_low(qkv_parts[0], qkv_came[0], needed=inner)]
        qkv_other = [rep_over(qkv_pair[0])]
        out_came, qkv_pair[0] = tie(out_came, qkv_pair[0])
        got_one, got_two, out_came = tie(got_one, got_two, out_came)
        out_pair = plus_low(out_part, out_came, needed=inner)
        out_other = rep_over(out_pair)
        keep_one, keep_two, out_pair = tie(keep_one, keep_two, out_pair)
        last_one = plus_low(keep_one, got_one, 1)
        last_two = plus_low(keep_two, got_two, 1)
        qkv_came[1], last_one, last_two = tie(qkv_came[1], last_one, last_two)
        qkv_pair.append(plus_low(qkv_parts[1], qkv_came[1], needed=inner))
        qkv_other.append(rep_over(qkv_pair[1]))
        down_late, grad_late, qkv_pair[1] = tie(list(zip(down_total, down_back)), grad_out, qkv_pair[1])
        down_grad = row_grads(inner, down_late, wide // 2)
        found = jnp.where(inner == 1, down_late[1][0][wide // 2:], down_late[1][1][wide // 2:])
        out_bias_grad = sums_of(found, cols)
        grad_rows = lax.dynamic_slice_in_dim(grad_late, place * own_rows, own_rows, 1)
        grad_rows = grad_rows.transpose(1, 0, 2).reshape(own_rows, D)
        qkv_other[0], down_grad, grad_rows, out_bias_grad = tie(
            qkv_other[0], down_grad, grad_rows, out_bias_grad
        )
        qkv_total = [plus_low(qkv_pair[0], qkv_other[0], needed=inner)]
        qkv_back = [rep_out(qkv_total[0])]
        norm_got_one, norm_got_two, qkv_total[0] = tie(norm_got_one, norm_got_two, qkv_total[0])
        norm_last_one = plus_low(norm_keep_one, norm_got_one, 1)
        norm_last_two = plus_low(norm_keep_two, norm_got_two, 1)
        up_back[1], norm_last_one, norm_last_two = tie(up_back[1], norm_last_one, norm_last_two)
        norm_last_one, norm_last_two = flip(norm_last_one, 4), flip(norm_last_two, 2)
        up_grad, gain_two_grad, shift_two_grad, sum_up = column_grads(
            inner, list(zip(up_total, up_back)), up_weight, ln2_gain, ln2_bias, wide // 2, 1, True
        )
        qkv_other[1], up_grad = tie(qkv_other[1], up_grad)
        qkv_total.append(plus_low(qkv_pair[1], qkv_other[1], needed=inner))
        qkv_back.append(rep_out(qkv_total[1]))
        out_other, qkv_back[0], norm_last_one, norm_last_two, last_one, last_two, qkv_total[1] = tie(
            out_other, qkv_back[0], norm_last_one, norm_last_two, last_one, last_two, qkv_total[1]
        )
        last_one, last_two = flip(last_one, 4), flip(last_two, 2)
        out_total = plus_low(out_pair, out_other, needed=inner)
        out_back = rep_out(out_total)
        norm_last_one, norm_last_two, out_total = tie(norm_last_one, norm_last_two, out_total)
        tokens_grad = token_grads(
            resid, grad_rows,
            [(norm_keep_one, norm_got_one, norm_last_one), (norm_keep_two, norm_got_two, norm_last_two)],
        )
        last_one, last_two, tokens_grad = tie(last_one, last_two, tokens_grad)
        out_given = out_blocks(
            tables[0], tables[1], own, [(keep_one, got_one, last_one), (keep_two, got_two, last_two)],
            out_bias.astype(f32) + down_bias.astype(f32),
        )
        qkv_back, out_given = tie(qkv_back, out_given)
        qkv_grad, gain_one_grad, shift_one_grad, sum_qkv = column_grads(
            inner, list(zip(qkv_total, qkv_back)), qkv_weight, ln1_gain, ln1_bias, HD, 2, False, token
        )
        out_back, qkv_grad = tie(out_back, qkv_grad)
        out_grad = row_grads(inner, [(out_total, out_back)])
    else:
        sums = jnp.concatenate([sum_mixed[0], sum_hidden[0]])
        sums, out_bias_grad = lax.psum((sums, sum_cot), "rep")
        sums = lax.all_gather(sums, "shard")
        sum_qkv = sums[:, :share_cols].reshape(HEADS, 3, HD).transpose(1, 0, 2).reshape(3 * D)
        sum_up = sums[:, share_cols:].reshape(FF)
        qkv_found, up_found = qkv_found[:, :cols], [found[:, :cols] for found in up_found]
        out_sum, qkv_sum, up_sum, down_sum = lax.psum(
            (token_dot(context, grad_out), qkv_found, jnp.concatenate(up_found, axis=2), jnp.concatenate(down_parts)), "rep"
        )
        terms = dot(context, out_w, 1, 0) + dot(active, down_w, 1, 0)
        terms = lax.dynamic_update_slice_in_dim(
            terms,
            lax.dynamic_slice_in_dim(terms, place * own_rows, own_rows, 0) + resid.astype(f32),
            place * own_rows,
            0,
        )
        out_own = lax.psum_scatter(terms.astype(bf16), "shard", scatter_dimension=1, tiled=True)
        out_own = out_own.astype(f32)
        terms = dot(mixed_grad, qkv_w, 1, 1) + dot(hidden_grad, up_w, 1, 1)
        normed_grad = lax.psum_scatter(terms.astype(bf16), "shard", scatter_dimension=0, tiled=True)
        normed_grad = normed_grad.astype(f32)
        grad_rows = lax.dynamic_slice_in_dim(grad_out, place * own_rows, own_rows, 1)
        grad_rows = grad_rows.transpose(1, 0, 2).reshape(own_rows, D)

        out_own = out_own + (out_bias.astype(f32) + down_bias.astype(f32))
        out_own = out_own.astype(bf16).reshape(shards, MB, own, BLK, cols)
        out_given = jnp.stack([out_own[piece_of[m], m, inner_of[m]] for m in range(MB)])
        mean_grad = jnp.mean(normed_grad, axis=-1, keepdims=True)
        mean_proj = jnp.mean(normed_grad * normed_own, axis=-1, keepdims=True)
        tokens_grad = inv_std * (normed_grad - mean_grad - normed_own * mean_proj)
        tokens_grad = (grad_rows.astype(f32) + tokens_grad).astype(bf16)
    tokens_grad = tokens_grad.reshape(MB, own, BLK, D)

    if not cube:
        def finish(sums, weight, gain, shift, total):
            sums = sums.astype(f32)
            grads = gain.astype(f32)[:, None] * sums + shift.astype(f32)[:, None] * total
            weight = weight.astype(f32)
            return grads, jnp.sum(weight * sums, axis=1), jnp.sum(weight * total, axis=1)

        qkv_rows = qkv_sum.reshape(HEADS, split, cols, share_cols).transpose(2, 0, 1, 3)
        qkv_rows = qkv_rows.reshape(cols, HEADS, 3, HD).transpose(0, 2, 1, 3).reshape(cols, 3 * D)
        up_rows = up_sum.transpose(1, 0, 2).reshape(cols, FF)
        qkv_grad, gain_one_grad, shift_one_grad = finish(
            qkv_rows, qkv_weight, ln1_gain, ln1_bias, sum_qkv
        )
        out_grad = out_sum.astype(f32)
        down_grad = down_sum.astype(f32)
        up_grad, gain_two_grad, shift_two_grad = finish(
            up_rows, up_weight, ln2_gain, ln2_bias, sum_up
        )

    qkv_bias_grad = lax.dynamic_slice_in_dim(sum_qkv, place * 3 * cols, 3 * cols)
    up_bias_grad = lax.dynamic_slice_in_dim(sum_up, place * wide, wide)
    return (
        out_given,
        tokens_grad,
        gain_one_grad.reshape(cols),
        shift_one_grad.reshape(cols),
        gain_two_grad.reshape(cols),
        shift_two_grad.reshape(cols),
        qkv_grad,
        qkv_bias_grad,
        out_grad,
        out_bias_grad,
        up_grad,
        up_bias_grad,
        down_grad,
        out_bias_grad,
    )


def solution(mesh):
    in_specs = (
        P(None, ("rep", "shard"), None, None),
        P(None, "rep", None, "shard"),
        P(None, "rep", None),
        P(None, "rep", None),
        P(None, "rep", None),
        P("shard"),
        P("shard"),
        P("shard"),
        P("shard"),
        P("shard", None),
        P("shard"),
        P("shard", None),
        P("shard"),
        P("shard", None),
        P("shard"),
        P("shard", None),
        P("shard"),
    )
    out_specs = (
        P(None, "rep", None, "shard"),
        P(None, ("rep", "shard"), None, None),
        P("shard"),
        P("shard"),
        P("shard"),
        P("shard"),
        P("shard", None),
        P("shard"),
        P("shard", None),
        P("shard"),
        P("shard", None),
        P("shard"),
        P("shard", None),
        P("shard"),
    )
    return jax.shard_map(local, mesh=mesh, in_specs=in_specs, out_specs=out_specs, check_vma=False)
```
